32 devices in a mesh: tile: 4 (over y, x), tm: 8 (over z, core).
Axes of the slice: x: 2, y: 2, z: 4, core: 2. Of those that a mesh axis runs over, the one named last changes fastest.
Arguments:
- histories: bfloat16 [4, 32, 128, 1024], P('tile', 'tm'), may hold values from -6 to 6
- gain_time: float32 [1024], replicated, may hold values from 0.25 to 1.75
- wq_time: bfloat16 [1024, 1024], replicated
- wkv_time: bfloat16 [1024, 512], replicated
- wo_time: bfloat16 [1024, 1024], replicated, may hold values from -0.1875 to 0.1875
- gain_space: float32 [1024], replicated, may hold values from 0.25 to 1.75
- wq_space: bfloat16 [1024, 1024], replicated
- wkv_space: bfloat16 [1024, 512], replicated
- wo_space: bfloat16 [1024, 1024], replicated, may hold values from -0.1875 to 0.1875
- neighbours: int32 [4, 4], P('tile'), may hold values from 0 to 3, as said below
- nbr_valid: int32 [4, 4], P('tile'), may hold values from 0 to 1, as said below
- agent_valid: int32 [4, 32], P('tile'), may hold values from 0 to 1
Outputs:
- updated: bfloat16 [4, 32, 128, 1024], P('tile', 'tm')
The draws below stay inside these ranges and needn't reach their ends.
Inputs may be any that keep to these rules, and one draw needn't show every extreme that they name: `neighbours`: row i starts with tile i; the entries of a row are distinct tiles. `nbr_valid`: the first entry of every row is 1; row 0 is all ones; other rows keep differing shares of their entries.
All inputs are finite; a program needn't handle non-finite values.
Results may differ from the reference program's by a relative error of at most 0.014.
The reference program's roundings to bfloat16 on the way count: a program that leaves them out, or rounds other values in their place, can miss the bound.
Values may be sent and summed in bfloat16 or wider, within the bound.
No kernel may reach another device: no remote copies, remote signals or barrier semaphores. Data moves between devices by JAX's collectives and lax.ppermute only.
A program may use at most 128 MiB of HBM per device.

```python
import jax
import jax.numpy as jnp
from jax import lax

D = 1024
HEADS = 16
KV_HEADS = 4
HEAD_DIM = 64
STEPS = 128
AGENTS = 32
TILES = 4
NBRS = 4


def attention_pair(key):
    key_query, key_keys, key_values = jax.random.split(key, 3)
    width_kv = KV_HEADS * HEAD_DIM
    w_query = jax.random.normal(key_query, (D, D), jnp.float32) * D ** (-0.5)
    w_keys = jax.random.normal(key_keys, (D, width_kv), jnp.float32) * D ** (-0.5)
    w_values = jax.random.normal(key_values, (D, width_kv), jnp.float32) * D ** (-0.5)
    return (w_query, jnp.concatenate([w_keys, w_values], axis=1))


def draw_wq_time(key, part):
    return attention_pair(jax.random.fold_in(key, 101))[0].astype(jnp.bfloat16)


def draw_wkv_time(key, part):
    return attention_pair(jax.random.fold_in(key, 101))[1].astype(jnp.bfloat16)


def draw_wq_space(key, part):
    return attention_pair(jax.random.fold_in(key, 202))[0].astype(jnp.bfloat16)


def draw_wkv_space(key, part):
    return attention_pair(jax.random.fold_in(key, 202))[1].astype(jnp.bfloat16)


def draw_neighbours(key, part):
    base = jax.random.fold_in(key, 303)

    def one_row(row_key, tile_number):
        order = jax.random.permutation(row_key, TILES - 1).astype(jnp.int32)
        other_tiles = (tile_number + 1 + order) % TILES
        return jnp.concatenate([tile_number[None], other_tiles[:NBRS - 1]])
    row_keys = jax.random.split(base, TILES)
    return jax.vmap(one_row)(row_keys, jnp.arange(TILES, dtype=jnp.int32)).astype(jnp.int32)


def draw_nbr_valid(key, part):
    key_level, key_flags = jax.random.split(jax.random.fold_in(key, 404))
    level = jax.random.randint(key_level, (TILES, 1), 1, 5)
    flags = jax.random.randint(key_flags, (TILES, NBRS), 0, 4) < level
    column = jnp.arange(NBRS)[None, :] == 0
    first_row = jnp.arange(TILES)[:, None] == 0
    return (flags | column | first_row).astype(jnp.int32)


def draw_agent_valid(key, part):
    flags = jax.random.randint(jax.random.fold_in(key, 505), (TILES, AGENTS), 0, 4) > 0
    column = jnp.arange(AGENTS)[None, :] == 0
    return (flags | column).astype(jnp.int32)


def block_scale(own_key, shape, pieces, low, largest):
    level, own = 1.0, jax.random.fold_in(own_key, 6)
    for axis_at, blocks in pieces:
        steps = jnp.exp(jax.random.uniform(jax.random.fold_in(own, axis_at), (blocks,), jnp.float32, low / len(pieces), largest / len(pieces)))
        level = level * jnp.repeat(steps, shape[axis_at] // blocks).reshape([-1 if axis == axis_at else 1 for axis in range(len(shape))])
    return level


def gaussian(own_key, dims, width, limit, pieces=(), kind=jnp.bfloat16):
    array = jax.random.normal(own_key, dims, jnp.float32) * width
    if len(pieces) > 0:
        array = block_scale(own_key, dims, pieces, -0.22, 0.18) * array
    return jnp.clip(array, min=-limit, max=limit).astype(kind)


def setup_inputs(seed: int = 0) -> dict:
    arg_keys = jax.random.split(jax.random.key(seed), 13)
    return {
        "histories": gaussian(arg_keys[0], (TILES, AGENTS, STEPS, D), 1.0, 6.0, ((0, 4), (1, 8))),
        "gain_time": jnp.clip(1.0 + 0.15 * jax.random.normal(arg_keys[1], (D,), jnp.float32), 0.25, 1.75),
        "wq_time": draw_wq_time(jax.random.fold_in(arg_keys[12], 71), 0),
        "wkv_time": draw_wkv_time(jax.random.fold_in(arg_keys[12], 71), 0),
        "wo_time": gaussian(arg_keys[4], (D, D), D ** -0.5, 0.1875),
        "gain_space": jnp.clip(1.0 + 0.15 * jax.random.normal(arg_keys[5], (D,), jnp.float32), 0.25, 1.75),
        "wq_space": draw_wq_space(jax.random.fold_in(arg_keys[12], 71), 0),
        "wkv_space": draw_wkv_space(jax.random.fold_in(arg_keys[12], 71), 0),
        "wo_space": gaussian(arg_keys[8], (D, D), D ** -0.5, 0.1875),
        "neighbours": draw_neighbours(jax.random.fold_in(arg_keys[12], 71), 0),
        "nbr_valid": draw_nbr_valid(jax.random.fold_in(arg_keys[12], 71), 0),
        "agent_valid": draw_agent_valid(jax.random.fold_in(arg_keys[12], 71), 0),
    }


def norm_rows(values, gain):
    wide = values.astype(jnp.float32)
    meansq = lax.optimization_barrier(jnp.mean(wide * wide, axis=-1, keepdims=True))
    return (wide * lax.rsqrt(meansq + 1e-05) * gain.astype(jnp.float32)).astype(jnp.bfloat16)

def temporal_block(history, gain, w_query, w_keyval, w_out):
    batch, nsteps, model_width = history.shape
    groups = HEADS // KV_HEADS
    normed = norm_rows(history, gain).reshape(batch * nsteps, model_width)
    queries = jnp.dot(normed, w_query, preferred_element_type=jnp.float32).astype(jnp.bfloat16)
    queries = queries.reshape(batch, nsteps, KV_HEADS, groups, HEAD_DIM)
    keyval = jnp.dot(normed, w_keyval, preferred_element_type=jnp.float32).astype(jnp.bfloat16)
    keyval = keyval.reshape(batch, nsteps, 2, KV_HEADS, HEAD_DIM)
    logit_scores = jnp.einsum('bskgd,btkd->bkgst', queries.astype(jnp.float32), keyval[:, :, 0].astype(jnp.float32))
    logit_scores = logit_scores * HEAD_DIM ** (-0.5)
    causal = jnp.arange(nsteps)[:, None] >= jnp.arange(nsteps)[None, :]
    logit_scores = jnp.where(causal, logit_scores, -1e+30)
    row_top = lax.optimization_barrier(jnp.max(logit_scores, axis=-1, keepdims=True))
    expd = jnp.where(causal, jnp.exp(logit_scores - row_top), 0.0)
    probs = (expd / lax.optimization_barrier(jnp.sum(expd, axis=-1, keepdims=True))).astype(jnp.bfloat16)
    mixed = jnp.einsum('bkgst,btkd->bskgd', probs.astype(jnp.float32), keyval[:, :, 1].astype(jnp.float32))
    mixed = mixed.astype(jnp.bfloat16).reshape(batch * nsteps, model_width)
    projected = jnp.dot(mixed, w_out, preferred_element_type=jnp.float32)
    return (history.astype(jnp.float32) + projected.reshape(batch, nsteps, model_width)).astype(jnp.bfloat16)

def reference(histories, gain_time, wq_time, wkv_time, wo_time, gain_space, wq_space, wkv_space, wo_space, neighbours, nbr_valid, agent_valid):
    groups = HEADS // KV_HEADS
    time_mixed = lax.map(lambda block: temporal_block(block, gain_time, wq_time, wkv_time, wo_time), histories)
    normed = norm_rows(time_mixed, gain_space)
    flat = normed.reshape(-1, D)
    queries = jnp.dot(flat, wq_space, preferred_element_type=jnp.float32).astype(jnp.bfloat16)
    queries = queries.reshape(TILES, AGENTS, STEPS, KV_HEADS, groups, HEAD_DIM)
    key_values = jnp.dot(flat, wkv_space, preferred_element_type=jnp.float32).astype(jnp.bfloat16)
    key_values = key_values.reshape(TILES, AGENTS, STEPS, 2 * KV_HEADS * HEAD_DIM)
    alive_mask = agent_valid.astype(jnp.float32)

    def one_tile(scan_item):
        tile_queries, tile_list, tile_valid, tile_state = scan_item
        chosen = key_values[tile_list]
        key_weight = (tile_valid.astype(jnp.float32)[:, None] * alive_mask[tile_list]).reshape(-1)
        chosen = jnp.transpose(chosen, (2, 0, 1, 3)).reshape(STEPS, NBRS * AGENTS, 2, KV_HEADS, HEAD_DIM)
        step_queries = jnp.transpose(tile_queries, (1, 0, 2, 3, 4))

        def one_step(paired):
            current_query, current_keyvalue = paired
            logit_scores = jnp.einsum('nfqe,yfe->fqny', current_query.astype(jnp.float32), current_keyvalue[:, 0].astype(jnp.float32))
            logit_scores = logit_scores * HEAD_DIM ** (-0.5)
            logit_scores = jnp.where(key_weight > 0, logit_scores, -1e+30)
            row_top = lax.optimization_barrier(jnp.max(logit_scores, axis=-1, keepdims=True))
            weights = jnp.exp(logit_scores - row_top) * key_weight
            rounded_result = lax.optimization_barrier(weights.astype(jnp.bfloat16)).astype(jnp.float32)
            summed_values = jnp.einsum('zxrv,vzc->rzxc', rounded_result, current_keyvalue[:, 1].astype(jnp.float32))
            denominator = jnp.transpose(lax.optimization_barrier(jnp.sum(weights, axis=-1)), (2, 0, 1))
            return (summed_values / denominator[..., None]).astype(jnp.bfloat16)
        mixed = lax.map(one_step, (step_queries, chosen))
        mixed = jnp.transpose(mixed, (1, 0, 2, 3, 4)).reshape(AGENTS * STEPS, D)
        projected = jnp.dot(mixed, wo_space, preferred_element_type=jnp.float32)
        return (tile_state.astype(jnp.float32) + projected.reshape(AGENTS, STEPS, D)).astype(jnp.bfloat16)
    return lax.map(one_tile, (queries, neighbours, nbr_valid, time_mixed))
```

```python
import functools

import jax
import jax.numpy as jnp
from jax import lax
from jax.experimental import pallas as pl
from jax.experimental.pallas import tpu as pltpu
from jax.sharding import Mesh
from jax.sharding import PartitionSpec as P

HEADS = 16
KV_HEADS = 4
HEAD_DIM = 64
GROUPS = HEADS // KV_HEADS
KEYS = KV_HEADS * HEAD_DIM
WIDE = GROUPS * HEAD_DIM
SCALE = HEAD_DIM ** (-0.5)
NEG = -1e30
LANES = 128
COLS = 256
HALVES = 2
VMEM_BYTES = 56 * 1024 * 1024
F32 = jnp.float32
BF16 = jnp.bfloat16
ROWS_BY_COLS = (((1,), (1,)), ((), ()))


def norm_rows(values, gain):
    wide = values.astype(F32)
    meansq = jnp.mean(wide * wide, axis=-1, keepdims=True)
    return (wide * lax.rsqrt(meansq + 1e-05) * gain).astype(BF16)


def to_blocks(values, agents, steps, local):
    split = values.reshape(agents, steps // local, local, values.shape[-1])
    return jnp.transpose(split, (1, 0, 2, 3)).reshape(steps // local, agents * local, values.shape[-1])


def from_blocks(values, agents, steps, local):
    split = values.reshape(steps // local, agents, local, values.shape[-1])
    return jnp.transpose(split, (1, 0, 2, 3)).reshape(agents * steps, values.shape[-1])


def time_kernel(
    agents, steps, local, blocked,
    hist, gain_t, gain_s, wq_hbm, wkv_hbm, wo_hbm, wkv2_hbm,
    mid, second, kv_out,
    wq, wkv, wo, wkv2, normed, query, keyval, mix, sems,
):
    rows, width = hist.shape
    loads = [
        pltpu.make_async_copy(source, target, sems.at[i])
        for i, (source, target) in enumerate(
            ((wq_hbm, wq), (wkv_hbm, wkv), (wo_hbm, wo), (wkv2_hbm, wkv2))
        )
    ]
    for load in loads:
        load.start()
    for a in range(agents):
        part = pl.ds(a * steps, steps)
        normed[part, :] = norm_rows(hist[part, :], gain_t[...])
    loads[0].wait()
    for c in range(0, width, COLS):
        query[:, c : c + COLS] = jnp.dot(
            normed[...], wq[:, c : c + COLS], preferred_element_type=F32
        ).astype(BF16)
    loads[1].wait()
    for c in range(0, 2 * KEYS, COLS):
        keyval[:, c : c + COLS] = jnp.dot(
            normed[...], wkv[:, c : c + COLS], preferred_element_type=F32
        ).astype(BF16)
    lane_head = lax.broadcasted_iota(jnp.int32, (steps, WIDE), 1) // HEAD_DIM
    causal = lax.broadcasted_iota(jnp.int32, (steps, steps), 0) >= lax.broadcasted_iota(
        jnp.int32, (steps, steps), 1
    )

    def spread(part):
        repeated = jnp.concatenate([part] * GROUPS, axis=1)
        zero = jnp.zeros_like(repeated)
        return jnp.concatenate(
            [jnp.where(lane_head == j, repeated, zero) for j in range(GROUPS)], axis=0
        )

    def one_agent(a, carry):
        part = pl.ds(pl.multiple_of(a * steps, steps), steps)
        for k in range(KV_HEADS):
            wide = slice(k * WIDE, (k + 1) * WIDE)
            keys = spread(keyval[part, k * HEAD_DIM : (k + 1) * HEAD_DIM])
            vals = spread(keyval[part, KEYS + k * HEAD_DIM : KEYS + (k + 1) * HEAD_DIM])
            scores = lax.dot_general(
                query[part, wide], keys, ROWS_BY_COLS, preferred_element_type=F32
            )
            expd, sums = [], []
            for j in range(GROUPS):
                head = jnp.where(causal, scores[:, j * steps : (j + 1) * steps] * SCALE, NEG)
                top = jnp.max(head, axis=-1, keepdims=True)
                grown = jnp.exp(head - top)
                sums.append(jnp.sum(grown, axis=-1, keepdims=True))
                expd.append(grown.astype(BF16))
            mixed = jnp.dot(jnp.concatenate(expd, axis=1), vals, preferred_element_type=F32)
            inverse = jnp.concatenate(
                [jnp.broadcast_to(1.0 / s, (steps, HEAD_DIM)) for s in sums], axis=1
            )
            mix[part, wide] = (mixed * inverse).astype(BF16)
        return carry

    lax.fori_loop(0, agents, one_agent, 0)
    loads[2].wait()
    for c in range(0, width, COLS):
        cols = slice(c, c + COLS)
        projected = jnp.dot(mix[...], wo[:, cols], preferred_element_type=F32)
        mid[:, cols] = (hist[:, cols].astype(F32) + projected).astype(BF16)
    for a in range(agents):
        part = pl.ds(a * steps, steps)
        second[part, :] = norm_rows(mid[part, :], gain_s[...])
    loads[3].wait()
    for c in range(0, 2 * KEYS, COLS):
        cols = slice(c, c + COLS)
        result = jnp.dot(second[...], wkv2[:, cols], preferred_element_type=F32)
        if blocked:
            kv_out[:, :, cols] = to_blocks(result, agents, steps, local).astype(BF16)
        else:
            kv_out[:, cols] = result.astype(BF16)


def query_kernel(agents, steps, local, blocked, second, wq, meta, out):
    width = second.shape[1]
    for c in range(0, width, COLS):
        cols = slice(c, c + COLS)
        result = jnp.dot(second[...], wq[:, cols], preferred_element_type=F32)
        if blocked:
            out[:, :, cols] = to_blocks(result, agents, steps, local).astype(BF16)
        else:
            out[:, cols] = result.astype(BF16)
    lines = jnp.broadcast_to(meta[0:1, :], (out.shape[-2], LANES)).astype(BF16)
    if blocked:
        out[:, :, width:] = jnp.broadcast_to(lines[None], (out.shape[0], out.shape[1], LANES))
    else:
        out[:, width:] = lines


def one_hot(shape, group, local, dtype=BF16):
    row = lax.broadcasted_iota(jnp.int32, shape, 0)
    col = lax.broadcasted_iota(jnp.int32, shape, 1)
    wanted = (row % group) * local + row // group
    return jnp.where(col == wanted, 1.0, 0.0).astype(dtype)


def space_kernel(
    local, block, q_in, own, other, weight, out, query, keyval, mix
):
    rows, width = out.shape
    group = block // local
    total = rows // local
    if local > 1:
        order = one_hot((block, block), group, local)

    def by_steps(source, target, offset, cols):
        for b in range(rows // block):
            piece = source[b * block : (b + 1) * block, cols]
            if local > 1:
                piece = jnp.dot(order, piece, preferred_element_type=F32).astype(BF16)
            target[:, offset + b * group : offset + (b + 1) * group, cols] = piece.reshape(
                local, group, piece.shape[1]
            )

    for c in range(0, width, COLS):
        by_steps(q_in, query, 0, slice(c, c + COLS))
    for c in range(0, 2 * KEYS, COLS):
        by_steps(own, keyval, 0, slice(c, c + COLS))
        by_steps(other, keyval, total, slice(c, c + COLS))

    def one_step(s, carry):
        mask = jnp.concatenate([weight[...]] * GROUPS, axis=0)
        for k in range(KV_HEADS):
            wide = slice(k * WIDE, (k + 1) * WIDE)
            heads = query[s, :, wide]
            heads = jnp.concatenate(
                [heads[:, j * HEAD_DIM : (j + 1) * HEAD_DIM] for j in range(GROUPS)], axis=0
            )
            keys = keyval[s, :, k * HEAD_DIM : (k + 1) * HEAD_DIM]
            vals = keyval[s, :, KEYS + k * HEAD_DIM : KEYS + (k + 1) * HEAD_DIM]
            scores = lax.dot_general(heads, keys, ROWS_BY_COLS, preferred_element_type=F32)
            scores = jnp.where(mask > 0, scores * SCALE, NEG)
            top = jnp.max(scores, axis=-1, keepdims=True)
            grown = jnp.exp(scores - top) * mask
            sums = jnp.sum(grown, axis=-1, keepdims=True)
            mixed = jnp.dot(grown.astype(BF16), vals, preferred_element_type=F32) / sums
            mixed = mixed.astype(BF16)
            mix[s, :, wide] = jnp.concatenate(
                [mixed[j * total : (j + 1) * total] for j in range(GROUPS)], axis=1
            )
        return carry

    lax.fori_loop(0, local, one_step, 0)
    for b in range(rows // block):
        for c in range(0, width, COLS):
            cols = slice(c, c + COLS)
            piece = mix[:, b * group : (b + 1) * group, cols].reshape(block, COLS)
            if local > 1:
                piece = lax.dot_general(
                    order, piece, (((0,), (0,)), ((), ())), preferred_element_type=F32
                ).astype(BF16)
            out[b * block : (b + 1) * block, cols] = piece


def out_kernel(agents, steps, local, blocked, mix, mid, wo, out):
    width = mid.shape[1]
    for c in range(0, width, COLS):
        cols = slice(c, c + COLS)
        projected = jnp.dot(mix[...], wo[:, cols], preferred_element_type=F32)
        if blocked:
            projected = from_blocks(projected, agents, steps, local)
        out[:, cols] = (mid[:, cols].astype(F32) + projected).astype(BF16)


def call(kernel, shapes, args, hbm=(), scratch=(), flops=0):
    moved = sum(a.size * a.dtype.itemsize for a in args)
    moved += sum(s.size * s.dtype.itemsize for s in shapes)
    return pl.pallas_call(
        kernel,
        out_shape=shapes if len(shapes) > 1 else shapes[0],
        in_specs=[
            pl.BlockSpec(memory_space=pl.ANY if i in hbm else pltpu.VMEM) for i in range(len(args))
        ],
        out_specs=[pl.BlockSpec(memory_space=pltpu.VMEM)] * len(shapes)
        if len(shapes) > 1
        else pl.BlockSpec(memory_space=pltpu.VMEM),
        scratch_shapes=list(scratch),
        compiler_params=pltpu.CompilerParams(vmem_limit_bytes=VMEM_BYTES),
        cost_estimate=pl.CostEstimate(flops=flops, bytes_accessed=moved, transcendentals=0),
    )(*args)


def per_device(
    histories,
    gain_time,
    wq_time,
    wkv_time,
    wo_time,
    gain_space,
    wq_space,
    wkv_space,
    wo_space,
    neighbours,
    nbr_valid,
    agent_valid,
):
    agents, steps, width = histories.shape[1:]
    tiles, rest = lax.axis_size("tile"), lax.axis_size("rest")
    spread = ("tile", "rest")
    parts = tiles * rest
    local = steps // parts
    rows = agents * steps
    blocked = local % 8 == 0
    struct = jax.ShapeDtypeStruct

    hist = histories.reshape(rows, width)
    kv_shape = (parts, agents * local, 2 * KEYS) if blocked else (rows, 2 * KEYS)
    mid, second, kv = call(
        functools.partial(time_kernel, agents, steps, local, blocked),
        [struct((rows, width), BF16), struct((rows, width), BF16), struct(kv_shape, BF16)],
        [hist, gain_time[None], gain_space[None], wq_time, wkv_time, wo_time, wkv_space],
        hbm=(3, 4, 5, 6),
        scratch=[
            pltpu.VMEM(wq_time.shape, BF16),
            pltpu.VMEM(wkv_time.shape, BF16),
            pltpu.VMEM(wo_time.shape, BF16),
            pltpu.VMEM(wkv_space.shape, BF16),
            pltpu.VMEM((rows, width), BF16),
            pltpu.VMEM((rows, width), BF16),
            pltpu.VMEM((rows, 2 * KEYS), BF16),
            pltpu.VMEM((rows, width), BF16),
            pltpu.SemaphoreType.DMA((4,)),
        ],
        flops=2 * rows * width * (2 * width + 4 * KEYS),
    )
    if not blocked:
        kv = to_blocks(kv, agents, steps, local)
    own = lax.all_to_all(kv, spread, split_axis=0, concat_axis=0, tiled=True)
    own = own.reshape(rows, 2 * KEYS)
    swap = [(h, HALVES - 1 - h) for h in range(HALVES)]
    other = lax.ppermute(own, "half", swap)

    listed = jnp.sum(
        jnp.where(
            neighbours[0][:, None] == jnp.arange(tiles)[None, :], nbr_valid[0][:, None], 0
        ),
        axis=0,
    )
    alive = agent_valid[0]
    meta = jnp.concatenate([alive, listed])
    meta = jnp.pad(meta, (0, LANES - meta.shape[0])).astype(F32)
    meta = jnp.broadcast_to(meta[None], (8, LANES))
    second, own = lax.optimization_barrier((second, own))
    q_shape = (parts, agents * local, width + LANES) if blocked else (rows, width + LANES)
    q = call(
        functools.partial(query_kernel, agents, steps, local, blocked),
        [struct(q_shape, BF16)],
        [second, wq_space, meta],
        flops=2 * rows * width * width,
    )
    if not blocked:
        q = to_blocks(q, agents, steps, local)
    q = lax.all_to_all(q, spread, split_axis=0, concat_axis=0, tiled=True)

    lines = q.reshape(tiles, rest, agents * local, width + LANES)[:, 0, 0, width:].astype(F32)
    group = rest * agents
    half = lax.axis_index("half")
    alive_all = lines[:, : HALVES * group].reshape(tiles, HALVES, group)
    alive_own = lax.dynamic_index_in_dim(alive_all, half, 1, keepdims=False)
    alive_other = lax.dynamic_index_in_dim(alive_all, 1 - half, 1, keepdims=False)
    listed_all = lines[:, HALVES * group : HALVES * group + tiles]
    weight = listed_all[:, None, :, None] * jnp.stack([alive_own, alive_other])[None]
    weight = jnp.repeat(weight.reshape(tiles, -1), group, axis=0)

    block = max(COLS, local) if rows % max(COLS, local) == 0 else rows
    mix = call(
        functools.partial(space_kernel, local, block),
        [struct((rows, width), BF16)],
        [q.reshape(rows, width + LANES), own, other, weight],
        scratch=[
            pltpu.VMEM((local, rows // local, width), BF16),
            pltpu.VMEM((local, HALVES * rows // local, 2 * KEYS), BF16),
            pltpu.VMEM((local, rows // local, width), BF16),
        ],
        flops=8 * rows * rows // local * width,
    )
    mix = lax.all_to_all(
        mix.reshape(parts, agents * local, width), spread, split_axis=0, concat_axis=0, tiled=True
    )
    if not blocked:
        mix = from_blocks(mix, agents, steps, local)
    out = call(
        functools.partial(out_kernel, agents, steps, local, blocked),
        [struct((rows, width), BF16)],
        [mix.reshape(rows, width), mid, wo_space],
        flops=2 * rows * width * width,
    )
    return out.reshape(1, agents, steps, width)


def solution(mesh):
    tiles, members = mesh.devices.shape
    split = Mesh(
        mesh.devices.reshape(tiles, HALVES, members // HALVES), ("tile", "half", "rest")
    )
    states = P("tile", ("half", "rest"), None, None)
    listing = P("tile", None)
    return jax.shard_map(
        per_device,
        mesh=split,
        in_specs=(states,) + (P(),) * 8 + (listing,) * 3,
        out_specs=states,
        check_vma=False,
    )
```

```python
import functools
import math

import jax
import jax.numpy as jnp
from jax import lax
from jax.experimental import pallas as pl
from jax.experimental.pallas import tpu as pltpu
from jax.sharding import Mesh
from jax.sharding import PartitionSpec as P

HEADS = 16
KV_HEADS = 4
HEAD_DIM = 64
GROUPS = HEADS // KV_HEADS
KEYS = KV_HEADS * HEAD_DIM
WIDE = GROUPS * HEAD_DIM
SCALE = HEAD_DIM ** (-0.5)
EXP2_SCALE = SCALE * math.log2(math.e)
NEG = -1e30
LANES = 128
COLS = 256
HALVES = 2
MIB = 1024 * 1024
F32 = jnp.float32
BF16 = jnp.bfloat16
ROWS_BY_COLS = (((1,), (1,)), ((), ()))


def norm_rows(values, gain):
    wide = values.astype(F32)
    meansq = jnp.mean(wide * wide, axis=-1, keepdims=True)
    return (wide * lax.rsqrt(meansq + 1e-05) * gain).astype(BF16)


def to_blocks(values, agents, steps, local):
    split = values.reshape(agents, steps // local, local, values.shape[-1])
    return jnp.transpose(split, (1, 0, 2, 3)).reshape(steps // local, agents * local, values.shape[-1])


def from_blocks(values, agents, steps, local):
    split = values.reshape(steps // local, agents, local, values.shape[-1])
    return jnp.transpose(split, (1, 0, 2, 3)).reshape(agents * steps, values.shape[-1])


def time_kernel(
    agents, steps, local, blocked,
    hist, gain_t, gain_s, wq_hbm, wkv_hbm, wo_hbm, wkv2_hbm,
    mid, second, kv_out,
    wq, wkv, wo, wkv2, normed, query, keyval, mix, sems,
):
    rows, width = hist.shape
    loads = [
        pltpu.make_async_copy(source, target, sems.at[i])
        for i, (source, target) in enumerate(
            ((wq_hbm, wq), (wkv_hbm, wkv), (wo_hbm, wo), (wkv2_hbm, wkv2))
        )
    ]
    for load in loads:
        load.start()
    for a in range(agents):
        part = pl.ds(a * steps, steps)
        normed[part, :] = norm_rows(hist[part, :], gain_t[...])
    loads[0].wait()
    for c in range(0, width, COLS):
        query[:, c : c + COLS] = jnp.dot(
            normed[...], wq[:, c : c + COLS], preferred_element_type=F32
        ).astype(BF16)
    loads[1].wait()
    for c in range(0, 2 * KEYS, COLS):
        keyval[:, c : c + COLS] = jnp.dot(
            normed[...], wkv[:, c : c + COLS], preferred_element_type=F32
        ).astype(BF16)
    causal = lax.broadcasted_iota(jnp.int32, (steps, steps), 0) <= lax.broadcasted_iota(
        jnp.int32, (steps, steps), 1
    )
    causal = jnp.concatenate([causal] * GROUPS, axis=1)
    for a in range(agents):
        part = slice(a * steps, (a + 1) * steps)
        for k in range(KV_HEADS):
            wide = slice(k * WIDE, (k + 1) * WIDE)
            keys = keyval[part, k * HEAD_DIM : (k + 1) * HEAD_DIM]
            vals = keyval[part, KEYS + k * HEAD_DIM : KEYS + (k + 1) * HEAD_DIM]
            heads = query[part, wide].T
            heads = jnp.concatenate(
                [heads[j * HEAD_DIM : (j + 1) * HEAD_DIM] for j in range(GROUPS)], axis=1
            )
            scores = jnp.dot(keys, heads, preferred_element_type=F32)
            scores = jnp.where(causal, scores, NEG)
            top = jnp.max(scores, axis=0, keepdims=True)
            grown = jnp.exp2((scores - top) * EXP2_SCALE)
            sums = jnp.sum(grown, axis=0, keepdims=True)
            mixed = jnp.dot(vals.T, grown.astype(BF16), preferred_element_type=F32) * (1.0 / sums)
            mixed = jnp.concatenate(
                [mixed[:, j * steps : (j + 1) * steps] for j in range(GROUPS)], axis=0
            )
            mix[part, wide] = mixed.astype(BF16).T
    loads[2].wait()
    for c in range(0, width, COLS):
        cols = slice(c, c + COLS)
        projected = jnp.dot(mix[...], wo[:, cols], preferred_element_type=F32)
        mid[:, cols] = (hist[:, cols].astype(F32) + projected).astype(BF16)
    for a in range(agents):
        part = pl.ds(a * steps, steps)
        second[part, :] = norm_rows(mid[part, :], gain_s[...])
    loads[3].wait()
    for c in range(0, 2 * KEYS, COLS):
        cols = slice(c, c + COLS)
        result = jnp.dot(second[...], wkv2[:, cols], preferred_element_type=F32)
        if blocked:
            kv_out[:, :, cols] = to_blocks(result, agents, steps, local).astype(BF16)
        else:
            kv_out[:, cols] = result.astype(BF16)


def query_kernel(agents, steps, local, blocked, second, wq, meta, out):
    width = second.shape[1]
    for c in range(0, width, COLS):
        cols = slice(c, c + COLS)
        result = jnp.dot(second[...], wq[:, cols], preferred_element_type=F32)
        if blocked:
            out[:, :, cols] = to_blocks(result, agents, steps, local).astype(BF16)
        else:
            out[:, cols] = result.astype(BF16)
    lines = jnp.broadcast_to(meta[0:1, :], (out.shape[-2], LANES)).astype(BF16)
    if blocked:
        out[:, :, width:] = jnp.broadcast_to(lines[None], (out.shape[0], out.shape[1], LANES))
    else:
        out[:, width:] = lines


def one_hot(shape, group, local, dtype=BF16):
    row = lax.broadcasted_iota(jnp.int32, shape, 0)
    col = lax.broadcasted_iota(jnp.int32, shape, 1)
    wanted = (row % group) * local + row // group
    return jnp.where(col == wanted, 1.0, 0.0).astype(dtype)


def key_weights(notes, local, tiles, total):
    rows = notes.shape[0]
    group = total // tiles
    shape = (total, rows)
    row, col = (lax.broadcasted_iota(jnp.int32, shape, d) for d in range(2))
    pick = jnp.where(col == row * local, 1.0, 0.0).astype(BF16)
    lines = jnp.dot(pick, notes, preferred_element_type=F32).astype(BF16)
    shape = (LANES, HALVES * total)
    lane, key = (lax.broadcasted_iota(jnp.int32, shape, d) for d in range(2))
    half, tile, agent = key // total, key % total // group, key % group
    spread = jnp.where(lane == HALVES * group + tile, 1.0, 0.0).astype(BF16)
    listed = jnp.dot(lines, spread, preferred_element_type=F32)
    spread = jnp.where(lane == half * group + agent, 1.0, 0.0).astype(BF16)
    alive = jnp.dot(lines, spread, preferred_element_type=F32)
    shape = (total, HALVES * total)
    row, key = (lax.broadcasted_iota(jnp.int32, shape, d) for d in range(2))
    first = row == key % total // group * group
    alive = jnp.sum(jnp.where(first, alive, 0.0), axis=0, keepdims=True)
    return listed * alive


def space_kernel(
    local, block, tiles, q_in, own, other, out, query, keyval, mix
):
    rows, width = out.shape
    group = block // local
    total = rows // local
    weight = key_weights(q_in[:, width:], local, tiles, total)
    if local > 1:
        order = one_hot((block, block), group, local)

    def by_steps(source, target, offset, cols):
        for b in range(rows // block):
            piece = source[b * block : (b + 1) * block, cols]
            if local > 1:
                piece = jnp.dot(order, piece, preferred_element_type=F32).astype(BF16)
            target[:, offset + b * group : offset + (b + 1) * group, cols] = piece.reshape(
                local, group, piece.shape[1]
            )

    for c in range(0, width, COLS):
        by_steps(q_in, query, 0, slice(c, c + COLS))
    for c in range(0, 2 * KEYS, COLS):
        by_steps(own, keyval, 0, slice(c, c + COLS))
        by_steps(other, keyval, total, slice(c, c + COLS))

    def one_step(s, carry):
        mask = jnp.concatenate([weight] * GROUPS, axis=0)
        for k in range(KV_HEADS):
            wide = slice(k * WIDE, (k + 1) * WIDE)
            heads = query[s, :, wide]
            heads = jnp.concatenate(
                [heads[:, j * HEAD_DIM : (j + 1) * HEAD_DIM] for j in range(GROUPS)], axis=0
            )
            keys = keyval[s, :, k * HEAD_DIM : (k + 1) * HEAD_DIM]
            vals = keyval[s, :, KEYS + k * HEAD_DIM : KEYS + (k + 1) * HEAD_DIM]
            scores = lax.dot_general(heads, keys, ROWS_BY_COLS, preferred_element_type=F32)
            scores = jnp.where(mask > 0, scores, NEG)
            top = jnp.max(scores, axis=-1, keepdims=True)
            grown = jnp.exp2((scores - top) * EXP2_SCALE) * mask
            sums = jnp.sum(grown, axis=-1, keepdims=True)
            mixed = jnp.dot(grown.astype(BF16), vals, preferred_element_type=F32) / sums
            mixed = mixed.astype(BF16)
            mix[s, :, wide] = jnp.concatenate(
                [mixed[j * total : (j + 1) * total] for j in range(GROUPS)], axis=1
            )
        return carry

    lax.fori_loop(0, local, one_step, 0, unroll=2 if local % 2 == 0 else 1)
    for b in range(rows // block):
        for c in range(0, width, COLS):
            cols = slice(c, c + COLS)
            piece = mix[:, b * group : (b + 1) * group, cols].reshape(block, COLS)
            if local > 1:
                piece = lax.dot_general(
                    order, piece, (((0,), (0,)), ((), ())), preferred_element_type=F32
                ).astype(BF16)
            out[b * block : (b + 1) * block, cols] = piece


def out_kernel(agents, steps, local, blocked, mix, mid, wo, out):
    width = mid.shape[1]
    for c in range(0, width, COLS):
        cols = slice(c, c + COLS)
        projected = jnp.dot(mix[...], wo[:, cols], preferred_element_type=F32)
        if blocked:
            projected = from_blocks(projected, agents, steps, local)
        out[:, cols] = (mid[:, cols].astype(F32) + projected).astype(BF16)


def call(kernel, shapes, args, hbm=(), scratch=(), flops=0, mib=16):
    moved = sum(a.size * a.dtype.itemsize for a in args)
    moved += sum(s.size * s.dtype.itemsize for s in shapes)
    return pl.pallas_call(
        kernel,
        out_shape=shapes if len(shapes) > 1 else shapes[0],
        in_specs=[
            pl.BlockSpec(memory_space=pl.ANY if i in hbm else pltpu.VMEM) for i in range(len(args))
        ],
        out_specs=[pl.BlockSpec(memory_space=pltpu.VMEM)] * len(shapes)
        if len(shapes) > 1
        else pl.BlockSpec(memory_space=pltpu.VMEM),
        scratch_shapes=list(scratch),
        compiler_params=pltpu.CompilerParams(vmem_limit_bytes=mib * MIB),
        cost_estimate=pl.CostEstimate(flops=flops, bytes_accessed=moved, transcendentals=0),
    )(*args)


def per_device(
    histories,
    gain_time,
    wq_time,
    wkv_time,
    wo_time,
    gain_space,
    wq_space,
    wkv_space,
    wo_space,
    neighbours,
    nbr_valid,
    agent_valid,
):
    agents, steps, width = histories.shape[1:]
    tiles, rest = lax.axis_size("tile"), lax.axis_size("rest")
    spread = ("tile", "rest")
    parts = tiles * rest
    local = steps // parts
    rows = agents * steps
    blocked = local % 8 == 0
    struct = jax.ShapeDtypeStruct

    hist = histories.reshape(rows, width)
    kv_shape = (parts, agents * local, 2 * KEYS) if blocked else (rows, 2 * KEYS)
    mid, second, kv = call(
        functools.partial(time_kernel, agents, steps, local, blocked),
        [struct((rows, width), BF16), struct((rows, width), BF16), struct(kv_shape, BF16)],
        [hist, gain_time[None], gain_space[None], wq_time, wkv_time, wo_time, wkv_space],
        hbm=(3, 4, 5, 6),
        scratch=[
            pltpu.VMEM(wq_time.shape, BF16),
            pltpu.VMEM(wkv_time.shape, BF16),
            pltpu.VMEM(wo_time.shape, BF16),
            pltpu.VMEM(wkv_space.shape, BF16),
            pltpu.VMEM((rows, width), BF16),
            pltpu.VMEM((rows, width), BF16),
            pltpu.VMEM((rows, 2 * KEYS), BF16),
            pltpu.VMEM((rows, width), BF16),
            pltpu.SemaphoreType.DMA((4,)),
        ],
        flops=2 * rows * width * (2 * width + 4 * KEYS),
        mib=24,
    )
    if not blocked:
        kv = to_blocks(kv, agents, steps, local)
    listed = jnp.sum(
        jnp.where(
            neighbours[0][:, None] == jnp.arange(tiles)[None, :], nbr_valid[0][:, None], 0
        ),
        axis=0,
    )
    group = rest * agents
    alive = jnp.where(lax.axis_index("half") == 0, agent_valid[0], jnp.roll(agent_valid[0], -group))
    meta = jnp.concatenate([alive, listed])
    meta = jnp.pad(meta, (0, LANES - meta.shape[0])).astype(F32)
    meta = jnp.broadcast_to(meta[None], (8, LANES))
    own = lax.all_to_all(kv, spread, split_axis=0, concat_axis=0, tiled=True)
    own = own.reshape(rows, 2 * KEYS)
    q_shape = (parts, agents * local, width + LANES) if blocked else (rows, width + LANES)
    q = call(
        functools.partial(query_kernel, agents, steps, local, blocked),
        [struct(q_shape, BF16)],
        [second, wq_space, meta],
        flops=2 * rows * width * width,
    )
    if not blocked:
        q = to_blocks(q, agents, steps, local)
    q, own = lax.optimization_barrier((q, own))
    swap = [(h, HALVES - 1 - h) for h in range(HALVES)]
    other = lax.ppermute(own, "half", swap)
    q = lax.all_to_all(q, spread, split_axis=0, concat_axis=0, tiled=True)

    block = max(COLS, local) if rows % max(COLS, local) == 0 else rows
    mix = call(
        functools.partial(space_kernel, local, block, tiles),
        [struct((rows, width), BF16)],
        [q.reshape(rows, width + LANES), own, other],
        scratch=[
            pltpu.VMEM((local, rows // local, width), BF16),
            pltpu.VMEM((local, HALVES * rows // local, 2 * KEYS), BF16),
            pltpu.VMEM((local, rows // local, width), BF16),
        ],
        flops=8 * rows * rows // local * width,
        mib=16 + 16 * GROUPS * HALVES * (rows // local) ** 2 // MIB,
    )
    mix = lax.all_to_all(
        mix.reshape(parts, agents * local, width), spread, split_axis=0, concat_axis=0, tiled=True
    )
    if not blocked:
        mix = from_blocks(mix, agents, steps, local)
    out = call(
        functools.partial(out_kernel, agents, steps, local, blocked),
        [struct((rows, width), BF16)],
        [mix.reshape(rows, width), mid, wo_space],
        flops=2 * rows * width * width,
    )
    return out.reshape(1, agents, steps, width)


def solution(mesh):
    tiles, members = mesh.devices.shape
    split = Mesh(
        mesh.devices.reshape(tiles, HALVES, members // HALVES), ("tile", "half", "rest")
    )
    states = P("tile", ("half", "rest"), None, None)
    listing = P("tile", None)
    return jax.shard_map(
        per_device,
        mesh=split,
        in_specs=(states,) + (P(),) * 8 + (listing,) * 3,
        out_specs=states,
        check_vma=False,
    )
```

```python
import functools
import math

import jax
import jax.numpy as jnp
from jax import lax
from jax.experimental import pallas as pl
from jax.experimental.pallas import tpu as pltpu
from jax.sharding import Mesh
from jax.sharding import PartitionSpec as P

HEADS = 16
KV_HEADS = 4
HEAD_DIM = 64
GROUPS = HEADS // KV_HEADS
KEYS = KV_HEADS * HEAD_DIM
WIDE = GROUPS * HEAD_DIM
SCALE = HEAD_DIM ** (-0.5)
EXP2_SCALE = SCALE * math.log2(math.e)
NEG = -1e30
LANES = 128
COLS = 256
HALVES = 2
MIB = 1024 * 1024
F32 = jnp.float32
BF16 = jnp.bfloat16
ROWS_BY_COLS = (((1,), (1,)), ((), ()))


def norm_rows(values, gain):
    wide = values.astype(F32)
    meansq = jnp.mean(wide * wide, axis=-1, keepdims=True)
    return (wide * lax.rsqrt(meansq + 1e-05) * gain).astype(BF16)


def to_blocks(values, agents, steps, local):
    split = values.reshape(agents, steps // local, local, values.shape[-1])
    return jnp.transpose(split, (1, 0, 2, 3)).reshape(steps // local, agents * local, values.shape[-1])


def from_blocks(values, agents, steps, local):
    split = values.reshape(steps // local, agents, local, values.shape[-1])
    return jnp.transpose(split, (1, 0, 2, 3)).reshape(agents * steps, values.shape[-1])


def time_kernel(
    agents, steps, local, blocked,
    hist_hbm, gain_t, gain_s, wq_hbm, wkv_hbm, wo_hbm, wkv2_hbm,
    mid_hbm, kv_out,
    hist, wq, wkv, wo, wkv2, normed, query, keyval, mix, mid, hist_sems, wq_sems, sems, out_sem,
):
    rows, width = hist.shape
    hist_loads, wq_loads = [], []
    for a in range(agents):
        part = pl.ds(a * steps, steps)
        hist_loads.append(
            pltpu.make_async_copy(hist_hbm.at[part, :], hist.at[part, :], hist_sems.at[a])
        )
    for c in range(0, width, COLS):
        cols = pl.ds(c, COLS)
        wq_loads.append(
            pltpu.make_async_copy(wq_hbm.at[:, cols], wq.at[:, cols], wq_sems.at[c // COLS])
        )
    loads = [
        pltpu.make_async_copy(source, target, sems.at[i])
        for i, (source, target) in enumerate(((wkv_hbm, wkv), (wo_hbm, wo), (wkv2_hbm, wkv2)))
    ]
    for load in hist_loads + wq_loads + loads:
        load.start()
    for a in range(agents):
        part = pl.ds(a * steps, steps)
        hist_loads[a].wait()
        normed[part, :] = norm_rows(hist[part, :], gain_t[...])
    for c in range(0, width, COLS):
        wq_loads[c // COLS].wait()
        query[:, c : c + COLS] = jnp.dot(
            normed[...], wq[:, c : c + COLS], preferred_element_type=F32
        ).astype(BF16)
    loads[0].wait()
    for c in range(0, 2 * KEYS, COLS):
        keyval[:, c : c + COLS] = jnp.dot(
            normed[...], wkv[:, c : c + COLS], preferred_element_type=F32
        ).astype(BF16)
    causal = lax.broadcasted_iota(jnp.int32, (steps, steps), 0) <= lax.broadcasted_iota(
        jnp.int32, (steps, steps), 1
    )
    causal = jnp.concatenate([causal] * GROUPS, axis=1)
    for a in range(agents):
        part = slice(a * steps, (a + 1) * steps)
        for k in range(KV_HEADS):
            wide = slice(k * WIDE, (k + 1) * WIDE)
            keys = keyval[part, k * HEAD_DIM : (k + 1) * HEAD_DIM]
            vals = keyval[part, KEYS + k * HEAD_DIM : KEYS + (k + 1) * HEAD_DIM]
            heads = query[part, wide].T
            heads = jnp.concatenate(
                [heads[j * HEAD_DIM : (j + 1) * HEAD_DIM] for j in range(GROUPS)], axis=1
            )
            scores = jnp.dot(keys, heads, preferred_element_type=F32)
            scores = jnp.where(causal, scores, NEG)
            top = jnp.max(scores, axis=0, keepdims=True)
            grown = jnp.exp2((scores - top) * EXP2_SCALE)
            sums = jnp.sum(grown, axis=0, keepdims=True)
            mixed = jnp.dot(vals.T, grown.astype(BF16), preferred_element_type=F32) * (1.0 / sums)
            mixed = jnp.concatenate(
                [mixed[:, j * steps : (j + 1) * steps] for j in range(GROUPS)], axis=0
            )
            mix[part, wide] = mixed.astype(BF16).T
    loads[1].wait()
    for c in range(0, width, COLS):
        cols = slice(c, c + COLS)
        projected = jnp.dot(mix[...], wo[:, cols], preferred_element_type=F32)
        mid[:, cols] = (hist[:, cols].astype(F32) + projected).astype(BF16)
    keep = pltpu.make_async_copy(mid, mid_hbm, out_sem)
    keep.start()
    for a in range(agents):
        part = pl.ds(a * steps, steps)
        normed[part, :] = norm_rows(mid[part, :], gain_s[...])
    loads[2].wait()
    for c in range(0, 2 * KEYS, COLS):
        cols = slice(c, c + COLS)
        result = jnp.dot(normed[...], wkv2[:, cols], preferred_element_type=F32)
        if blocked:
            kv_out[:, :, cols] = to_blocks(result, agents, steps, local).astype(BF16)
        else:
            kv_out[:, cols] = result.astype(BF16)
    keep.wait()


def query_kernel(agents, steps, local, blocked, mid, gain, wq, meta, out, second):
    width = mid.shape[1]
    for a in range(agents):
        part = pl.ds(a * steps, steps)
        second[part, :] = norm_rows(mid[part, :], gain[...])
    for c in range(0, width, COLS):
        cols = slice(c, c + COLS)
        result = jnp.dot(second[...], wq[:, cols], preferred_element_type=F32)
        if blocked:
            out[:, :, cols] = to_blocks(result, agents, steps, local).astype(BF16)
        else:
            out[:, cols] = result.astype(BF16)
    lines = jnp.broadcast_to(meta[0:1, :], (out.shape[-2], LANES)).astype(BF16)
    if blocked:
        out[:, :, width:] = jnp.broadcast_to(lines[None], (out.shape[0], out.shape[1], LANES))
    else:
        out[:, width:] = lines


def one_hot(shape, group, local, dtype=BF16):
    row = lax.broadcasted_iota(jnp.int32, shape, 0)
    col = lax.broadcasted_iota(jnp.int32, shape, 1)
    wanted = (row % group) * local + row // group
    return jnp.where(col == wanted, 1.0, 0.0).astype(dtype)


def key_weights(notes, local, tiles, total):
    rows = notes.shape[0]
    group = total // tiles
    shape = (total, rows)
    row, col = (lax.broadcasted_iota(jnp.int32, shape, d) for d in range(2))
    pick = jnp.where(col == row * local, 1.0, 0.0).astype(BF16)
    lines = jnp.dot(pick, notes, preferred_element_type=F32).astype(BF16)
    shape = (LANES, HALVES * total)
    lane, key = (lax.broadcasted_iota(jnp.int32, shape, d) for d in range(2))
    half, tile, agent = key // total, key % total // group, key % group
    spread = jnp.where(lane == HALVES * group + tile, 1.0, 0.0).astype(BF16)
    listed = jnp.dot(lines, spread, preferred_element_type=F32)
    spread = jnp.where(lane == half * group + agent, 1.0, 0.0).astype(BF16)
    alive = jnp.dot(lines, spread, preferred_element_type=F32)
    shape = (total, HALVES * total)
    row, key = (lax.broadcasted_iota(jnp.int32, shape, d) for d in range(2))
    first = row == key % total // group * group
    alive = jnp.sum(jnp.where(first, alive, 0.0), axis=0, keepdims=True)
    return listed * alive


def space_kernel(
    local, block, tiles, q_in, own, other, out, query, keyval, mix
):
    rows, width = out.shape
    group = block // local
    total = rows // local
    weight = key_weights(q_in[:, width:], local, tiles, total)
    if local > 1:
        order = one_hot((block, block), group, local)

    def by_steps(source, target, offset, cols):
        for b in range(rows // block):
            piece = source[b * block : (b + 1) * block, cols]
            if local > 1:
                piece = jnp.dot(order, piece, preferred_element_type=F32).astype(BF16)
            target[:, offset + b * group : offset + (b + 1) * group, cols] = piece.reshape(
                local, group, piece.shape[1]
            )

    for c in range(0, width, COLS):
        by_steps(q_in, query, 0, slice(c, c + COLS))
    for c in range(0, 2 * KEYS, COLS):
        by_steps(own, keyval, 0, slice(c, c + COLS))
        by_steps(other, keyval, total, slice(c, c + COLS))

    def one_step(s, carry):
        mask = jnp.concatenate([weight] * GROUPS, axis=0)
        for k in range(KV_HEADS):
            wide = slice(k * WIDE, (k + 1) * WIDE)
            heads = query[s, :, wide]
            heads = jnp.concatenate(
                [heads[:, j * HEAD_DIM : (j + 1) * HEAD_DIM] for j in range(GROUPS)], axis=0
            )
            keys = keyval[s, :, k * HEAD_DIM : (k + 1) * HEAD_DIM]
            vals = keyval[s, :, KEYS + k * HEAD_DIM : KEYS + (k + 1) * HEAD_DIM]
            scores = lax.dot_general(heads, keys, ROWS_BY_COLS, preferred_element_type=F32)
            scores = jnp.where(mask > 0, scores, NEG)
            top = jnp.max(scores, axis=-1, keepdims=True)
            grown = jnp.exp2((scores - top) * EXP2_SCALE) * mask
            sums = jnp.sum(grown, axis=-1, keepdims=True)
            mixed = jnp.dot(grown.astype(BF16), vals, preferred_element_type=F32) / sums
            mixed = mixed.astype(BF16)
            mix[s, :, wide] = jnp.concatenate(
                [mixed[j * total : (j + 1) * total] for j in range(GROUPS)], axis=1
            )
        return carry

    lax.fori_loop(0, local, one_step, 0, unroll=2 if local % 2 == 0 else 1)
    for b in range(rows // block):
        for c in range(0, width, COLS):
            cols = slice(c, c + COLS)
            piece = mix[:, b * group : (b + 1) * group, cols].reshape(block, COLS)
            if local > 1:
                piece = lax.dot_general(
                    order, piece, (((0,), (0,)), ((), ())), preferred_element_type=F32
                ).astype(BF16)
            out[b * block : (b + 1) * block, cols] = piece


def out_kernel(agents, steps, local, blocked, mix, mid, wo, out):
    width = mid.shape[1]
    for c in range(0, width, COLS):
        cols = slice(c, c + COLS)
        projected = jnp.dot(mix[...], wo[:, cols], preferred_element_type=F32)
        if blocked:
            projected = from_blocks(projected, agents, steps, local)
        out[:, cols] = (mid[:, cols].astype(F32) + projected).astype(BF16)


def call(kernel, shapes, args, hbm=(), hbm_out=(), scratch=(), flops=0, mib=16):
    moved = sum(a.size * a.dtype.itemsize for a in args)
    moved += sum(s.size * s.dtype.itemsize for s in shapes)

    def specs(count, far):
        return [
            pl.BlockSpec(memory_space=pl.ANY if i in far else pltpu.VMEM) for i in range(count)
        ]

    results = pl.pallas_call(
        kernel,
        out_shape=list(shapes),
        in_specs=specs(len(args), hbm),
        out_specs=specs(len(shapes), hbm_out),
        scratch_shapes=list(scratch),
        compiler_params=pltpu.CompilerParams(vmem_limit_bytes=mib * MIB),
        cost_estimate=pl.CostEstimate(flops=flops, bytes_accessed=moved, transcendentals=0),
    )(*args)
    return results if len(shapes) > 1 else results[0]


def per_device(
    histories,
    gain_time,
    wq_time,
    wkv_time,
    wo_time,
    gain_space,
    wq_space,
    wkv_space,
    wo_space,
    neighbours,
    nbr_valid,
    agent_valid,
):
    agents, steps, width = histories.shape[1:]
    tiles, rest = lax.axis_size("tile"), lax.axis_size("rest")
    spread = ("tile", "rest")
    parts = tiles * rest
    local = steps // parts
    rows = agents * steps
    blocked = local % 8 == 0
    struct = jax.ShapeDtypeStruct

    hist = histories.reshape(rows, width)
    kv_shape = (parts, agents * local, 2 * KEYS) if blocked else (rows, 2 * KEYS)
    mid, kv = call(
        functools.partial(time_kernel, agents, steps, local, blocked),
        [struct((rows, width), BF16), struct(kv_shape, BF16)],
        [hist, gain_time[None], gain_space[None], wq_time, wkv_time, wo_time, wkv_space],
        hbm=(0, 3, 4, 5, 6),
        hbm_out=(0,),
        scratch=[
            pltpu.VMEM((rows, width), BF16),
            pltpu.VMEM(wq_time.shape, BF16),
            pltpu.VMEM(wkv_time.shape, BF16),
            pltpu.VMEM(wo_time.shape, BF16),
            pltpu.VMEM(wkv_space.shape, BF16),
            pltpu.VMEM((rows, width), BF16),
            pltpu.VMEM((rows, width), BF16),
            pltpu.VMEM((rows, 2 * KEYS), BF16),
            pltpu.VMEM((rows, width), BF16),
            pltpu.VMEM((rows, width), BF16),
            pltpu.SemaphoreType.DMA((agents,)),
            pltpu.SemaphoreType.DMA((width // COLS,)),
            pltpu.SemaphoreType.DMA((3,)),
            pltpu.SemaphoreType.DMA,
        ],
        flops=2 * rows * width * (2 * width + 4 * KEYS),
        mib=56,
    )
    if not blocked:
        kv = to_blocks(kv, agents, steps, local)
    listed = jnp.sum(
        jnp.where(
            neighbours[0][:, None] == jnp.arange(tiles)[None, :], nbr_valid[0][:, None], 0
        ),
        axis=0,
    )
    group = rest * agents
    alive = jnp.where(lax.axis_index("half") == 0, agent_valid[0], jnp.roll(agent_valid[0], -group))
    meta = jnp.concatenate([alive, listed])
    meta = jnp.pad(meta, (0, LANES - meta.shape[0])).astype(F32)
    meta = jnp.broadcast_to(meta[None], (8, LANES))
    own = lax.all_to_all(kv, spread, split_axis=0, concat_axis=0, tiled=True)
    own = own.reshape(rows, 2 * KEYS)
    q_shape = (parts, agents * local, width + LANES) if blocked else (rows, width + LANES)
    q = call(
        functools.partial(query_kernel, agents, steps, local, blocked),
        [struct(q_shape, BF16)],
        [mid, gain_space[None], wq_space, meta],
        scratch=[pltpu.VMEM((rows, width), BF16)],
        flops=2 * rows * width * width,
    )
    if not blocked:
        q = to_blocks(q, agents, steps, local)
    swap = [(h, HALVES - 1 - h) for h in range(HALVES)]
    other = lax.ppermute(own, "half", swap)
    q = lax.all_to_all(q, spread, split_axis=0, concat_axis=0, tiled=True)

    block = max(COLS, local) if rows % max(COLS, local) == 0 else rows
    mix = call(
        functools.partial(space_kernel, local, block, tiles),
        [struct((rows, width), BF16)],
        [q.reshape(rows, width + LANES), own, other],
        scratch=[
            pltpu.VMEM((local, rows // local, width), BF16),
            pltpu.VMEM((local, HALVES * rows // local, 2 * KEYS), BF16),
            pltpu.VMEM((local, rows // local, width), BF16),
        ],
        flops=8 * rows * rows // local * width,
        mib=16 + 16 * GROUPS * HALVES * (rows // local) ** 2 // MIB,
    )
    mix = lax.all_to_all(
        mix.reshape(parts, agents * local, width), spread, split_axis=0, concat_axis=0, tiled=True
    )
    if not blocked:
        mix = from_blocks(mix, agents, steps, local)
    out = call(
        functools.partial(out_kernel, agents, steps, local, blocked),
        [struct((rows, width), BF16)],
        [mix.reshape(rows, width), mid, wo_space],
        flops=2 * rows * width * width,
    )
    return out.reshape(1, agents, steps, width)


def solution(mesh):
    tiles, members = mesh.devices.shape
    split = Mesh(
        mesh.devices.reshape(tiles, HALVES, members // HALVES), ("tile", "half", "rest")
    )
    states = P("tile", ("half", "rest"), None, None)
    listing = P("tile", None)
    return jax.shard_map(
        per_device,
        mesh=split,
        in_specs=(states,) + (P(),) * 8 + (listing,) * 3,
        out_specs=states,
        check_vma=False,
    )
```

```python
import functools
import math

import jax
import jax.numpy as jnp
from jax import lax
from jax.experimental import pallas as pl
from jax.experimental.pallas import tpu as pltpu
from jax.sharding import Mesh
from jax.sharding import PartitionSpec as P

HEADS = 16
KV_HEADS = 4
HEAD_DIM = 64
GROUPS = HEADS // KV_HEADS
KEYS = KV_HEADS * HEAD_DIM
WIDE = GROUPS * HEAD_DIM
SCALE = HEAD_DIM ** (-0.5)
EXP2_SCALE = SCALE * math.log2(math.e)
NEG = -1e30
LANES = 128
COLS = 256
HALVES = 2
DEPTH = 2
MIB = 1024 * 1024
F32 = jnp.float32
BF16 = jnp.bfloat16
ROWS_BY_COLS = (((1,), (1,)), ((), ()))


def norm_rows(values, gain):
    wide = values.astype(F32)
    meansq = jnp.mean(wide * wide, axis=-1, keepdims=True)
    return (wide * lax.rsqrt(meansq + 1e-05) * gain).astype(BF16)


def to_blocks(values, agents, steps, local):
    split = values.reshape(agents, steps // local, local, values.shape[-1])
    return jnp.transpose(split, (1, 0, 2, 3)).reshape(steps // local, agents * local, values.shape[-1])


def from_blocks(values, agents, steps, local):
    split = values.reshape(steps // local, agents, local, values.shape[-1])
    return jnp.transpose(split, (1, 0, 2, 3)).reshape(agents * steps, values.shape[-1])


def staggered(units, first, second, third):
    scores, grown = {}, {}
    for i in range(len(units) + 2 * DEPTH):
        if i < len(units):
            scores[i] = first(*units[i])
        if 0 <= i - DEPTH < len(units):
            grown[i - DEPTH] = second(scores.pop(i - DEPTH))
        if 0 <= i - 2 * DEPTH < len(units):
            third(units[i - 2 * DEPTH], *grown.pop(i - 2 * DEPTH))


def time_kernel(
    agents, steps, local, blocked,
    hist_hbm, gain_t, gain_s, wq_hbm, wkv_hbm, wo_hbm, wkv2_hbm,
    mid_hbm, kv_out,
    hist, wq, wkv, wo, wkv2, normed, query, keyval, mix, mid, hist_sems, wq_sems, sems, out_sem,
):
    rows, width = hist.shape
    hist_loads, wq_loads = [], []
    for a in range(agents):
        part = pl.ds(a * steps, steps)
        hist_loads.append(
            pltpu.make_async_copy(hist_hbm.at[part, :], hist.at[part, :], hist_sems.at[a])
        )
    for c in range(0, width, COLS):
        cols = pl.ds(c, COLS)
        wq_loads.append(
            pltpu.make_async_copy(wq_hbm.at[:, cols], wq.at[:, cols], wq_sems.at[c // COLS])
        )
    loads = [
        pltpu.make_async_copy(source, target, sems.at[i])
        for i, (source, target) in enumerate(((wkv_hbm, wkv), (wo_hbm, wo), (wkv2_hbm, wkv2)))
    ]
    for load in hist_loads + loads[:1]:
        load.start()
    for a in range(agents):
        part = pl.ds(a * steps, steps)
        hist_loads[a].wait()
        if a == 0:
            for load in wq_loads:
                load.start()
        normed[part, :] = norm_rows(hist[part, :], gain_t[...])
    loads[0].wait()
    for c in range(0, 2 * KEYS, COLS):
        keyval[:, c : c + COLS] = jnp.dot(
            normed[...], wkv[:, c : c + COLS], preferred_element_type=F32
        ).astype(BF16)
    for load in loads[1:]:
        load.start()
    for c in range(0, width, COLS):
        wq_loads[c // COLS].wait()
        query[:, c : c + COLS] = jnp.dot(
            normed[...], wq[:, c : c + COLS], preferred_element_type=F32
        ).astype(BF16)
    causal = lax.broadcasted_iota(jnp.int32, (steps, steps), 0) <= lax.broadcasted_iota(
        jnp.int32, (steps, steps), 1
    )
    causal = jnp.concatenate([causal] * GROUPS, axis=1)

    def scores_of(a, k):
        part = slice(a * steps, (a + 1) * steps)
        heads = query[part, k * WIDE : (k + 1) * WIDE].T
        heads = jnp.concatenate(
            [heads[j * HEAD_DIM : (j + 1) * HEAD_DIM] for j in range(GROUPS)], axis=1
        )
        keys = keyval[part, k * HEAD_DIM : (k + 1) * HEAD_DIM]
        return jnp.dot(keys, heads, preferred_element_type=F32)

    def grow(scores):
        scores = jnp.where(causal, scores, NEG)
        top = jnp.max(scores, axis=0, keepdims=True)
        grown = jnp.exp2((scores - top) * EXP2_SCALE)
        return grown.astype(BF16), jnp.sum(grown, axis=0, keepdims=True)

    def values_of(unit, grown, sums):
        a, k = unit
        part = slice(a * steps, (a + 1) * steps)
        vals = keyval[part, KEYS + k * HEAD_DIM : KEYS + (k + 1) * HEAD_DIM]
        mixed = jnp.dot(vals.T, grown, preferred_element_type=F32) * (1.0 / sums)
        mixed = jnp.concatenate(
            [mixed[:, j * steps : (j + 1) * steps] for j in range(GROUPS)], axis=0
        )
        mix[part, k * WIDE : (k + 1) * WIDE] = mixed.astype(BF16).T

    units = [(a, k) for a in range(agents) for k in range(KV_HEADS)]
    staggered(units, scores_of, grow, values_of)
    loads[1].wait()
    for c in range(0, width, COLS):
        cols = slice(c, c + COLS)
        projected = jnp.dot(mix[...], wo[:, cols], preferred_element_type=F32)
        mid[:, cols] = (hist[:, cols].astype(F32) + projected).astype(BF16)
    keep = pltpu.make_async_copy(mid, mid_hbm, out_sem)
    keep.start()
    for a in range(agents):
        part = pl.ds(a * steps, steps)
        normed[part, :] = norm_rows(mid[part, :], gain_s[...])
    loads[2].wait()
    for c in range(0, 2 * KEYS, COLS):
        cols = slice(c, c + COLS)
        result = jnp.dot(normed[...], wkv2[:, cols], preferred_element_type=F32)
        if blocked:
            kv_out[:, :, cols] = to_blocks(result, agents, steps, local).astype(BF16)
        else:
            kv_out[:, cols] = result.astype(BF16)
    keep.wait()


def query_kernel(agents, steps, local, blocked, mid, gain, wq, meta, out, second):
    width = mid.shape[1]
    for a in range(agents):
        part = pl.ds(a * steps, steps)
        second[part, :] = norm_rows(mid[part, :], gain[...])
    for c in range(0, width, COLS):
        cols = slice(c, c + COLS)
        result = jnp.dot(second[...], wq[:, cols], preferred_element_type=F32)
        if blocked:
            out[:, :, cols] = to_blocks(result, agents, steps, local).astype(BF16)
        else:
            out[:, cols] = result.astype(BF16)
    lines = jnp.broadcast_to(meta[0:1, :], (out.shape[-2], LANES)).astype(BF16)
    if blocked:
        out[:, :, width:] = jnp.broadcast_to(lines[None], (out.shape[0], out.shape[1], LANES))
    else:
        out[:, width:] = lines


def one_hot(shape, group, local, dtype=BF16):
    row = lax.broadcasted_iota(jnp.int32, shape, 0)
    col = lax.broadcasted_iota(jnp.int32, shape, 1)
    wanted = (row % group) * local + row // group
    return jnp.where(col == wanted, 1.0, 0.0).astype(dtype)


def key_weights(notes, local, tiles, total):
    rows = notes.shape[0]
    group = total // tiles
    shape = (total, rows)
    row, col = (lax.broadcasted_iota(jnp.int32, shape, d) for d in range(2))
    pick = jnp.where(col == row * local, 1.0, 0.0).astype(BF16)
    lines = jnp.dot(pick, notes, preferred_element_type=F32).astype(BF16)
    shape = (LANES, HALVES * total)
    lane, key = (lax.broadcasted_iota(jnp.int32, shape, d) for d in range(2))
    half, tile, agent = key // total, key % total // group, key % group
    spread = jnp.where(lane == HALVES * group + tile, 1.0, 0.0).astype(BF16)
    listed = jnp.dot(lines, spread, preferred_element_type=F32)
    spread = jnp.where(lane == half * group + agent, 1.0, 0.0).astype(BF16)
    alive = jnp.dot(lines, spread, preferred_element_type=F32)
    shape = (total, HALVES * total)
    row, key = (lax.broadcasted_iota(jnp.int32, shape, d) for d in range(2))
    first = row == key % total // group * group
    alive = jnp.sum(jnp.where(first, alive, 0.0), axis=0, keepdims=True)
    return listed * alive


def by_steps(source, target, local, block, total, offset=0):
    rows, width = source.shape[0], target.shape[-1]
    group = block // local
    order = one_hot((block, block), group, local)
    for c in range(0, width, COLS):
        cols = slice(c, c + COLS)
        for b in range(rows // block):
            piece = source[b * block : (b + 1) * block, cols]
            if local > 1:
                piece = jnp.dot(order, piece, preferred_element_type=F32).astype(BF16)
            at = offset + b * group
            target[:, at : at + group, cols] = piece.reshape(local, group, piece.shape[1])


def keys_kernel(local, block, source, out):
    by_steps(source, out, local, block, out.shape[1])


def space_kernel(
    local, block, tiles, pair, q_in, own, other_in, out, query, other, mix
):
    rows, width = out.shape
    group = block // local
    total = rows // local
    columns = pair * total
    by_steps(q_in, query, local, block, total)
    by_steps(other_in, other, local, block, total)
    weight = key_weights(q_in[:, width:], local, tiles, total)
    together = GROUPS if columns <= LANES else 1
    weight = jnp.concatenate([weight.T] * (pair * together), axis=1)
    valid = weight > 0
    lane = lax.broadcasted_iota(jnp.int32, (HEAD_DIM, columns), 1) // total

    def both(s, part):
        return jnp.concatenate([own[s, :, part], other[s, :, part]], axis=0)

    def scores_of(p, k, heads):
        turned = query[p * pair : (p + 1) * pair, :, k * WIDE : (k + 1) * WIDE]
        turned = turned.reshape(columns, WIDE).T
        turned = [turned[j * HEAD_DIM : (j + 1) * HEAD_DIM] for j in heads]
        if pair > 1:
            zero = jnp.zeros((HEAD_DIM, columns), BF16)
            turned = [
                jnp.concatenate([jnp.where(lane == s, t, zero) for s in range(pair)], axis=0)
                for t in turned
            ]
        part = slice(k * HEAD_DIM, (k + 1) * HEAD_DIM)
        keys = jnp.concatenate([both(p * pair + s, part) for s in range(pair)], axis=1)
        return jnp.dot(keys, jnp.concatenate(turned, axis=1), preferred_element_type=F32)

    def grow(scores):
        scores = jnp.where(valid, scores, NEG)
        top = jnp.max(scores, axis=0, keepdims=True)
        grown = jnp.exp2((scores - top) * EXP2_SCALE) * weight
        return grown.astype(BF16), jnp.sum(grown, axis=0, keepdims=True)

    def values_of(unit, grown, sums):
        p, k, heads = unit
        part = slice(KEYS + k * HEAD_DIM, KEYS + (k + 1) * HEAD_DIM)
        vals = jnp.concatenate([both(p * pair + s, part).T for s in range(pair)], axis=0)
        mixed = jnp.dot(vals, grown, preferred_element_type=F32)
        inverse = 1.0 / sums
        parts = []
        for i in range(len(heads)):
            cols = slice(i * columns, (i + 1) * columns)
            chosen = mixed[:HEAD_DIM, cols]
            for s in range(1, pair):
                chosen = jnp.where(lane == s, mixed[s * HEAD_DIM : (s + 1) * HEAD_DIM, cols], chosen)
            parts.append(chosen * inverse[:, cols])
        mixed = jnp.concatenate(parts, axis=0).astype(BF16).T
        start = k * WIDE + heads[0] * HEAD_DIM
        mix[p * pair : (p + 1) * pair, :, start : start + len(heads) * HEAD_DIM] = mixed.reshape(
            pair, total, len(heads) * HEAD_DIM
        )

    units = [
        (p, k, tuple(range(j, j + together)))
        for p in range(local // pair)
        for k in range(KV_HEADS)
        for j in range(0, GROUPS, together)
    ]
    staggered(units, scores_of, grow, values_of)
    order = one_hot((block, block), group, local)
    for b in range(rows // block):
        for c in range(0, width, COLS):
            cols = slice(c, c + COLS)
            piece = mix[:, b * group : (b + 1) * group, cols].reshape(block, COLS)
            if local > 1:
                piece = lax.dot_general(
                    order, piece, (((0,), (0,)), ((), ())), preferred_element_type=F32
                ).astype(BF16)
            out[b * block : (b + 1) * block, cols] = piece


def out_kernel(agents, steps, local, blocked, mix, mid, wo, out):
    width = mid.shape[1]
    for c in range(0, width, COLS):
        cols = slice(c, c + COLS)
        projected = jnp.dot(mix[...], wo[:, cols], preferred_element_type=F32)
        if blocked:
            projected = from_blocks(projected, agents, steps, local)
        out[:, cols] = (mid[:, cols].astype(F32) + projected).astype(BF16)


def call(kernel, shapes, args, hbm=(), hbm_out=(), scratch=(), flops=0, mib=16):
    moved = sum(a.size * a.dtype.itemsize for a in args)
    moved += sum(s.size * s.dtype.itemsize for s in shapes)

    def specs(count, far):
        return [
            pl.BlockSpec(memory_space=pl.ANY if i in far else pltpu.VMEM) for i in range(count)
        ]

    results = pl.pallas_call(
        kernel,
        out_shape=list(shapes),
        in_specs=specs(len(args), hbm),
        out_specs=specs(len(shapes), hbm_out),
        scratch_shapes=list(scratch),
        compiler_params=pltpu.CompilerParams(vmem_limit_bytes=mib * MIB),
        cost_estimate=pl.CostEstimate(flops=flops, bytes_accessed=moved, transcendentals=0),
    )(*args)
    return results if len(shapes) > 1 else results[0]


def per_device(
    histories,
    gain_time,
    wq_time,
    wkv_time,
    wo_time,
    gain_space,
    wq_space,
    wkv_space,
    wo_space,
    neighbours,
    nbr_valid,
    agent_valid,
):
    agents, steps, width = histories.shape[1:]
    tiles, rest = lax.axis_size("tile"), lax.axis_size("rest")
    spread = ("tile", "rest")
    parts = tiles * rest
    local = steps // parts
    rows = agents * steps
    blocked = local % 8 == 0
    struct = jax.ShapeDtypeStruct

    hist = histories.reshape(rows, width)
    kv_shape = (parts, agents * local, 2 * KEYS) if blocked else (rows, 2 * KEYS)
    mid, kv = call(
        functools.partial(time_kernel, agents, steps, local, blocked),
        [struct((rows, width), BF16), struct(kv_shape, BF16)],
        [hist, gain_time[None], gain_space[None], wq_time, wkv_time, wo_time, wkv_space],
        hbm=(0, 3, 4, 5, 6),
        hbm_out=(0,),
        scratch=[
            pltpu.VMEM((rows, width), BF16),
            pltpu.VMEM(wq_time.shape, BF16),
            pltpu.VMEM(wkv_time.shape, BF16),
            pltpu.VMEM(wo_time.shape, BF16),
            pltpu.VMEM(wkv_space.shape, BF16),
            pltpu.VMEM((rows, width), BF16),
            pltpu.VMEM((rows, width), BF16),
            pltpu.VMEM((rows, 2 * KEYS), BF16),
            pltpu.VMEM((rows, width), BF16),
            pltpu.VMEM((rows, width), BF16),
            pltpu.SemaphoreType.DMA((agents,)),
            pltpu.SemaphoreType.DMA((width // COLS,)),
            pltpu.SemaphoreType.DMA((3,)),
            pltpu.SemaphoreType.DMA,
        ],
        flops=2 * rows * width * (2 * width + 4 * KEYS),
        mib=56,
    )
    if not blocked:
        kv = to_blocks(kv, agents, steps, local)
    listed = jnp.sum(
        jnp.where(
            neighbours[0][:, None] == jnp.arange(tiles)[None, :], nbr_valid[0][:, None], 0
        ),
        axis=0,
    )
    group = rest * agents
    alive = jnp.where(lax.axis_index("half") == 0, agent_valid[0], jnp.roll(agent_valid[0], -group))
    meta = jnp.concatenate([alive, listed])
    meta = jnp.pad(meta, (0, LANES - meta.shape[0])).astype(F32)
    meta = jnp.broadcast_to(meta[None], (8, LANES))
    own = lax.all_to_all(kv, spread, split_axis=0, concat_axis=0, tiled=True)
    own = own.reshape(rows, 2 * KEYS)
    q_shape = (parts, agents * local, width + LANES) if blocked else (rows, width + LANES)
    q = call(
        functools.partial(query_kernel, agents, steps, local, blocked),
        [struct(q_shape, BF16)],
        [mid, gain_space[None], wq_space, meta],
        scratch=[pltpu.VMEM((rows, width), BF16)],
        flops=2 * rows * width * width,
    )
    if not blocked:
        q = to_blocks(q, agents, steps, local)
    swap = [(h, HALVES - 1 - h) for h in range(HALVES)]
    other = lax.ppermute(own, "half", swap)
    total = rows // local
    block = max(COLS, local) if rows % max(COLS, local) == 0 else rows
    own = call(
        functools.partial(keys_kernel, local, block),
        [struct((local, total, 2 * KEYS), BF16)],
        [own],
        flops=2 * rows * block * 2 * KEYS,
    )
    q, own = lax.optimization_barrier((q, own))
    q = lax.all_to_all(q, spread, split_axis=0, concat_axis=0, tiled=True)

    pair = LANES // total if total < LANES and local % (LANES // total) == 0 else 1
    mix = call(
        functools.partial(space_kernel, local, block, tiles, pair),
        [struct((rows, width), BF16)],
        [q.reshape(rows, width + LANES), own, other],
        scratch=[
            pltpu.VMEM((local, total, width), BF16),
            pltpu.VMEM((local, total, 2 * KEYS), BF16),
            pltpu.VMEM((local, total, width), BF16),
        ],
        flops=8 * rows * total * width,
        mib=16 + 16 * GROUPS * HALVES * total**2 // MIB,
    )
    mix = lax.all_to_all(
        mix.reshape(parts, agents * local, width), spread, split_axis=0, concat_axis=0, tiled=True
    )
    if not blocked:
        mix = from_blocks(mix, agents, steps, local)
    out = call(
        functools.partial(out_kernel, agents, steps, local, blocked),
        [struct((rows, width), BF16)],
        [mix.reshape(rows, width), mid, wo_space],
        flops=2 * rows * width * width,
    )
    return out.reshape(1, agents, steps, width)


def solution(mesh):
    tiles, members = mesh.devices.shape
    split = Mesh(
        mesh.devices.reshape(tiles, HALVES, members // HALVES), ("tile", "half", "rest")
    )
    states = P("tile", ("half", "rest"), None, None)
    listing = P("tile", None)
    return jax.shard_map(
        per_device,
        mesh=split,
        in_specs=(states,) + (P(),) * 8 + (listing,) * 3,
        out_specs=states,
        check_vma=False,
    )
```

```python
import functools
import math

import jax
import jax.numpy as jnp
from jax import lax
from jax.experimental import pallas as pl
from jax.experimental.pallas import tpu as pltpu
from jax.sharding import Mesh
from jax.sharding import PartitionSpec as P

HEADS = 16
KV_HEADS = 4
HEAD_DIM = 64
GROUPS = HEADS // KV_HEADS
KEYS = KV_HEADS * HEAD_DIM
WIDE = GROUPS * HEAD_DIM
SCALE = HEAD_DIM ** (-0.5)
EXP2_SCALE = SCALE * math.log2(math.e)
NEG = -1e30
LANES = 128
COLS = 256
HALVES = 2
DEPTH = 2
SHADOW = 10000
MIB = 1024 * 1024
F32 = jnp.float32
BF16 = jnp.bfloat16
ROWS_BY_COLS = (((1,), (1,)), ((), ()))


def norm_rows(values, gain):
    wide = values.astype(F32)
    meansq = jnp.mean(wide * wide, axis=-1, keepdims=True)
    return (wide * lax.rsqrt(meansq + 1e-05) * gain).astype(BF16)


def to_blocks(values, agents, steps, local):
    split = values.reshape(agents, steps // local, local, values.shape[-1])
    return jnp.transpose(split, (1, 0, 2, 3)).reshape(steps // local, agents * local, values.shape[-1])


def from_blocks(values, agents, steps, local):
    split = values.reshape(steps // local, agents, local, values.shape[-1])
    return jnp.transpose(split, (1, 0, 2, 3)).reshape(agents * steps, values.shape[-1])


def staggered(units, first, second, third):
    scores, grown = {}, {}
    for i in range(len(units) + 2 * DEPTH):
        if i < len(units):
            scores[i] = first(*units[i])
        if 0 <= i - DEPTH < len(units):
            grown[i - DEPTH] = second(scores.pop(i - DEPTH))
        if 0 <= i - 2 * DEPTH < len(units):
            third(units[i - 2 * DEPTH], *grown.pop(i - 2 * DEPTH))


def time_kernel(
    agents, steps, local, blocked,
    hist_hbm, gain_t, gain_s, wq_hbm, wkv_hbm, wo_hbm, wkv2_hbm,
    mid_hbm, kv_out,
    hist, wq, wkv, wo, wkv2, normed, query, keyval, mix, mid, hist_sems, wq_sems, sems, out_sem,
):
    rows, width = hist.shape
    hist_loads, wq_loads = [], []
    for a in range(agents):
        part = pl.ds(a * steps, steps)
        hist_loads.append(
            pltpu.make_async_copy(hist_hbm.at[part, :], hist.at[part, :], hist_sems.at[a])
        )
    for c in range(0, width, COLS):
        cols = pl.ds(c, COLS)
        wq_loads.append(
            pltpu.make_async_copy(wq_hbm.at[:, cols], wq.at[:, cols], wq_sems.at[c // COLS])
        )
    loads = [
        pltpu.make_async_copy(source, target, sems.at[i])
        for i, (source, target) in enumerate(((wkv_hbm, wkv), (wo_hbm, wo), (wkv2_hbm, wkv2)))
    ]
    for load in hist_loads + loads[:1]:
        load.start()
    for a in range(agents):
        part = pl.ds(a * steps, steps)
        hist_loads[a].wait()
        if a == 0:
            for load in wq_loads:
                load.start()
        normed[part, :] = norm_rows(hist[part, :], gain_t[...])
    loads[0].wait()
    for c in range(0, 2 * KEYS, COLS):
        keyval[:, c : c + COLS] = jnp.dot(
            normed[...], wkv[:, c : c + COLS], preferred_element_type=F32
        ).astype(BF16)
    for load in loads[1:]:
        load.start()
    for c in range(0, width, COLS):
        wq_loads[c // COLS].wait()
        query[:, c : c + COLS] = jnp.dot(
            normed[...], wq[:, c : c + COLS], preferred_element_type=F32
        ).astype(BF16)
    causal = lax.broadcasted_iota(jnp.int32, (steps, steps), 0) <= lax.broadcasted_iota(
        jnp.int32, (steps, steps), 1
    )
    causal = jnp.concatenate([causal] * GROUPS, axis=1)

    def scores_of(a, k):
        part = slice(a * steps, (a + 1) * steps)
        heads = query[part, k * WIDE : (k + 1) * WIDE].T
        heads = jnp.concatenate(
            [heads[j * HEAD_DIM : (j + 1) * HEAD_DIM] for j in range(GROUPS)], axis=1
        )
        keys = keyval[part, k * HEAD_DIM : (k + 1) * HEAD_DIM]
        return jnp.dot(keys, heads, preferred_element_type=F32)

    def grow(scores):
        scores = jnp.where(causal, scores, NEG)
        top = jnp.max(scores, axis=0, keepdims=True)
        grown = jnp.exp2((scores - top) * EXP2_SCALE)
        return grown.astype(BF16), jnp.sum(grown, axis=0, keepdims=True)

    def values_of(unit, grown, sums):
        a, k = unit
        part = slice(a * steps, (a + 1) * steps)
        vals = keyval[part, KEYS + k * HEAD_DIM : KEYS + (k + 1) * HEAD_DIM]
        mixed = jnp.dot(vals.T, grown, preferred_element_type=F32) * (1.0 / sums)
        mixed = jnp.concatenate(
            [mixed[:, j * steps : (j + 1) * steps] for j in range(GROUPS)], axis=0
        )
        mix[part, k * WIDE : (k + 1) * WIDE] = mixed.astype(BF16).T

    units = [(a, k) for a in range(agents) for k in range(KV_HEADS)]
    staggered(units, scores_of, grow, values_of)
    loads[1].wait()
    for c in range(0, width, COLS):
        cols = slice(c, c + COLS)
        projected = jnp.dot(mix[...], wo[:, cols], preferred_element_type=F32)
        mid[:, cols] = (hist[:, cols].astype(F32) + projected).astype(BF16)
    keep = pltpu.make_async_copy(mid, mid_hbm, out_sem)
    keep.start()
    for a in range(agents):
        part = pl.ds(a * steps, steps)
        normed[part, :] = norm_rows(mid[part, :], gain_s[...])
    loads[2].wait()
    for c in range(0, 2 * KEYS, COLS):
        cols = slice(c, c + COLS)
        result = jnp.dot(normed[...], wkv2[:, cols], preferred_element_type=F32)
        if blocked:
            kv_out[:, :, cols] = to_blocks(result, agents, steps, local).astype(BF16)
        else:
            kv_out[:, cols] = result.astype(BF16)
    keep.wait()


def query_kernel(agents, steps, local, blocked, mid, gain, wq, meta, out, second):
    width = mid.shape[1]
    for a in range(agents):
        part = pl.ds(a * steps, steps)
        second[part, :] = norm_rows(mid[part, :], gain[...])
    for c in range(0, width, COLS):
        cols = slice(c, c + COLS)
        result = jnp.dot(second[...], wq[:, cols], preferred_element_type=F32)
        if blocked:
            out[:, :, cols] = to_blocks(result, agents, steps, local).astype(BF16)
        else:
            out[:, cols] = result.astype(BF16)
    lines = jnp.broadcast_to(meta[0:1, :], (out.shape[-2], LANES)).astype(BF16)
    if blocked:
        out[:, :, width:] = jnp.broadcast_to(lines[None], (out.shape[0], out.shape[1], LANES))
    else:
        out[:, width:] = lines


def one_hot(shape, group, local, dtype=BF16):
    row = lax.broadcasted_iota(jnp.int32, shape, 0)
    col = lax.broadcasted_iota(jnp.int32, shape, 1)
    wanted = (row % group) * local + row // group
    return jnp.where(col == wanted, 1.0, 0.0).astype(dtype)


def key_weights(notes, local, tiles, total):
    rows = notes.shape[0]
    group = total // tiles
    shape = (total, rows)
    row, col = (lax.broadcasted_iota(jnp.int32, shape, d) for d in range(2))
    pick = jnp.where(col == row * local, 1.0, 0.0).astype(BF16)
    lines = jnp.dot(pick, notes, preferred_element_type=F32).astype(BF16)
    shape = (LANES, HALVES * total)
    lane, key = (lax.broadcasted_iota(jnp.int32, shape, d) for d in range(2))
    half, tile, agent = key // total, key % total // group, key % group
    spread = jnp.where(lane == HALVES * group + tile, 1.0, 0.0).astype(BF16)
    listed = jnp.dot(lines, spread, preferred_element_type=F32)
    spread = jnp.where(lane == half * group + agent, 1.0, 0.0).astype(BF16)
    alive = jnp.dot(lines, spread, preferred_element_type=F32)
    shape = (total, HALVES * total)
    row, key = (lax.broadcasted_iota(jnp.int32, shape, d) for d in range(2))
    first = row == key % total // group * group
    alive = jnp.sum(jnp.where(first, alive, 0.0), axis=0, keepdims=True)
    return listed * alive


def by_steps(source, target, local, block, total, offset=0):
    rows, width = source.shape[0], target.shape[-1]
    group = block // local
    order = one_hot((block, block), group, local)
    for c in range(0, width, COLS):
        cols = slice(c, c + COLS)
        for b in range(rows // block):
            piece = source[b * block : (b + 1) * block, cols]
            if local > 1:
                piece = jnp.dot(order, piece, preferred_element_type=F32).astype(BF16)
            at = offset + b * group
            target[:, at : at + group, cols] = piece.reshape(local, group, piece.shape[1])


def keys_kernel(local, block, source, out):
    by_steps(source, out, local, block, out.shape[1])


def space_kernel(
    local, block, tiles, pair, q_in, own, other_in, out, query, other, mix
):
    rows, width = out.shape
    group = block // local
    total = rows // local
    columns = pair * total
    by_steps(q_in, query, local, block, total)
    by_steps(other_in, other, local, block, total)
    weight = key_weights(q_in[:, width:], local, tiles, total)
    together = GROUPS if columns <= LANES else 1
    weight = jnp.concatenate([weight.T] * (pair * together), axis=1)
    valid = weight > 0
    lane = lax.broadcasted_iota(jnp.int32, (HEAD_DIM, columns), 1) // total

    def both(s, part):
        return jnp.concatenate([own[s, :, part], other[s, :, part]], axis=0)

    def scores_of(p, k, heads):
        turned = query[p * pair : (p + 1) * pair, :, k * WIDE : (k + 1) * WIDE]
        turned = turned.reshape(columns, WIDE).T
        turned = [turned[j * HEAD_DIM : (j + 1) * HEAD_DIM] for j in heads]
        if pair > 1:
            zero = jnp.zeros((HEAD_DIM, columns), BF16)
            turned = [
                jnp.concatenate([jnp.where(lane == s, t, zero) for s in range(pair)], axis=0)
                for t in turned
            ]
        part = slice(k * HEAD_DIM, (k + 1) * HEAD_DIM)
        keys = jnp.concatenate([both(p * pair + s, part) for s in range(pair)], axis=1)
        return jnp.dot(keys, jnp.concatenate(turned, axis=1), preferred_element_type=F32)

    def grow(scores):
        scores = jnp.where(valid, scores, NEG)
        top = jnp.max(scores, axis=0, keepdims=True)
        grown = jnp.exp2((scores - top) * EXP2_SCALE) * weight
        return grown.astype(BF16), jnp.sum(grown, axis=0, keepdims=True)

    def values_of(unit, grown, sums):
        p, k, heads = unit
        part = slice(KEYS + k * HEAD_DIM, KEYS + (k + 1) * HEAD_DIM)
        vals = jnp.concatenate([both(p * pair + s, part).T for s in range(pair)], axis=0)
        mixed = jnp.dot(vals, grown, preferred_element_type=F32)
        inverse = 1.0 / sums
        parts = []
        for i in range(len(heads)):
            cols = slice(i * columns, (i + 1) * columns)
            chosen = mixed[:HEAD_DIM, cols]
            for s in range(1, pair):
                chosen = jnp.where(lane == s, mixed[s * HEAD_DIM : (s + 1) * HEAD_DIM, cols], chosen)
            parts.append(chosen * inverse[:, cols])
        mixed = jnp.concatenate(parts, axis=0).astype(BF16).T
        start = k * WIDE + heads[0] * HEAD_DIM
        mix[p * pair : (p + 1) * pair, :, start : start + len(heads) * HEAD_DIM] = mixed.reshape(
            pair, total, len(heads) * HEAD_DIM
        )

    units = [
        (p, k, tuple(range(j, j + together)))
        for p in range(local // pair)
        for k in range(KV_HEADS)
        for j in range(0, GROUPS, together)
    ]
    staggered(units, scores_of, grow, values_of)
    order = one_hot((block, block), group, local)
    for b in range(rows // block):
        for c in range(0, width, COLS):
            cols = slice(c, c + COLS)
            piece = mix[:, b * group : (b + 1) * group, cols].reshape(block, COLS)
            if local > 1:
                piece = lax.dot_general(
                    order, piece, (((0,), (0,)), ((), ())), preferred_element_type=F32
                ).astype(BF16)
            out[b * block : (b + 1) * block, cols] = piece


def out_kernel(agents, steps, local, blocked, mix, mid, wo, out):
    width = mid.shape[1]
    for c in range(0, width, COLS):
        cols = slice(c, c + COLS)
        projected = jnp.dot(mix[...], wo[:, cols], preferred_element_type=F32)
        if blocked:
            projected = from_blocks(projected, agents, steps, local)
        out[:, cols] = (mid[:, cols].astype(F32) + projected).astype(BF16)


def call(kernel, shapes, args, hbm=(), hbm_out=(), scratch=(), flops=0, mib=16):
    moved = sum(a.size * a.dtype.itemsize for a in args)
    moved += sum(s.size * s.dtype.itemsize for s in shapes)

    def specs(count, far):
        return [
            pl.BlockSpec(memory_space=pl.ANY if i in far else pltpu.VMEM) for i in range(count)
        ]

    results = pl.pallas_call(
        kernel,
        out_shape=list(shapes),
        in_specs=specs(len(args), hbm),
        out_specs=specs(len(shapes), hbm_out),
        scratch_shapes=list(scratch),
        compiler_params=pltpu.CompilerParams(vmem_limit_bytes=mib * MIB),
        cost_estimate=pl.CostEstimate(flops=flops, bytes_accessed=moved, transcendentals=0),
    )(*args)
    return results if len(shapes) > 1 else results[0]


def per_device(
    histories,
    gain_time,
    wq_time,
    wkv_time,
    wo_time,
    gain_space,
    wq_space,
    wkv_space,
    wo_space,
    neighbours,
    nbr_valid,
    agent_valid,
):
    agents, steps, width = histories.shape[1:]
    tiles, rest = lax.axis_size("tile"), lax.axis_size("rest")
    spread = ("tile", "rest")
    parts = tiles * rest
    local = steps // parts
    rows = agents * steps
    blocked = local % 8 == 0
    struct = jax.ShapeDtypeStruct

    hist = histories.reshape(rows, width)
    kv_shape = (parts, agents * local, 2 * KEYS) if blocked else (rows, 2 * KEYS)
    mid, kv = call(
        functools.partial(time_kernel, agents, steps, local, blocked),
        [struct((rows, width), BF16), struct(kv_shape, BF16)],
        [hist, gain_time[None], gain_space[None], wq_time, wkv_time, wo_time, wkv_space],
        hbm=(0, 3, 4, 5, 6),
        hbm_out=(0,),
        scratch=[
            pltpu.VMEM((rows, width), BF16),
            pltpu.VMEM(wq_time.shape, BF16),
            pltpu.VMEM(wkv_time.shape, BF16),
            pltpu.VMEM(wo_time.shape, BF16),
            pltpu.VMEM(wkv_space.shape, BF16),
            pltpu.VMEM((rows, width), BF16),
            pltpu.VMEM((rows, width), BF16),
            pltpu.VMEM((rows, 2 * KEYS), BF16),
            pltpu.VMEM((rows, width), BF16),
            pltpu.VMEM((rows, width), BF16),
            pltpu.SemaphoreType.DMA((agents,)),
            pltpu.SemaphoreType.DMA((width // COLS,)),
            pltpu.SemaphoreType.DMA((3,)),
            pltpu.SemaphoreType.DMA,
        ],
        flops=2 * rows * width * (2 * width + 4 * KEYS),
        mib=56,
    )
    if not blocked:
        kv = to_blocks(kv, agents, steps, local)
    listed = jnp.sum(
        jnp.where(
            neighbours[0][:, None] == jnp.arange(tiles)[None, :], nbr_valid[0][:, None], 0
        ),
        axis=0,
    )
    group = rest * agents
    alive = jnp.where(lax.axis_index("half") == 0, agent_valid[0], jnp.roll(agent_valid[0], -group))
    meta = jnp.concatenate([alive, listed])
    meta = jnp.pad(meta, (0, LANES - meta.shape[0])).astype(F32)
    meta = jnp.broadcast_to(meta[None], (8, LANES))
    own = lax.all_to_all(kv, spread, split_axis=0, concat_axis=0, tiled=True)
    own = own.reshape(rows, 2 * KEYS)
    q_shape = (parts, agents * local, width + LANES) if blocked else (rows, width + LANES)
    q = call(
        functools.partial(query_kernel, agents, steps, local, blocked),
        [struct(q_shape, BF16)],
        [mid, gain_space[None], wq_space, meta],
        scratch=[pltpu.VMEM((rows, width), BF16)],
        flops=2 * rows * width * width,
    )
    if not blocked:
        q = to_blocks(q, agents, steps, local)
    swap = [(h, HALVES - 1 - h) for h in range(HALVES)]
    other = lax.ppermute(own, "half", swap)
    total = rows // local
    block = max(COLS, local) if rows % max(COLS, local) == 0 else rows
    q, own = lax.optimization_barrier((q, own))
    own = call(
        functools.partial(keys_kernel, local, block),
        [struct((local, total, 2 * KEYS), BF16)],
        [own],
        flops=SHADOW * rows * block * 2 * KEYS,
    )
    q = lax.all_to_all(q, spread, split_axis=0, concat_axis=0, tiled=True)

    pair = LANES // total if total < LANES and local % (LANES // total) == 0 else 1
    mix = call(
        functools.partial(space_kernel, local, block, tiles, pair),
        [struct((rows, width), BF16)],
        [q.reshape(rows, width + LANES), own, other],
        scratch=[
            pltpu.VMEM((local, total, width), BF16),
            pltpu.VMEM((local, total, 2 * KEYS), BF16),
            pltpu.VMEM((local, total, width), BF16),
        ],
        flops=8 * rows * total * width,
        mib=16 + 16 * GROUPS * HALVES * total**2 // MIB,
    )
    mix = lax.all_to_all(
        mix.reshape(parts, agents * local, width), spread, split_axis=0, concat_axis=0, tiled=True
    )
    if not blocked:
        mix = from_blocks(mix, agents, steps, local)
    out = call(
        functools.partial(out_kernel, agents, steps, local, blocked),
        [struct((rows, width), BF16)],
        [mix.reshape(rows, width), mid, wo_space],
        flops=2 * rows * width * width,
    )
    return out.reshape(1, agents, steps, width)


def solution(mesh):
    tiles, members = mesh.devices.shape
    split = Mesh(
        mesh.devices.reshape(tiles, HALVES, members // HALVES), ("tile", "half", "rest")
    )
    states = P("tile", ("half", "rest"), None, None)
    listing = P("tile", None)
    return jax.shard_map(
        per_device,
        mesh=split,
        in_specs=(states,) + (P(),) * 8 + (listing,) * 3,
        out_specs=states,
        check_vma=False,
    )
```

```python
import functools
import math

import jax
import jax.numpy as jnp
from jax import lax
from jax.experimental import pallas as pl
from jax.experimental.pallas import tpu as pltpu
from jax.sharding import Mesh
from jax.sharding import PartitionSpec as P

HEADS = 16
KV_HEADS = 4
HEAD_DIM = 64
GROUPS = HEADS // KV_HEADS
KEYS = KV_HEADS * HEAD_DIM
WIDE = GROUPS * HEAD_DIM
SCALE = HEAD_DIM ** (-0.5)
EXP2_SCALE = SCALE * math.log2(math.e)
NEG = -1e30
LANES = 128
COLS = 256
HALVES = 2
PLANES = 2
CORES = 2
DEPTH = 2
SHADOW = 10000
MIB = 1024 * 1024
F32 = jnp.float32
BF16 = jnp.bfloat16
ROWS_BY_COLS = (((1,), (1,)), ((), ()))


def norm_rows(values, gain):
    wide = values.astype(F32)
    meansq = jnp.mean(wide * wide, axis=-1, keepdims=True)
    return (wide * lax.rsqrt(meansq + 1e-05) * gain).astype(BF16)


def to_blocks(values, agents, steps, local):
    split = values.reshape(agents, steps // local, local, values.shape[-1])
    return jnp.transpose(split, (1, 0, 2, 3)).reshape(steps // local, agents * local, values.shape[-1])


def from_blocks(values, agents, steps, local):
    split = values.reshape(steps // local, agents, local, values.shape[-1])
    return jnp.transpose(split, (1, 0, 2, 3)).reshape(agents * steps, values.shape[-1])


def staggered(units, first, second, third):
    scores, grown = {}, {}
    for i in range(len(units) + 2 * DEPTH):
        if i < len(units):
            scores[i] = first(*units[i])
        if 0 <= i - DEPTH < len(units):
            grown[i - DEPTH] = second(scores.pop(i - DEPTH))
        if 0 <= i - 2 * DEPTH < len(units):
            third(units[i - 2 * DEPTH], *grown.pop(i - 2 * DEPTH))


def time_kernel(
    agents, steps, local, blocked,
    hist_hbm, gain_t, gain_s, wq_hbm, wkv_hbm, wo_hbm, wkv2_hbm,
    mid_hbm, kv_out,
    hist, wq, wkv, wo, wkv2, normed, query, keyval, mix, mid, hist_sems, wq_sems, sems, out_sem,
):
    rows, width = hist.shape
    hist_loads, wq_loads = [], []
    for a in range(agents):
        part = pl.ds(a * steps, steps)
        hist_loads.append(
            pltpu.make_async_copy(hist_hbm.at[part, :], hist.at[part, :], hist_sems.at[a])
        )
    for c in range(0, width, COLS):
        cols = pl.ds(c, COLS)
        wq_loads.append(
            pltpu.make_async_copy(wq_hbm.at[:, cols], wq.at[:, cols], wq_sems.at[c // COLS])
        )
    loads = [
        pltpu.make_async_copy(source, target, sems.at[i])
        for i, (source, target) in enumerate(((wkv_hbm, wkv), (wo_hbm, wo), (wkv2_hbm, wkv2)))
    ]
    for load in hist_loads + loads[:1]:
        load.start()
    for a in range(agents):
        part = pl.ds(a * steps, steps)
        hist_loads[a].wait()
        if a == 0:
            for load in wq_loads:
                load.start()
        normed[part, :] = norm_rows(hist[part, :], gain_t[...])
    loads[0].wait()
    for c in range(0, 2 * KEYS, COLS):
        keyval[:, c : c + COLS] = jnp.dot(
            normed[...], wkv[:, c : c + COLS], preferred_element_type=F32
        ).astype(BF16)
    for load in loads[1:]:
        load.start()
    for c in range(0, width, COLS):
        wq_loads[c // COLS].wait()
        query[:, c : c + COLS] = jnp.dot(
            normed[...], wq[:, c : c + COLS], preferred_element_type=F32
        ).astype(BF16)
    causal = lax.broadcasted_iota(jnp.int32, (steps, steps), 0) <= lax.broadcasted_iota(
        jnp.int32, (steps, steps), 1
    )
    causal = jnp.concatenate([causal] * GROUPS, axis=1)

    def scores_of(a, k):
        part = slice(a * steps, (a + 1) * steps)
        heads = query[part, k * WIDE : (k + 1) * WIDE].T
        heads = jnp.concatenate(
            [heads[j * HEAD_DIM : (j + 1) * HEAD_DIM] for j in range(GROUPS)], axis=1
        )
        keys = keyval[part, k * HEAD_DIM : (k + 1) * HEAD_DIM]
        return jnp.dot(keys, heads, preferred_element_type=F32)

    def grow(scores):
        scores = jnp.where(causal, scores, NEG)
        top = jnp.max(scores, axis=0, keepdims=True)
        grown = jnp.exp2((scores - top) * EXP2_SCALE)
        return grown.astype(BF16), jnp.sum(grown, axis=0, keepdims=True)

    def values_of(unit, grown, sums):
        a, k = unit
        part = slice(a * steps, (a + 1) * steps)
        vals = keyval[part, KEYS + k * HEAD_DIM : KEYS + (k + 1) * HEAD_DIM]
        mixed = jnp.dot(vals.T, grown, preferred_element_type=F32) * (1.0 / sums)
        mixed = jnp.concatenate(
            [mixed[:, j * steps : (j + 1) * steps] for j in range(GROUPS)], axis=0
        )
        mix[part, k * WIDE : (k + 1) * WIDE] = mixed.astype(BF16).T

    units = [(a, k) for a in range(agents) for k in range(KV_HEADS)]
    staggered(units, scores_of, grow, values_of)
    loads[1].wait()
    for c in range(0, width, COLS):
        cols = slice(c, c + COLS)
        projected = jnp.dot(mix[...], wo[:, cols], preferred_element_type=F32)
        mid[:, cols] = (hist[:, cols].astype(F32) + projected).astype(BF16)
    keep = pltpu.make_async_copy(mid, mid_hbm, out_sem)
    keep.start()
    for a in range(agents):
        part = pl.ds(a * steps, steps)
        normed[part, :] = norm_rows(mid[part, :], gain_s[...])
    loads[2].wait()
    for c in range(0, 2 * KEYS, COLS):
        cols = slice(c, c + COLS)
        result = jnp.dot(normed[...], wkv2[:, cols], preferred_element_type=F32)
        if blocked:
            kv_out[:, :, cols] = to_blocks(result, agents, steps, local).astype(BF16)
        else:
            kv_out[:, cols] = result.astype(BF16)
    keep.wait()


def query_kernel(agents, steps, local, blocked, cross, mid, gain, wq, meta, *rest):
    if cross:
        place, same, other, second = rest
        outs, swapped = (same, other), place[0] == 1
    else:
        out, second = rest
        outs = (out,)
    width = mid.shape[1]
    for a in range(agents):
        part = pl.ds(a * steps, steps)
        second[part, :] = norm_rows(mid[part, :], gain[...])
    for c in range(0, width, COLS):
        cols = slice(c, c + COLS)
        result = jnp.dot(second[...], wq[:, cols], preferred_element_type=F32)
        if cross:
            result = to_blocks(result, agents, steps, local).astype(BF16)
            result = result.reshape(-1, PLANES, CORES * result.shape[1], COLS)
            low, high = result[:, 0], result[:, 1]
            same[:, :, cols] = jnp.where(swapped, high, low).reshape(same.shape[:2] + (COLS,))
            other[:, :, cols] = jnp.where(swapped, low, high).reshape(same.shape[:2] + (COLS,))
        elif blocked:
            out[:, :, cols] = to_blocks(result, agents, steps, local).astype(BF16)
        else:
            out[:, cols] = result.astype(BF16)
    for out in outs:
        lines = jnp.broadcast_to(meta[0:1, :], (out.shape[-2], LANES)).astype(BF16)
        if blocked:
            out[:, :, width:] = jnp.broadcast_to(lines[None], out.shape[:2] + (LANES,))
        else:
            out[:, width:] = lines


def one_hot(shape, group, local, dtype=BF16):
    row = lax.broadcasted_iota(jnp.int32, shape, 0)
    col = lax.broadcasted_iota(jnp.int32, shape, 1)
    wanted = (row % group) * local + row // group
    return jnp.where(col == wanted, 1.0, 0.0).astype(dtype)


def key_weights(notes, local, tiles, total, stride):
    rows = notes.shape[0]
    group = total // tiles
    shape = (total, rows)
    row, col = (lax.broadcasted_iota(jnp.int32, shape, d) for d in range(2))
    pick = jnp.where(col == row * local, 1.0, 0.0).astype(BF16)
    lines = jnp.dot(pick, notes, preferred_element_type=F32).astype(BF16)
    shape = (LANES, HALVES * total)
    lane, key = (lax.broadcasted_iota(jnp.int32, shape, d) for d in range(2))
    half, tile, agent = key // total, key % total // group, key % group
    spread = jnp.where(lane == HALVES * group + tile, 1.0, 0.0).astype(BF16)
    listed = jnp.dot(lines, spread, preferred_element_type=F32)
    spread = jnp.where(lane == half * group + agent, 1.0, 0.0).astype(BF16)
    alive = jnp.dot(lines, spread, preferred_element_type=F32)
    shape = (total, HALVES * total)
    row, key = (lax.broadcasted_iota(jnp.int32, shape, d) for d in range(2))
    first = row == key % total // group * stride
    alive = jnp.sum(jnp.where(first, alive, 0.0), axis=0, keepdims=True)
    return listed * alive


def by_steps(source, target, local, block, rows, sources=1):
    width = target.shape[-1]
    group = block // local
    order = one_hot((block, block), group, local)
    for c in range(0, width, COLS):
        cols = slice(c, c + COLS)
        for b in range(rows // block):
            if sources > 1:
                share = source.shape[1] // sources
                piece = source[:, b * share : (b + 1) * share, cols].reshape(block, COLS)
            else:
                piece = source[b * block : (b + 1) * block, cols]
            if local > 1:
                piece = jnp.dot(order, piece, preferred_element_type=F32).astype(BF16)
            target[:, b * group : (b + 1) * group, cols] = piece.reshape(local, group, piece.shape[1])


def keys_kernel(local, block, source, out):
    by_steps(source, out, local, block, source.shape[0])


def space_kernel(
    local, block, tiles, pair, sources, q_in, own, other_in, *refs
):
    *place, out, query, other, mix = refs
    rows, width = other_in.shape[0], out.shape[-1]
    group = block // local
    total = rows // local
    columns = pair * total
    by_steps(q_in, query, local, block, rows, sources)
    by_steps(other_in, other, local, block, rows)
    if sources > 1:
        share = q_in.shape[1] // sources
        notes = [q_in[:, i * share : (i + 1) * share, width:] for i in range(sources)]
        notes = jnp.concatenate([part.reshape(block, LANES) for part in notes], axis=0)
    else:
        notes = q_in[:, width:]
    weight = key_weights(notes, local, tiles, total, total // sources // tiles)
    together = GROUPS if columns <= LANES else 1
    weight = jnp.concatenate([weight.T] * (pair * together), axis=1)
    valid = weight > 0
    lane = lax.broadcasted_iota(jnp.int32, (HEAD_DIM, columns), 1) // total

    def both(s, part):
        return jnp.concatenate([own[s, :, part], other[s, :, part]], axis=0)

    def scores_of(p, k, heads):
        turned = query[p * pair : (p + 1) * pair, :, k * WIDE : (k + 1) * WIDE]
        turned = turned.reshape(columns, WIDE).T
        turned = [turned[j * HEAD_DIM : (j + 1) * HEAD_DIM] for j in heads]
        if pair > 1:
            zero = jnp.zeros((HEAD_DIM, columns), BF16)
            turned = [
                jnp.concatenate([jnp.where(lane == s, t, zero) for s in range(pair)], axis=0)
                for t in turned
            ]
        part = slice(k * HEAD_DIM, (k + 1) * HEAD_DIM)
        keys = jnp.concatenate([both(p * pair + s, part) for s in range(pair)], axis=1)
        return jnp.dot(keys, jnp.concatenate(turned, axis=1), preferred_element_type=F32)

    def grow(scores):
        scores = jnp.where(valid, scores, NEG)
        top = jnp.max(scores, axis=0, keepdims=True)
        grown = jnp.exp2((scores - top) * EXP2_SCALE) * weight
        return grown.astype(BF16), jnp.sum(grown, axis=0, keepdims=True)

    def values_of(unit, grown, sums):
        p, k, heads = unit
        part = slice(KEYS + k * HEAD_DIM, KEYS + (k + 1) * HEAD_DIM)
        vals = jnp.concatenate([both(p * pair + s, part).T for s in range(pair)], axis=0)
        mixed = jnp.dot(vals, grown, preferred_element_type=F32)
        inverse = 1.0 / sums
        parts = []
        for i in range(len(heads)):
            cols = slice(i * columns, (i + 1) * columns)
            chosen = mixed[:HEAD_DIM, cols]
            for s in range(1, pair):
                chosen = jnp.where(lane == s, mixed[s * HEAD_DIM : (s + 1) * HEAD_DIM, cols], chosen)
            parts.append(chosen * inverse[:, cols])
        mixed = jnp.concatenate(parts, axis=0).astype(BF16).T
        start = k * WIDE + heads[0] * HEAD_DIM
        mix[p * pair : (p + 1) * pair, :, start : start + len(heads) * HEAD_DIM] = mixed.reshape(
            pair, total, len(heads) * HEAD_DIM
        )

    units = [
        (p, k, tuple(range(j, j + together)))
        for p in range(local // pair)
        for k in range(KV_HEADS)
        for j in range(0, GROUPS, together)
    ]
    staggered(units, scores_of, grow, values_of)
    order = one_hot((block, block), group, local)
    for b in range(rows // block):
        for c in range(0, width, COLS):
            cols = slice(c, c + COLS)
            piece = mix[:, b * group : (b + 1) * group, cols].reshape(block, COLS)
            if local > 1:
                piece = lax.dot_general(
                    order, piece, (((0,), (0,)), ((), ())), preferred_element_type=F32
                ).astype(BF16)
            if sources > 1:
                plane = (place[0][0] + b) % PLANES
                out[:, plane, :, cols] = piece.reshape(out.shape[0], out.shape[2], COLS)
            else:
                out[b * block : (b + 1) * block, cols] = piece


def out_kernel(agents, steps, local, blocked, mix, mid, wo, out):
    width = mid.shape[1]
    for c in range(0, width, COLS):
        cols = slice(c, c + COLS)
        projected = jnp.dot(mix[...], wo[:, cols], preferred_element_type=F32)
        if blocked:
            projected = from_blocks(projected, agents, steps, local)
        out[:, cols] = (mid[:, cols].astype(F32) + projected).astype(BF16)


def call(kernel, shapes, args, hbm=(), hbm_out=(), smem=(), scratch=(), flops=0, mib=16):
    moved = sum(a.size * a.dtype.itemsize for a in args)
    moved += sum(s.size * s.dtype.itemsize for s in shapes)

    def specs(count, far, scalars=()):
        spaces = [pl.ANY if i in far else pltpu.VMEM for i in range(count)]
        return [
            pl.BlockSpec(memory_space=pltpu.SMEM if i in scalars else space)
            for i, space in enumerate(spaces)
        ]

    results = pl.pallas_call(
        kernel,
        out_shape=list(shapes),
        in_specs=specs(len(args), hbm, smem),
        out_specs=specs(len(shapes), hbm_out),
        scratch_shapes=list(scratch),
        compiler_params=pltpu.CompilerParams(vmem_limit_bytes=mib * MIB),
        cost_estimate=pl.CostEstimate(flops=flops, bytes_accessed=moved, transcendentals=0),
    )(*args)
    return results if len(shapes) > 1 else results[0]


def per_device(
    histories,
    gain_time,
    wq_time,
    wkv_time,
    wo_time,
    gain_space,
    wq_space,
    wkv_space,
    wo_space,
    neighbours,
    nbr_valid,
    agent_valid,
):
    agents, steps, width = histories.shape[1:]
    tiles, planes, cores = (lax.axis_size(name) for name in ("tile", "plane", "core"))
    rest = planes * cores
    spread = ("tile", "plane", "core")
    parts = tiles * rest
    local = steps // parts
    rows = agents * steps
    blocked = local % 8 == 0
    cross = blocked and planes == PLANES and cores == CORES and rows == 2 * COLS
    struct = jax.ShapeDtypeStruct

    hist = histories.reshape(rows, width)
    kv_shape = (parts, agents * local, 2 * KEYS) if blocked else (rows, 2 * KEYS)
    mid, kv = call(
        functools.partial(time_kernel, agents, steps, local, blocked),
        [struct((rows, width), BF16), struct(kv_shape, BF16)],
        [hist, gain_time[None], gain_space[None], wq_time, wkv_time, wo_time, wkv_space],
        hbm=(0, 3, 4, 5, 6),
        hbm_out=(0,),
        scratch=[
            pltpu.VMEM((rows, width), BF16),
            pltpu.VMEM(wq_time.shape, BF16),
            pltpu.VMEM(wkv_time.shape, BF16),
            pltpu.VMEM(wo_time.shape, BF16),
            pltpu.VMEM(wkv_space.shape, BF16),
            pltpu.VMEM((rows, width), BF16),
            pltpu.VMEM((rows, width), BF16),
            pltpu.VMEM((rows, 2 * KEYS), BF16),
            pltpu.VMEM((rows, width), BF16),
            pltpu.VMEM((rows, width), BF16),
            pltpu.SemaphoreType.DMA((agents,)),
            pltpu.SemaphoreType.DMA((width // COLS,)),
            pltpu.SemaphoreType.DMA((3,)),
            pltpu.SemaphoreType.DMA,
        ],
        flops=2 * rows * width * (2 * width + 4 * KEYS),
        mib=56,
    )
    if not blocked:
        kv = to_blocks(kv, agents, steps, local)
    listed = jnp.sum(
        jnp.where(
            neighbours[0][:, None] == jnp.arange(tiles)[None, :], nbr_valid[0][:, None], 0
        ),
        axis=0,
    )
    group = rest * agents
    alive = jnp.where(lax.axis_index("half") == 0, agent_valid[0], jnp.roll(agent_valid[0], -group))
    meta = jnp.concatenate([alive, listed])
    meta = jnp.pad(meta, (0, LANES - meta.shape[0])).astype(F32)
    meta = jnp.broadcast_to(meta[None], (8, LANES))
    own = lax.all_to_all(kv, spread, split_axis=0, concat_axis=0, tiled=True)
    own = own.reshape(rows, 2 * KEYS)
    place = lax.axis_index("plane").astype(jnp.int32).reshape(1)
    deep = width + LANES
    if cross:
        q_shapes = [(tiles * cores, agents * local, deep)] * 2
    else:
        q_shapes = [(parts, agents * local, deep) if blocked else (rows, deep)]
    q = call(
        functools.partial(query_kernel, agents, steps, local, blocked, cross),
        [struct(shape, BF16) for shape in q_shapes],
        [mid, gain_space[None], wq_space, meta] + ([place] if cross else []),
        smem=(4,),
        scratch=[pltpu.VMEM((rows, width), BF16)],
        flops=2 * rows * width * width,
    )
    if cross:
        turn = [(p, PLANES - 1 - p) for p in range(PLANES)]
        q = [q[0], lax.ppermute(q[1], "plane", turn)]
    else:
        q = [q if blocked else to_blocks(q, agents, steps, local)]
    swap = [(h, HALVES - 1 - h) for h in range(HALVES)]
    other = lax.ppermute(own, "half", swap)
    total = rows // local
    block = max(COLS, local) if rows % max(COLS, local) == 0 else rows
    *q, own = lax.optimization_barrier((*q, own))
    own = call(
        functools.partial(keys_kernel, local, block),
        [struct((local, total, 2 * KEYS), BF16)],
        [own],
        flops=SHADOW * rows * block * 2 * KEYS,
    )
    if cross:
        q = [jnp.concatenate(q, axis=1)]
    within = ("tile", "core") if cross else spread
    q = lax.all_to_all(q[0], within, split_axis=0, concat_axis=0, tiled=True)

    pair = LANES // total if total < LANES and local % (LANES // total) == 0 else 1
    mix = call(
        functools.partial(space_kernel, local, block, tiles, pair, PLANES if cross else 1),
        [struct((tiles, PLANES, rows // (tiles * PLANES), width) if cross else (rows, width), BF16)],
        [q if cross else q.reshape(rows, deep), own, other] + ([place] if cross else []),
        smem=(3,) if cross else (),
        scratch=[
            pltpu.VMEM((local, total, width), BF16),
            pltpu.VMEM((local, total, 2 * KEYS), BF16),
            pltpu.VMEM((local, total, width), BF16),
        ],
        flops=8 * rows * total * width,
        mib=16 + 16 * GROUPS * HALVES * total**2 // MIB,
    )
    mix = lax.all_to_all(
        mix.reshape(parts, agents * local, width), spread, split_axis=0, concat_axis=0, tiled=True
    )
    if not blocked:
        mix = from_blocks(mix, agents, steps, local)
    out = call(
        functools.partial(out_kernel, agents, steps, local, blocked),
        [struct((rows, width), BF16)],
        [mix.reshape(rows, width), mid, wo_space],
        flops=2 * rows * width * width,
    )
    return out.reshape(1, agents, steps, width)


def solution(mesh):
    tiles, members = mesh.devices.shape
    cores = CORES if members % (HALVES * CORES) == 0 else 1
    shape = (tiles, HALVES, members // HALVES // cores, cores)
    split = Mesh(mesh.devices.reshape(shape), ("tile", "half", "plane", "core"))
    states = P("tile", ("half", "plane", "core"), None, None)
    listing = P("tile", None)
    return jax.shard_map(
        per_device,
        mesh=split,
        in_specs=(states,) + (P(),) * 8 + (listing,) * 3,
        out_specs=states,
        check_vma=False,
    )
```

```python
import functools
import math

import jax
import jax.numpy as jnp
from jax import lax
from jax.experimental import pallas as pl
from jax.experimental.pallas import tpu as pltpu
from jax.sharding import Mesh
from jax.sharding import PartitionSpec as P

HEADS = 16
KV_HEADS = 4
HEAD_DIM = 64
GROUPS = HEADS // KV_HEADS
KEYS = KV_HEADS * HEAD_DIM
WIDE = GROUPS * HEAD_DIM
SCALE = HEAD_DIM ** (-0.5)
EXP2_SCALE = SCALE * math.log2(math.e)
NEG = -1e30
LANES = 128
COLS = 256
HALVES = 2
DEPTH = 2
SHADOW = 400
MIB = 1024 * 1024
F32 = jnp.float32
BF16 = jnp.bfloat16
ROWS_BY_COLS = (((1,), (1,)), ((), ()))


def norm_rows(values, gain):
    wide = values.astype(F32)
    meansq = jnp.mean(wide * wide, axis=-1, keepdims=True)
    return (wide * lax.rsqrt(meansq + 1e-05) * gain).astype(BF16)


def to_blocks(values, agents, steps, local):
    split = values.reshape(agents, steps // local, local, values.shape[-1])
    return jnp.transpose(split, (1, 0, 2, 3)).reshape(steps // local, agents * local, values.shape[-1])


def from_blocks(values, agents, steps, local):
    split = values.reshape(steps // local, agents, local, values.shape[-1])
    return jnp.transpose(split, (1, 0, 2, 3)).reshape(agents * steps, values.shape[-1])


def staggered(units, first, second, third):
    scores, grown = {}, {}
    for i in range(len(units) + 2 * DEPTH):
        if i < len(units):
            scores[i] = first(*units[i])
        if 0 <= i - DEPTH < len(units):
            grown[i - DEPTH] = second(scores.pop(i - DEPTH))
        if 0 <= i - 2 * DEPTH < len(units):
            third(units[i - 2 * DEPTH], *grown.pop(i - 2 * DEPTH))


def time_kernel(
    agents, steps, local, blocked,
    hist_hbm, gain_t, gain_s, wq_hbm, wkv_hbm, wo_hbm, wkv2_hbm, neighbours, nbr_valid, alive,
    mid_hbm, kv_out,
    hist, wq, wkv, wo, wkv2, normed, query, keyval, mix, mid, hist_sems, wq_sems, sems, out_sem,
):
    rows, width = hist.shape
    hist_loads, wq_loads = [], []
    for a in range(agents):
        part = pl.ds(a * steps, steps)
        hist_loads.append(
            pltpu.make_async_copy(hist_hbm.at[part, :], hist.at[part, :], hist_sems.at[a])
        )
    for c in range(0, width, COLS):
        cols = pl.ds(c, COLS)
        wq_loads.append(
            pltpu.make_async_copy(wq_hbm.at[:, cols], wq.at[:, cols], wq_sems.at[c // COLS])
        )
    loads = [
        pltpu.make_async_copy(source, target, sems.at[i])
        for i, (source, target) in enumerate(((wkv_hbm, wkv), (wo_hbm, wo), (wkv2_hbm, wkv2)))
    ]
    for load in hist_loads + loads[:1]:
        load.start()
    for a in range(agents):
        part = pl.ds(a * steps, steps)
        hist_loads[a].wait()
        if a == 0:
            for load in wq_loads:
                load.start()
        normed[part, :] = norm_rows(hist[part, :], gain_t[...])
    loads[0].wait()
    for c in range(0, 2 * KEYS, COLS):
        keyval[:, c : c + COLS] = jnp.dot(
            normed[...], wkv[:, c : c + COLS], preferred_element_type=F32
        ).astype(BF16)
    for load in loads[1:]:
        load.start()
    for c in range(0, width, COLS):
        wq_loads[c // COLS].wait()
        query[:, c : c + COLS] = jnp.dot(
            normed[...], wq[:, c : c + COLS], preferred_element_type=F32
        ).astype(BF16)
    causal = lax.broadcasted_iota(jnp.int32, (steps, steps), 0) <= lax.broadcasted_iota(
        jnp.int32, (steps, steps), 1
    )
    causal = jnp.concatenate([causal] * GROUPS, axis=1)

    def scores_of(a, k):
        part = slice(a * steps, (a + 1) * steps)
        heads = query[part, k * WIDE : (k + 1) * WIDE].T
        heads = jnp.concatenate(
            [heads[j * HEAD_DIM : (j + 1) * HEAD_DIM] for j in range(GROUPS)], axis=1
        )
        keys = keyval[part, k * HEAD_DIM : (k + 1) * HEAD_DIM]
        return jnp.dot(keys, heads, preferred_element_type=F32)

    def grow(scores):
        scores = jnp.where(causal, scores, NEG)
        top = jnp.max(scores, axis=0, keepdims=True)
        grown = jnp.exp2((scores - top) * EXP2_SCALE)
        return grown.astype(BF16), jnp.sum(grown, axis=0, keepdims=True)

    def values_of(unit, grown, sums):
        a, k = unit
        part = slice(a * steps, (a + 1) * steps)
        vals = keyval[part, KEYS + k * HEAD_DIM : KEYS + (k + 1) * HEAD_DIM]
        mixed = jnp.dot(vals.T, grown, preferred_element_type=F32) * (1.0 / sums)
        mixed = jnp.concatenate(
            [mixed[:, j * steps : (j + 1) * steps] for j in range(GROUPS)], axis=0
        )
        mix[part, k * WIDE : (k + 1) * WIDE] = mixed.astype(BF16).T

    units = [(a, k) for a in range(agents) for k in range(KV_HEADS)]
    staggered(units, scores_of, grow, values_of)
    loads[1].wait()
    for c in range(0, width, COLS):
        cols = slice(c, c + COLS)
        projected = jnp.dot(mix[...], wo[:, cols], preferred_element_type=F32)
        mid[:, cols] = (hist[:, cols].astype(F32) + projected).astype(BF16)
    keep = pltpu.make_async_copy(mid, mid_hbm, out_sem)
    keep.start()
    for a in range(agents):
        part = pl.ds(a * steps, steps)
        normed[part, :] = norm_rows(mid[part, :], gain_s[...])
    loads[2].wait()
    for c in range(0, 2 * KEYS, COLS):
        cols = slice(c, c + COLS)
        result = jnp.dot(normed[...], wkv2[:, cols], preferred_element_type=F32)
        if blocked:
            kv_out[:, :, cols] = to_blocks(result, agents, steps, local).astype(BF16)
        else:
            kv_out[:, cols] = result.astype(BF16)
    lane = lax.broadcasted_iota(jnp.int32, (1, LANES), 1)
    notes = jnp.zeros((1, LANES), F32)
    for i in range(alive.shape[1]):
        notes = jnp.where(lane == i, alive[0, i].astype(F32), notes)
    for i in range(neighbours.shape[1]):
        listed = lane == alive.shape[1] + neighbours[0, i]
        notes = notes + jnp.where(listed, nbr_valid[0, i].astype(F32), 0.0)
    notes = jnp.broadcast_to(notes, (kv_out.shape[-2], LANES)).astype(BF16)
    kv_out[..., 2 * KEYS :] = jnp.broadcast_to(notes, kv_out.shape[:-1] + (LANES,))
    keep.wait()


def query_kernel(agents, steps, local, blocked, mid, gain, wq, out, second):
    width = mid.shape[1]
    for a in range(agents):
        part = pl.ds(a * steps, steps)
        second[part, :] = norm_rows(mid[part, :], gain[...])
    for c in range(0, width, COLS):
        cols = slice(c, c + COLS)
        result = jnp.dot(second[...], wq[:, cols], preferred_element_type=F32)
        if blocked:
            out[:, :, cols] = to_blocks(result, agents, steps, local).astype(BF16)
        else:
            out[:, cols] = result.astype(BF16)


def one_hot(shape, group, local, dtype=BF16):
    row = lax.broadcasted_iota(jnp.int32, shape, 0)
    col = lax.broadcasted_iota(jnp.int32, shape, 1)
    wanted = (row % group) * local + row // group
    return jnp.where(col == wanted, 1.0, 0.0).astype(dtype)


def weight_kernel(local, tiles, half, kv_in, out):
    rows = kv_in.shape[0]
    total = rows // local
    group = total // tiles
    notes = kv_in[:, 2 * KEYS :]
    shape = (total, rows)
    row, col = (lax.broadcasted_iota(jnp.int32, shape, d) for d in range(2))
    pick = jnp.where(col == row * local, 1.0, 0.0).astype(BF16)
    lines = jnp.dot(pick, notes, preferred_element_type=F32).astype(BF16)
    shape = (HALVES * total, LANES)
    key, lane = (lax.broadcasted_iota(jnp.int32, shape, d) for d in range(2))
    side, tile, agent = (key // total + half[0]) % HALVES, key % total // group, key % group
    spread = jnp.where(lane == HALVES * group + tile, 1.0, 0.0).astype(BF16)
    listed = lax.dot_general(spread, lines, ROWS_BY_COLS, preferred_element_type=F32)
    spread = jnp.where(lane == side * group + agent, 1.0, 0.0).astype(BF16)
    alive = lax.dot_general(spread, lines, ROWS_BY_COLS, preferred_element_type=F32)
    shape = (HALVES * total, total)
    key, query = (lax.broadcasted_iota(jnp.int32, shape, d) for d in range(2))
    first = query == key % total // group * group
    alive = jnp.sum(jnp.where(first, alive, 0.0), axis=1, keepdims=True)
    out[...] = listed * alive


def by_steps(source, target, local, block):
    rows, width = source.shape[0], target.shape[-1]
    group = block // local
    order = one_hot((block, block), group, local)
    for c in range(0, width, COLS):
        cols = slice(c, c + COLS)
        for b in range(rows // block):
            piece = source[b * block : (b + 1) * block, cols]
            if local > 1:
                piece = jnp.dot(order, piece, preferred_element_type=F32).astype(BF16)
            target[:, b * group : (b + 1) * group, cols] = piece.reshape(local, group, piece.shape[1])


def keys_kernel(local, block, source, out):
    by_steps(source, out, local, block)


def space_kernel(
    local, block, pair, q_in, own, other, weights, out, query, mix
):
    rows, width = out.shape
    group = block // local
    total = rows // local
    columns = pair * total
    by_steps(q_in, query, local, block)
    together = GROUPS if columns <= LANES else 1
    weight = jnp.concatenate([weights[...]] * (pair * together), axis=1)
    valid = weight > 0
    lane = lax.broadcasted_iota(jnp.int32, (HEAD_DIM, columns), 1) // total

    def both(s, part):
        return jnp.concatenate([own[s, :, part], other[s, :, part]], axis=0)

    def scores_of(p, k, heads):
        turned = query[p * pair : (p + 1) * pair, :, k * WIDE : (k + 1) * WIDE]
        turned = turned.reshape(columns, WIDE).T
        turned = [turned[j * HEAD_DIM : (j + 1) * HEAD_DIM] for j in heads]
        if pair > 1:
            zero = jnp.zeros((HEAD_DIM, columns), BF16)
            turned = [
                jnp.concatenate([jnp.where(lane == s, t, zero) for s in range(pair)], axis=0)
                for t in turned
            ]
        part = slice(k * HEAD_DIM, (k + 1) * HEAD_DIM)
        keys = jnp.concatenate([both(p * pair + s, part) for s in range(pair)], axis=1)
        return jnp.dot(keys, jnp.concatenate(turned, axis=1), preferred_element_type=F32)

    def grow(scores):
        scores = jnp.where(valid, scores, NEG)
        top = jnp.max(scores, axis=0, keepdims=True)
        grown = jnp.exp2((scores - top) * EXP2_SCALE) * weight
        return grown.astype(BF16), jnp.sum(grown, axis=0, keepdims=True)

    def values_of(unit, grown, sums):
        p, k, heads = unit
        part = slice(KEYS + k * HEAD_DIM, KEYS + (k + 1) * HEAD_DIM)
        vals = jnp.concatenate([both(p * pair + s, part).T for s in range(pair)], axis=0)
        mixed = jnp.dot(vals, grown, preferred_element_type=F32)
        inverse = 1.0 / sums
        parts = []
        for i in range(len(heads)):
            cols = slice(i * columns, (i + 1) * columns)
            chosen = mixed[:HEAD_DIM, cols]
            for s in range(1, pair):
                chosen = jnp.where(lane == s, mixed[s * HEAD_DIM : (s + 1) * HEAD_DIM, cols], chosen)
            parts.append(chosen * inverse[:, cols])
        mixed = jnp.concatenate(parts, axis=0).astype(BF16).T
        start = k * WIDE + heads[0] * HEAD_DIM
        mix[p * pair : (p + 1) * pair, :, start : start + len(heads) * HEAD_DIM] = mixed.reshape(
            pair, total, len(heads) * HEAD_DIM
        )

    units = [
        (p, k, tuple(range(j, j + together)))
        for p in range(local // pair)
        for k in range(KV_HEADS)
        for j in range(0, GROUPS, together)
    ]
    staggered(units, scores_of, grow, values_of)
    order = one_hot((block, block), group, local)
    for b in range(rows // block):
        for c in range(0, width, COLS):
            cols = slice(c, c + COLS)
            piece = mix[:, b * group : (b + 1) * group, cols].reshape(block, COLS)
            if local > 1:
                piece = lax.dot_general(
                    order, piece, (((0,), (0,)), ((), ())), preferred_element_type=F32
                ).astype(BF16)
            out[b * block : (b + 1) * block, cols] = piece


def out_kernel(agents, steps, local, blocked, mix, mid, wo, out):
    width = mid.shape[1]
    for c in range(0, width, COLS):
        cols = slice(c, c + COLS)
        projected = jnp.dot(mix[...], wo[:, cols], preferred_element_type=F32)
        if blocked:
            projected = from_blocks(projected, agents, steps, local)
        out[:, cols] = (mid[:, cols].astype(F32) + projected).astype(BF16)


def call(kernel, shapes, args, hbm=(), hbm_out=(), smem=(), scratch=(), flops=0, mib=16):
    moved = sum(a.size * a.dtype.itemsize for a in args)
    moved += sum(s.size * s.dtype.itemsize for s in shapes)

    def specs(count, far, scalars=()):
        spaces = [pl.ANY if i in far else pltpu.VMEM for i in range(count)]
        return [
            pl.BlockSpec(memory_space=pltpu.SMEM if i in scalars else space)
            for i, space in enumerate(spaces)
        ]

    results = pl.pallas_call(
        kernel,
        out_shape=list(shapes),
        in_specs=specs(len(args), hbm, smem),
        out_specs=specs(len(shapes), hbm_out),
        scratch_shapes=list(scratch),
        compiler_params=pltpu.CompilerParams(vmem_limit_bytes=mib * MIB),
        cost_estimate=pl.CostEstimate(flops=flops, bytes_accessed=moved, transcendentals=0),
    )(*args)
    return results if len(shapes) > 1 else results[0]


def per_device(
    histories,
    gain_time,
    wq_time,
    wkv_time,
    wo_time,
    gain_space,
    wq_space,
    wkv_space,
    wo_space,
    neighbours,
    nbr_valid,
    agent_valid,
):
    agents, steps, width = histories.shape[1:]
    tiles, rest = lax.axis_size("tile"), lax.axis_size("rest")
    spread = ("tile", "rest")
    parts = tiles * rest
    local = steps // parts
    rows = agents * steps
    blocked = local % 8 == 0
    struct = jax.ShapeDtypeStruct

    hist = histories.reshape(rows, width)
    deep = 2 * KEYS + LANES
    kv_shape = (parts, agents * local, deep) if blocked else (rows, deep)
    mid, kv = call(
        functools.partial(time_kernel, agents, steps, local, blocked),
        [struct((rows, width), BF16), struct(kv_shape, BF16)],
        [hist, gain_time[None], gain_space[None], wq_time, wkv_time, wo_time, wkv_space]
        + [neighbours, nbr_valid, agent_valid],
        hbm=(0, 3, 4, 5, 6),
        smem=(7, 8, 9),
        hbm_out=(0,),
        scratch=[
            pltpu.VMEM((rows, width), BF16),
            pltpu.VMEM(wq_time.shape, BF16),
            pltpu.VMEM(wkv_time.shape, BF16),
            pltpu.VMEM(wo_time.shape, BF16),
            pltpu.VMEM(wkv_space.shape, BF16),
            pltpu.VMEM((rows, width), BF16),
            pltpu.VMEM((rows, width), BF16),
            pltpu.VMEM((rows, 2 * KEYS), BF16),
            pltpu.VMEM((rows, width), BF16),
            pltpu.VMEM((rows, width), BF16),
            pltpu.SemaphoreType.DMA((agents,)),
            pltpu.SemaphoreType.DMA((width // COLS,)),
            pltpu.SemaphoreType.DMA((3,)),
            pltpu.SemaphoreType.DMA,
        ],
        flops=2 * rows * width * (2 * width + 4 * KEYS),
        mib=56,
    )
    if not blocked:
        kv = to_blocks(kv, agents, steps, local)
    kv = lax.all_to_all(kv, spread, split_axis=0, concat_axis=0, tiled=True)
    kv = kv.reshape(rows, deep)
    q_shape = (parts, agents * local, width) if blocked else (rows, width)
    q = call(
        functools.partial(query_kernel, agents, steps, local, blocked),
        [struct(q_shape, BF16)],
        [mid, gain_space[None], wq_space],
        scratch=[pltpu.VMEM((rows, width), BF16)],
        flops=2 * rows * width * width,
    )
    if not blocked:
        q = to_blocks(q, agents, steps, local)
    total = rows // local
    block = max(COLS, local) if rows % max(COLS, local) == 0 else rows
    own = call(
        functools.partial(keys_kernel, local, block),
        [struct((local, total, 2 * KEYS), BF16)],
        [kv],
        flops=2 * rows * block * 2 * KEYS,
    )
    swap = [(h, HALVES - 1 - h) for h in range(HALVES)]
    other = lax.ppermute(own, "half", swap)
    q, own, kv = lax.optimization_barrier((q, own, kv))
    half = lax.axis_index("half").astype(jnp.int32).reshape(1)
    weight = call(
        functools.partial(weight_kernel, local, tiles),
        [struct((HALVES * total, total), F32)],
        [half, kv],
        smem=(0,),
        flops=SHADOW * rows * block * 2 * KEYS,
    )
    q = lax.all_to_all(q, spread, split_axis=0, concat_axis=0, tiled=True)

    pair = LANES // total if total < LANES and local % (LANES // total) == 0 else 1
    mix = call(
        functools.partial(space_kernel, local, block, pair),
        [struct((rows, width), BF16)],
        [q.reshape(rows, width), own, other, weight],
        scratch=[
            pltpu.VMEM((local, total, width), BF16),
            pltpu.VMEM((local, total, width), BF16),
        ],
        flops=8 * rows * total * width,
        mib=16 + 16 * GROUPS * HALVES * total**2 // MIB,
    )
    mix = lax.all_to_all(
        mix.reshape(parts, agents * local, width), spread, split_axis=0, concat_axis=0, tiled=True
    )
    if not blocked:
        mix = from_blocks(mix, agents, steps, local)
    out = call(
        functools.partial(out_kernel, agents, steps, local, blocked),
        [struct((rows, width), BF16)],
        [mix.reshape(rows, width), mid, wo_space],
        flops=2 * rows * width * width,
    )
    return out.reshape(1, agents, steps, width)


def solution(mesh):
    tiles, members = mesh.devices.shape
    split = Mesh(
        mesh.devices.reshape(tiles, HALVES, members // HALVES), ("tile", "half", "rest")
    )
    states = P("tile", ("half", "rest"), None, None)
    listing = P("tile", None)
    return jax.shard_map(
        per_device,
        mesh=split,
        in_specs=(states,) + (P(),) * 8 + (listing,) * 3,
        out_specs=states,
        check_vma=False,
    )
```

```python
import functools
import math

import jax
import jax.numpy as jnp
from jax import lax
from jax.experimental import pallas as pl
from jax.experimental.pallas import tpu as pltpu
from jax.sharding import Mesh
from jax.sharding import PartitionSpec as P

HEADS = 16
KV_HEADS = 4
HEAD_DIM = 64
GROUPS = HEADS // KV_HEADS
KEYS = KV_HEADS * HEAD_DIM
WIDE = GROUPS * HEAD_DIM
SCALE = HEAD_DIM ** (-0.5)
EXP2_SCALE = SCALE * math.log2(math.e)
NEG = -1e30
LANES = 128
COLS = 256
HALVES = 2
CHUNKS = 2
DEPTH = 2
MIB = 1024 * 1024
F32 = jnp.float32
BF16 = jnp.bfloat16
ROWS_BY_COLS = (((1,), (1,)), ((), ()))


def norm_rows(values, gain):
    wide = values.astype(F32)
    meansq = jnp.mean(wide * wide, axis=-1, keepdims=True)
    return (wide * lax.rsqrt(meansq + 1e-05) * gain).astype(BF16)


def one_hot(rows, source, turned=False):
    row = lax.broadcasted_iota(jnp.int32, (rows, rows), 1 if turned else 0)
    col = lax.broadcasted_iota(jnp.int32, (rows, rows), 0 if turned else 1)
    return jnp.where(col == source(row), 1.0, 0.0).astype(BF16)


def block_source(agents, span, local):
    return lambda row: row // local % agents * span + row // (local * agents) * local + row % local


def step_source(total, local):
    return lambda row: row % total * local + row // total


def moved(order, piece):
    return jnp.dot(order, piece, preferred_element_type=F32).astype(BF16)


def staggered(units, first, second, third):
    scores, grown = {}, {}
    for i in range(len(units) + 2 * DEPTH):
        if i < len(units):
            scores[i] = first(*units[i])
        if 0 <= i - DEPTH < len(units):
            grown[i - DEPTH] = second(scores.pop(i - DEPTH))
        if 0 <= i - 2 * DEPTH < len(units):
            third(units[i - 2 * DEPTH], *grown.pop(i - 2 * DEPTH))


def attend(members, pair, size, query, keyval, store, valid, weight=None):
    columns = pair * size
    together = GROUPS if columns <= LANES else 1
    valid = jnp.concatenate([valid] * together, axis=1)
    if weight is not None:
        weight = jnp.concatenate([weight] * together, axis=1)
    lane = lax.broadcasted_iota(jnp.int32, (HEAD_DIM, columns), 1) // size

    def scores_of(m, k, heads):
        turned = [query(m + s, slice(k * WIDE, (k + 1) * WIDE)) for s in range(pair)]
        turned = jnp.concatenate(turned, axis=0).T
        turned = [turned[j * HEAD_DIM : (j + 1) * HEAD_DIM] for j in heads]
        if pair > 1:
            zero = jnp.zeros((HEAD_DIM, columns), BF16)
            turned = [
                jnp.concatenate([jnp.where(lane == s, t, zero) for s in range(pair)], axis=0)
                for t in turned
            ]
        part = slice(k * HEAD_DIM, (k + 1) * HEAD_DIM)
        keys = jnp.concatenate([keyval(m + s, part) for s in range(pair)], axis=1)
        return jnp.dot(keys, jnp.concatenate(turned, axis=1), preferred_element_type=F32)

    def grow(scores):
        scores = jnp.where(valid, scores, NEG)
        top = jnp.max(scores, axis=0, keepdims=True)
        grown = jnp.exp2((scores - top) * EXP2_SCALE)
        if weight is not None:
            grown = grown * weight
        return grown.astype(BF16), jnp.sum(grown, axis=0, keepdims=True)

    def values_of(unit, grown, sums):
        m, k, heads = unit
        part = slice(KEYS + k * HEAD_DIM, KEYS + (k + 1) * HEAD_DIM)
        vals = jnp.concatenate([keyval(m + s, part).T for s in range(pair)], axis=0)
        mixed = jnp.dot(vals, grown, preferred_element_type=F32)
        inverse = 1.0 / sums
        parts = []
        for i in range(len(heads)):
            cols = slice(i * columns, (i + 1) * columns)
            chosen = mixed[:HEAD_DIM, cols]
            for s in range(1, pair):
                chosen = jnp.where(lane == s, mixed[s * HEAD_DIM : (s + 1) * HEAD_DIM, cols], chosen)
            parts.append(chosen * inverse[:, cols])
        mixed = jnp.concatenate(parts, axis=0).astype(BF16).T
        start = k * WIDE + heads[0] * HEAD_DIM
        store(m, slice(start, start + len(heads) * HEAD_DIM), mixed)

    units = [
        (m, k, tuple(range(j, j + together)))
        for m in range(0, members, pair)
        for k in range(KV_HEADS)
        for j in range(0, GROUPS, together)
    ]
    staggered(units, scores_of, grow, values_of)


def time_kernel(agents, steps, span, chunk, local, pair, *refs):
    hist_hbm, gain, wq_hbm, wkv_hbm, wo_hbm, *refs = refs
    before, refs = refs[:chunk], refs[chunk:]
    listing, refs = (refs[:3], refs[3:]) if chunk == 0 else ((), refs)
    mid, sent, keyval, *refs = refs
    hist, wq, wkv, wo, normed, query, mix, hist_sems, wq_sems, sems = refs
    rows, width = hist.shape
    hist_loads, wq_loads = [], []
    for a in range(agents):
        source = hist_hbm.at[pl.ds(a * steps + chunk * span, span), :]
        hist_loads.append(
            pltpu.make_async_copy(source, hist.at[pl.ds(a * span, span), :], hist_sems.at[a])
        )
    for c in range(0, width, COLS):
        cols = pl.ds(c, COLS)
        wq_loads.append(
            pltpu.make_async_copy(wq_hbm.at[:, cols], wq.at[:, cols], wq_sems.at[c // COLS])
        )
    loads = [
        pltpu.make_async_copy(wkv_hbm, wkv, sems.at[0]),
        pltpu.make_async_copy(wo_hbm, wo, sems.at[1]),
    ]
    for load in hist_loads + loads[:1]:
        load.start()
    for a in range(agents):
        part = pl.ds(a * span, span)
        hist_loads[a].wait()
        if a == 0:
            for load in wq_loads:
                load.start()
        normed[part, :] = norm_rows(hist[part, :], gain[...])
    loads[0].wait()
    for c in range(0, 2 * KEYS, COLS):
        keyval[:, c : c + COLS] = jnp.dot(
            normed[...], wkv[:, c : c + COLS], preferred_element_type=F32
        ).astype(BF16)
    loads[1].start()
    for c in range(0, width, COLS):
        wq_loads[c // COLS].wait()
        query[:, c : c + COLS] = jnp.dot(
            normed[...], wq[:, c : c + COLS], preferred_element_type=F32
        ).astype(BF16)

    keys = (chunk + 1) * span
    shape = (keys, pair * span)
    valid = lax.broadcasted_iota(jnp.int32, shape, 0) <= chunk * span + (
        lax.broadcasted_iota(jnp.int32, shape, 1) % span
    )

    def keyvals(a, cols):
        part = slice(a * span, (a + 1) * span)
        pieces = [ref[part, cols] for ref in (*before, keyval)]
        return jnp.concatenate(pieces, axis=0) if before else pieces[0]

    def store(a, cols, values):
        mix[a * span : (a + pair) * span, cols] = values

    attend(
        agents, pair, span, lambda a, cols: query[a * span : (a + 1) * span, cols],
        keyvals, store, valid,
    )
    order = one_hot(rows, block_source(agents, span, local))
    loads[1].wait()
    for c in range(0, width, COLS):
        cols = slice(c, c + COLS)
        projected = jnp.dot(mix[...], wo[:, cols], preferred_element_type=F32)
        piece = (hist[:, cols].astype(F32) + projected).astype(BF16)
        mid[:, cols] = piece
        sent[:, cols] = moved(order, piece)
    if listing:
        neighbours, nbr_valid, alive = listing
        lane = lax.broadcasted_iota(jnp.int32, (1, LANES), 1)
        notes = jnp.zeros((1, LANES), F32)
        for i in range(alive.shape[1]):
            notes = jnp.where(lane == i, alive[0, i].astype(F32), notes)
        for i in range(neighbours.shape[1]):
            listed = lane == alive.shape[1] + neighbours[0, i]
            notes = notes + jnp.where(listed, nbr_valid[0, i].astype(F32), 0.0)
        sent[:, width:] = jnp.broadcast_to(notes, (rows, LANES)).astype(BF16)


def keys_kernel(local, mid, gain, wkv, second, out):
    rows, width = second.shape
    total = rows // local
    second[...] = norm_rows(mid[:, :width], gain[...])
    if local > 1:
        order = one_hot(rows, step_source(total, local))
        for c in range(0, width, COLS):
            second[:, c : c + COLS] = moved(order, second[:, c : c + COLS])
    for c in range(0, 2 * KEYS, COLS):
        result = jnp.dot(second[...], wkv[:, c : c + COLS], preferred_element_type=F32)
        out[:, :, c : c + COLS] = result.astype(BF16).reshape(local, total, COLS)


def query_kernel(second, wq, out):
    local, total, width = out.shape
    for c in range(0, width, COLS):
        result = jnp.dot(second[...], wq[:, c : c + COLS], preferred_element_type=F32)
        out[:, :, c : c + COLS] = result.astype(BF16).reshape(local, total, COLS)


def weight_kernel(local, tiles, width, half, mid, out):
    rows = mid.shape[0]
    total = rows // local
    group = total // tiles
    notes = mid[:, width:]
    shape = (total, rows)
    row, col = (lax.broadcasted_iota(jnp.int32, shape, d) for d in range(2))
    pick = jnp.where(col == row * local, 1.0, 0.0).astype(BF16)
    lines = moved(pick, notes)
    shape = (HALVES * total, LANES)
    key, lane = (lax.broadcasted_iota(jnp.int32, shape, d) for d in range(2))
    side, tile, agent = (key // total + half[0]) % HALVES, key % total // group, key % group
    spread = jnp.where(lane == HALVES * group + tile, 1.0, 0.0).astype(BF16)
    listed = lax.dot_general(spread, lines, ROWS_BY_COLS, preferred_element_type=F32)
    spread = jnp.where(lane == side * group + agent, 1.0, 0.0).astype(BF16)
    alive = lax.dot_general(spread, lines, ROWS_BY_COLS, preferred_element_type=F32)
    shape = (HALVES * total, total)
    key, query = (lax.broadcasted_iota(jnp.int32, shape, d) for d in range(2))
    first = query == key % total // group * group
    alive = jnp.sum(jnp.where(first, alive, 0.0), axis=1, keepdims=True)
    out[...] = listed * alive


def space_kernel(pair, query, own, other, weights, out, mix):
    local, total, width = query.shape
    rows = local * total
    weight = jnp.concatenate([weights[...]] * pair, axis=1)

    def keyvals(s, cols):
        return jnp.concatenate([own[s, :, cols], other[s, :, cols]], axis=0)

    def store(s, cols, values):
        mix[s * total : (s + pair) * total, cols] = values

    attend(
        local, pair, total, lambda s, cols: query[s, :, cols], keyvals, store, weight > 0, weight
    )
    if local > 1:
        order = one_hot(rows, step_source(total, local), turned=True)
    for c in range(0, width, COLS):
        piece = mix[:, c : c + COLS]
        out[:, c : c + COLS] = moved(order, piece) if local > 1 else piece


def out_kernel(agents, span, local, chunks, *refs):
    mixes, mids, (wo, out, mix) = refs[:chunks], refs[chunks : 2 * chunks], refs[2 * chunks :]
    rows, width = mids[0].shape
    order = one_hot(rows, block_source(agents, span, local), turned=True)
    for c in range(0, width, COLS):
        for i in range(chunks):
            mix[i * rows : (i + 1) * rows, c : c + COLS] = moved(order, mixes[i][:, c : c + COLS])
    for c in range(0, width, COLS):
        cols = slice(c, c + COLS)
        projected = jnp.dot(mix[...], wo[:, cols], preferred_element_type=F32)
        for i in range(chunks):
            piece = mids[i][:, cols].astype(F32) + projected[i * rows : (i + 1) * rows]
            out[:, i * span : (i + 1) * span, cols] = piece.astype(BF16).reshape(agents, span, COLS)


def call(kernel, shapes, args, hbm=(), smem=(), scratch=(), flops=0, mib=16):
    touched = sum(a.size * a.dtype.itemsize for a in args)
    touched += sum(s.size * s.dtype.itemsize for s in shapes)
    spaces = [pl.ANY if i in hbm else pltpu.VMEM for i in range(len(args))]
    results = pl.pallas_call(
        kernel,
        out_shape=list(shapes),
        in_specs=[
            pl.BlockSpec(memory_space=pltpu.SMEM if i in smem else space)
            for i, space in enumerate(spaces)
        ],
        out_specs=[pl.BlockSpec(memory_space=pltpu.VMEM)] * len(shapes),
        scratch_shapes=list(scratch),
        compiler_params=pltpu.CompilerParams(vmem_limit_bytes=mib * MIB),
        cost_estimate=pl.CostEstimate(flops=flops, bytes_accessed=touched, transcendentals=0),
    )(*args)
    return results if len(shapes) > 1 else results[0]


def per_device(
    histories,
    gain_time,
    wq_time,
    wkv_time,
    wo_time,
    gain_space,
    wq_space,
    wkv_space,
    wo_space,
    neighbours,
    nbr_valid,
    agent_valid,
):
    agents, steps, width = histories.shape[1:]
    tiles, rest = lax.axis_size("tile"), lax.axis_size("rest")
    spread = ("tile", "rest")
    parts = tiles * rest
    chunks = CHUNKS if steps % (CHUNKS * parts) == 0 else 1
    span = steps // chunks
    local = span // parts
    rows = agents * span
    total = parts * agents
    struct = jax.ShapeDtypeStruct

    def beside(size, members):
        return LANES // size if size < LANES and members % (LANES // size) == 0 else 1

    hist = histories.reshape(agents * steps, width)
    mids, sents, before = [], [], []
    for i in range(chunks):
        deep = width + LANES if i == 0 else width
        mid, sent, keyval = call(
            functools.partial(time_kernel, agents, steps, span, i, local, beside(span, agents)),
            [struct((rows, width), BF16), struct((rows, deep), BF16), struct((rows, 2 * KEYS), BF16)],
            [hist, gain_time[None], wq_time, wkv_time, wo_time]
            + before
            + ([neighbours, nbr_valid, agent_valid] if i == 0 else []),
            hbm=(0, 2, 3, 4),
            smem=(5, 6, 7) if i == 0 else (),
            scratch=[
                pltpu.VMEM((rows, width), BF16),
                pltpu.VMEM(wq_time.shape, BF16),
                pltpu.VMEM(wkv_time.shape, BF16),
                pltpu.VMEM(wo_time.shape, BF16),
                pltpu.VMEM((rows, width), BF16),
                pltpu.VMEM((rows, width), BF16),
                pltpu.VMEM((rows, width), BF16),
                pltpu.SemaphoreType.DMA((agents,)),
                pltpu.SemaphoreType.DMA((width // COLS,)),
                pltpu.SemaphoreType.DMA((2,)),
            ],
            flops=2 * rows * width * (2 * width + 2 * KEYS),
            mib=56,
        )
        mids.append(mid)
        sents.append(sent.reshape(parts, agents * local, deep))
        before.append(keyval)

    swap = [(h, HALVES - 1 - h) for h in range(HALVES)]
    half = lax.axis_index("half").astype(jnp.int32).reshape(1)
    big = 16 + 16 * GROUPS * HALVES * total**2 // MIB
    mixes = []
    for i, sent in enumerate(sents):
        deep = sent.shape[-1]
        there = lax.all_to_all(sent, spread, split_axis=0, concat_axis=0, tiled=True)
        there = there.reshape(rows, deep)
        second, own = call(
            functools.partial(keys_kernel, local),
            [struct((rows, width), BF16), struct((local, total, 2 * KEYS), BF16)],
            [there, gain_space[None], wkv_space],
            flops=2 * rows * width * 2 * KEYS,
        )
        other = lax.ppermute(own, "half", swap)
        if i == 0:
            weight = call(
                functools.partial(weight_kernel, local, tiles, width),
                [struct((HALVES * total, total), F32)],
                [half, there],
                smem=(0,),
            )
        query = call(
            query_kernel,
            [struct((local, total, width), BF16)],
            [second, wq_space],
            flops=2 * rows * width * width,
        )
        mix = call(
            functools.partial(space_kernel, beside(total, local)),
            [struct((rows, width), BF16)],
            [query, own, other, weight],
            scratch=[pltpu.VMEM((rows, width), BF16)],
            flops=8 * rows * total * width,
            mib=big,
        )
        mix = mix.reshape(parts, agents * local, width)
        mix = lax.all_to_all(mix, spread, split_axis=0, concat_axis=0, tiled=True)
        mixes.append(mix.reshape(rows, width))
    out = call(
        functools.partial(out_kernel, agents, span, local, chunks),
        [struct((agents, steps, width), BF16)],
        mixes + mids + [wo_space],
        scratch=[pltpu.VMEM((agents * steps, width), BF16)],
        flops=2 * rows * width * width,
    )
    return out[None]


def solution(mesh):
    tiles, members = mesh.devices.shape
    split = Mesh(
        mesh.devices.reshape(tiles, HALVES, members // HALVES), ("tile", "half", "rest")
    )
    states = P("tile", ("half", "rest"), None, None)
    listing = P("tile", None)
    return jax.shard_map(
        per_device,
        mesh=split,
        in_specs=(states,) + (P(),) * 8 + (listing,) * 3,
        out_specs=states,
        check_vma=False,
    )
```

```python
import functools
import math

import jax
import jax.numpy as jnp
from jax import lax
from jax.experimental import pallas as pl
from jax.experimental.pallas import tpu as pltpu
from jax.sharding import Mesh
from jax.sharding import PartitionSpec as P

HEADS = 16
KV_HEADS = 4
HEAD_DIM = 64
GROUPS = HEADS // KV_HEADS
KEYS = KV_HEADS * HEAD_DIM
WIDE = GROUPS * HEAD_DIM
SCALE = HEAD_DIM ** (-0.5)
EXP2_SCALE = SCALE * math.log2(math.e)
NEG = -1e30
LANES = 128
COLS = 256
HALVES = 2
CHUNKS = 2
DEPTH = 2
SHADOW = 100
MIB = 1024 * 1024
F32 = jnp.float32
BF16 = jnp.bfloat16
ROWS_BY_COLS = (((1,), (1,)), ((), ()))


def norm_rows(values, gain):
    wide = values.astype(F32)
    meansq = jnp.mean(wide * wide, axis=-1, keepdims=True)
    return (wide * lax.rsqrt(meansq + 1e-05) * gain).astype(BF16)


def one_hot(rows, source, turned=False):
    row = lax.broadcasted_iota(jnp.int32, (rows, rows), 1 if turned else 0)
    col = lax.broadcasted_iota(jnp.int32, (rows, rows), 0 if turned else 1)
    return jnp.where(col == source(row), 1.0, 0.0).astype(BF16)


def block_source(agents, span, local):
    return lambda row: row // local % agents * span + row // (local * agents) * local + row % local


def step_source(total, local):
    return lambda row: row % total * local + row // total


def moved(order, piece):
    return jnp.dot(order, piece, preferred_element_type=F32).astype(BF16)


def staggered(units, first, second, third):
    scores, grown = {}, {}
    for i in range(len(units) + 2 * DEPTH):
        if i < len(units):
            scores[i] = first(*units[i])
        if 0 <= i - DEPTH < len(units):
            grown[i - DEPTH] = second(scores.pop(i - DEPTH))
        if 0 <= i - 2 * DEPTH < len(units):
            third(units[i - 2 * DEPTH], *grown.pop(i - 2 * DEPTH))


def attend(members, pair, size, query, keyval, store, valid, weight=None):
    columns = pair * size
    together = GROUPS if columns <= LANES else 1
    valid = jnp.concatenate([valid] * together, axis=1)
    if weight is not None:
        weight = jnp.concatenate([weight] * together, axis=1)
    lane = lax.broadcasted_iota(jnp.int32, (HEAD_DIM, columns), 1) // size

    def scores_of(m, k, heads):
        turned = [query(m + s, slice(k * WIDE, (k + 1) * WIDE)) for s in range(pair)]
        turned = jnp.concatenate(turned, axis=0).T
        turned = [turned[j * HEAD_DIM : (j + 1) * HEAD_DIM] for j in heads]
        if pair > 1:
            zero = jnp.zeros((HEAD_DIM, columns), BF16)
            turned = [
                jnp.concatenate([jnp.where(lane == s, t, zero) for s in range(pair)], axis=0)
                for t in turned
            ]
        part = slice(k * HEAD_DIM, (k + 1) * HEAD_DIM)
        keys = jnp.concatenate([keyval(m + s, part) for s in range(pair)], axis=1)
        return jnp.dot(keys, jnp.concatenate(turned, axis=1), preferred_element_type=F32)

    def grow(scores):
        scores = jnp.where(valid, scores, NEG)
        top = jnp.max(scores, axis=0, keepdims=True)
        grown = jnp.exp2((scores - top) * EXP2_SCALE)
        if weight is not None:
            grown = grown * weight
        return grown.astype(BF16), jnp.sum(grown, axis=0, keepdims=True)

    def values_of(unit, grown, sums):
        m, k, heads = unit
        part = slice(KEYS + k * HEAD_DIM, KEYS + (k + 1) * HEAD_DIM)
        vals = jnp.concatenate([keyval(m + s, part).T for s in range(pair)], axis=0)
        mixed = jnp.dot(vals, grown, preferred_element_type=F32)
        inverse = 1.0 / sums
        parts = []
        for i in range(len(heads)):
            cols = slice(i * columns, (i + 1) * columns)
            chosen = mixed[:HEAD_DIM, cols]
            for s in range(1, pair):
                chosen = jnp.where(lane == s, mixed[s * HEAD_DIM : (s + 1) * HEAD_DIM, cols], chosen)
            parts.append(chosen * inverse[:, cols])
        mixed = jnp.concatenate(parts, axis=0).astype(BF16).T
        start = k * WIDE + heads[0] * HEAD_DIM
        store(m, slice(start, start + len(heads) * HEAD_DIM), mixed)

    units = [
        (m, k, tuple(range(j, j + together)))
        for m in range(0, members, pair)
        for k in range(KV_HEADS)
        for j in range(0, GROUPS, together)
    ]
    staggered(units, scores_of, grow, values_of)


def time_kernel(agents, steps, span, chunk, local, pair, *refs):
    hist_hbm, gain, wq_hbm, wkv_hbm, wo_hbm, *refs = refs
    before, refs = refs[:chunk], refs[chunk:]
    listing, refs = (refs[:3], refs[3:]) if chunk == 0 else ((), refs)
    mid, sent, keyval, *refs = refs
    hist, wq, wkv, wo, normed, query, mix, hist_sems, wq_sems, sems = refs
    rows, width = hist.shape
    hist_loads, wq_loads = [], []
    for a in range(agents):
        source = hist_hbm.at[pl.ds(a * steps + chunk * span, span), :]
        hist_loads.append(
            pltpu.make_async_copy(source, hist.at[pl.ds(a * span, span), :], hist_sems.at[a])
        )
    for c in range(0, width, COLS):
        cols = pl.ds(c, COLS)
        wq_loads.append(
            pltpu.make_async_copy(wq_hbm.at[:, cols], wq.at[:, cols], wq_sems.at[c // COLS])
        )
    loads = [
        pltpu.make_async_copy(wkv_hbm, wkv, sems.at[0]),
        pltpu.make_async_copy(wo_hbm, wo, sems.at[1]),
    ]
    for load in hist_loads + loads[:1]:
        load.start()
    for a in range(agents):
        part = pl.ds(a * span, span)
        hist_loads[a].wait()
        if a == 0:
            for load in wq_loads:
                load.start()
        normed[part, :] = norm_rows(hist[part, :], gain[...])
    loads[0].wait()
    for c in range(0, 2 * KEYS, COLS):
        keyval[:, c : c + COLS] = jnp.dot(
            normed[...], wkv[:, c : c + COLS], preferred_element_type=F32
        ).astype(BF16)
    loads[1].start()
    for c in range(0, width, COLS):
        wq_loads[c // COLS].wait()
        query[:, c : c + COLS] = jnp.dot(
            normed[...], wq[:, c : c + COLS], preferred_element_type=F32
        ).astype(BF16)

    keys = (chunk + 1) * span
    shape = (keys, pair * span)
    valid = lax.broadcasted_iota(jnp.int32, shape, 0) <= chunk * span + (
        lax.broadcasted_iota(jnp.int32, shape, 1) % span
    )

    def keyvals(a, cols):
        part = slice(a * span, (a + 1) * span)
        pieces = [ref[part, cols] for ref in (*before, keyval)]
        return jnp.concatenate(pieces, axis=0) if before else pieces[0]

    def store(a, cols, values):
        mix[a * span : (a + pair) * span, cols] = values

    attend(
        agents, pair, span, lambda a, cols: query[a * span : (a + 1) * span, cols],
        keyvals, store, valid,
    )
    order = one_hot(rows, block_source(agents, span, local))
    loads[1].wait()
    for c in range(0, width, COLS):
        cols = slice(c, c + COLS)
        projected = jnp.dot(mix[...], wo[:, cols], preferred_element_type=F32)
        piece = (hist[:, cols].astype(F32) + projected).astype(BF16)
        mid[:, cols] = piece
        sent[:, cols] = moved(order, piece)
    if listing:
        neighbours, nbr_valid, alive = listing
        lane = lax.broadcasted_iota(jnp.int32, (1, LANES), 1)
        notes = jnp.zeros((1, LANES), F32)
        for i in range(alive.shape[1]):
            notes = jnp.where(lane == i, alive[0, i].astype(F32), notes)
        for i in range(neighbours.shape[1]):
            listed = lane == alive.shape[1] + neighbours[0, i]
            notes = notes + jnp.where(listed, nbr_valid[0, i].astype(F32), 0.0)
        sent[:, width:] = jnp.broadcast_to(notes, (rows, LANES)).astype(BF16)


def keys_kernel(local, mid, gain, wkv, second, out):
    rows, width = second.shape
    total = rows // local
    second[...] = norm_rows(mid[:, :width], gain[...])
    if local > 1:
        order = one_hot(rows, step_source(total, local))
        for c in range(0, width, COLS):
            second[:, c : c + COLS] = moved(order, second[:, c : c + COLS])
    for c in range(0, 2 * KEYS, COLS):
        result = jnp.dot(second[...], wkv[:, c : c + COLS], preferred_element_type=F32)
        out[:, :, c : c + COLS] = result.astype(BF16).reshape(local, total, COLS)


def query_kernel(second, wq, out):
    local, total, width = out.shape
    for c in range(0, width, COLS):
        result = jnp.dot(second[...], wq[:, c : c + COLS], preferred_element_type=F32)
        out[:, :, c : c + COLS] = result.astype(BF16).reshape(local, total, COLS)


def weight_kernel(local, tiles, width, half, mid, out):
    rows = mid.shape[0]
    total = rows // local
    group = total // tiles
    notes = mid[:, width:]
    shape = (total, rows)
    row, col = (lax.broadcasted_iota(jnp.int32, shape, d) for d in range(2))
    pick = jnp.where(col == row * local, 1.0, 0.0).astype(BF16)
    lines = moved(pick, notes)
    shape = (HALVES * total, LANES)
    key, lane = (lax.broadcasted_iota(jnp.int32, shape, d) for d in range(2))
    side, tile, agent = (key // total + half[0]) % HALVES, key % total // group, key % group
    spread = jnp.where(lane == HALVES * group + tile, 1.0, 0.0).astype(BF16)
    listed = lax.dot_general(spread, lines, ROWS_BY_COLS, preferred_element_type=F32)
    spread = jnp.where(lane == side * group + agent, 1.0, 0.0).astype(BF16)
    alive = lax.dot_general(spread, lines, ROWS_BY_COLS, preferred_element_type=F32)
    shape = (HALVES * total, total)
    key, query = (lax.broadcasted_iota(jnp.int32, shape, d) for d in range(2))
    first = query == key % total // group * group
    alive = jnp.sum(jnp.where(first, alive, 0.0), axis=1, keepdims=True)
    out[...] = listed * alive


def space_kernel(pair, query, own, other, weights, out, mix):
    local, total, width = query.shape
    rows = local * total
    weight = jnp.concatenate([weights[...]] * pair, axis=1)

    def keyvals(s, cols):
        return jnp.concatenate([own[s, :, cols], other[s, :, cols]], axis=0)

    def store(s, cols, values):
        mix[s * total : (s + pair) * total, cols] = values

    attend(
        local, pair, total, lambda s, cols: query[s, :, cols], keyvals, store, weight > 0, weight
    )
    if local > 1:
        order = one_hot(rows, step_source(total, local), turned=True)
    for c in range(0, width, COLS):
        piece = mix[:, c : c + COLS]
        out[:, c : c + COLS] = moved(order, piece) if local > 1 else piece


def out_kernel(agents, span, local, chunks, *refs):
    mixes, mids, (wo, out, mix) = refs[:chunks], refs[chunks : 2 * chunks], refs[2 * chunks :]
    rows, width = mids[0].shape
    order = one_hot(rows, block_source(agents, span, local), turned=True)
    for c in range(0, width, COLS):
        for i in range(chunks):
            mix[i * rows : (i + 1) * rows, c : c + COLS] = moved(order, mixes[i][:, c : c + COLS])
    for c in range(0, width, COLS):
        cols = slice(c, c + COLS)
        projected = jnp.dot(mix[...], wo[:, cols], preferred_element_type=F32)
        for i in range(chunks):
            piece = mids[i][:, cols].astype(F32) + projected[i * rows : (i + 1) * rows]
            out[:, i * span : (i + 1) * span, cols] = piece.astype(BF16).reshape(agents, span, COLS)


def call(kernel, shapes, args, hbm=(), smem=(), scratch=(), flops=0, mib=16):
    touched = sum(a.size * a.dtype.itemsize for a in args)
    touched += sum(s.size * s.dtype.itemsize for s in shapes)
    spaces = [pl.ANY if i in hbm else pltpu.VMEM for i in range(len(args))]
    results = pl.pallas_call(
        kernel,
        out_shape=list(shapes),
        in_specs=[
            pl.BlockSpec(memory_space=pltpu.SMEM if i in smem else space)
            for i, space in enumerate(spaces)
        ],
        out_specs=[pl.BlockSpec(memory_space=pltpu.VMEM)] * len(shapes),
        scratch_shapes=list(scratch),
        compiler_params=pltpu.CompilerParams(vmem_limit_bytes=mib * MIB),
        cost_estimate=pl.CostEstimate(flops=flops, bytes_accessed=touched, transcendentals=0),
    )(*args)
    return results if len(shapes) > 1 else results[0]


def per_device(
    histories,
    gain_time,
    wq_time,
    wkv_time,
    wo_time,
    gain_space,
    wq_space,
    wkv_space,
    wo_space,
    neighbours,
    nbr_valid,
    agent_valid,
):
    agents, steps, width = histories.shape[1:]
    tiles, rest = lax.axis_size("tile"), lax.axis_size("rest")
    spread = ("tile", "rest")
    parts = tiles * rest
    chunks = CHUNKS if steps % (CHUNKS * parts) == 0 else 1
    span = steps // chunks
    local = span // parts
    rows = agents * span
    total = parts * agents
    struct = jax.ShapeDtypeStruct

    def beside(size, members):
        return LANES // size if size < LANES and members % (LANES // size) == 0 else 1

    hist = histories.reshape(agents * steps, width)
    mids, sents, before = [], [], []
    for i in range(chunks):
        deep = width + LANES if i == 0 else width
        mid, sent, keyval = call(
            functools.partial(time_kernel, agents, steps, span, i, local, beside(span, agents)),
            [struct((rows, width), BF16), struct((rows, deep), BF16), struct((rows, 2 * KEYS), BF16)],
            [hist, gain_time[None], wq_time, wkv_time, wo_time]
            + before
            + ([neighbours, nbr_valid, agent_valid] if i == 0 else []),
            hbm=(0, 2, 3, 4),
            smem=(5, 6, 7) if i == 0 else (),
            scratch=[
                pltpu.VMEM((rows, width), BF16),
                pltpu.VMEM(wq_time.shape, BF16),
                pltpu.VMEM(wkv_time.shape, BF16),
                pltpu.VMEM(wo_time.shape, BF16),
                pltpu.VMEM((rows, width), BF16),
                pltpu.VMEM((rows, width), BF16),
                pltpu.VMEM((rows, width), BF16),
                pltpu.SemaphoreType.DMA((agents,)),
                pltpu.SemaphoreType.DMA((width // COLS,)),
                pltpu.SemaphoreType.DMA((2,)),
            ],
            flops=2 * rows * width * (2 * width + 2 * KEYS),
            mib=56,
        )
        mids.append(mid)
        sents.append(sent.reshape(parts, agents * local, deep))
        before.append(keyval)

    swap = [(h, HALVES - 1 - h) for h in range(HALVES)]
    half = lax.axis_index("half").astype(jnp.int32).reshape(1)
    big = 16 + 16 * GROUPS * HALVES * total**2 // MIB
    homes, mixes = [], []
    for i, sent in enumerate(sents):
        deep = sent.shape[-1]
        there = lax.all_to_all(sent, spread, split_axis=0, concat_axis=0, tiled=True)
        there = there.reshape(rows, deep)
        if i + 1 < chunks:
            there, sents[i + 1] = lax.optimization_barrier((there, sents[i + 1]))
        second, own = call(
            functools.partial(keys_kernel, local),
            [struct((rows, width), BF16), struct((local, total, 2 * KEYS), BF16)],
            [there, gain_space[None], wkv_space],
            flops=2 * rows * width * 2 * KEYS,
        )
        other = lax.ppermute(own, "half", swap)
        if i == 0:
            weight = call(
                functools.partial(weight_kernel, local, tiles, width),
                [struct((HALVES * total, total), F32)],
                [half, there],
                smem=(0,),
            )
        query = call(
            query_kernel,
            [struct((local, total, width), BF16)],
            [second, wq_space],
            flops=(2 if i == 0 else SHADOW) * rows * width * width,
        )
        homes.append((query, own, other))
    for i in range(chunks - 1):
        (query, own, other), (later, *held) = homes[i], homes[i + 1]
        own, held[0] = lax.optimization_barrier((own, held[0]))
        homes[i], homes[i + 1] = (query, own, other), (later, *held)
    for query, own, other in homes:
        mix = call(
            functools.partial(space_kernel, beside(total, local)),
            [struct((rows, width), BF16)],
            [query, own, other, weight],
            scratch=[pltpu.VMEM((rows, width), BF16)],
            flops=8 * rows * total * width,
            mib=big,
        )
        mix = mix.reshape(parts, agents * local, width)
        mix = lax.all_to_all(mix, spread, split_axis=0, concat_axis=0, tiled=True)
        mixes.append(mix.reshape(rows, width))
    out = call(
        functools.partial(out_kernel, agents, span, local, chunks),
        [struct((agents, steps, width), BF16)],
        mixes + mids + [wo_space],
        scratch=[pltpu.VMEM((agents * steps, width), BF16)],
        flops=2 * rows * width * width,
    )
    return out[None]


def solution(mesh):
    tiles, members = mesh.devices.shape
    split = Mesh(
        mesh.devices.reshape(tiles, HALVES, members // HALVES), ("tile", "half", "rest")
    )
    states = P("tile", ("half", "rest"), None, None)
    listing = P("tile", None)
    return jax.shard_map(
        per_device,
        mesh=split,
        in_specs=(states,) + (P(),) * 8 + (listing,) * 3,
        out_specs=states,
        check_vma=False,
    )
```

```python
import functools
import math

import jax
import jax.numpy as jnp
from jax import lax
from jax.experimental import pallas as pl
from jax.experimental.pallas import tpu as pltpu
from jax.sharding import Mesh
from jax.sharding import PartitionSpec as P

HEADS = 16
KV_HEADS = 4
HEAD_DIM = 64
GROUPS = HEADS // KV_HEADS
KEYS = KV_HEADS * HEAD_DIM
WIDE = GROUPS * HEAD_DIM
SCALE = HEAD_DIM ** (-0.5)
EXP2_SCALE = SCALE * math.log2(math.e)
NEG = -1e30
LANES = 128
COLS = 256
HALVES = 2
CHUNKS = 2
DEPTH = 2
SHADOW = 100
MIB = 1024 * 1024
F32 = jnp.float32
BF16 = jnp.bfloat16
ROWS_BY_COLS = (((1,), (1,)), ((), ()))


def norm_rows(values, gain):
    wide = values.astype(F32)
    meansq = jnp.mean(wide * wide, axis=-1, keepdims=True)
    return (wide * lax.rsqrt(meansq + 1e-05) * gain).astype(BF16)


def one_hot(rows, target):
    row = lax.broadcasted_iota(jnp.int32, (rows, rows), 0)
    wanted = target(lax.broadcasted_iota(jnp.int32, (1, rows), 1))
    return jnp.where(row == wanted, 1.0, 0.0).astype(BF16)


def regroup(row, first, second, third):
    i, j, k = row // (second * third), row // third % second, row % third
    return (j * first + i) * third + k


def moved(order, piece):
    return jnp.dot(order, piece, preferred_element_type=F32).astype(BF16)


def staggered(units, first, second, third):
    scores, grown = {}, {}
    for i in range(len(units) + 2 * DEPTH):
        if i < len(units):
            scores[i] = first(*units[i])
        if 0 <= i - DEPTH < len(units):
            grown[i - DEPTH] = second(scores.pop(i - DEPTH))
        if 0 <= i - 2 * DEPTH < len(units):
            third(units[i - 2 * DEPTH], *grown.pop(i - 2 * DEPTH))


def attend(members, pair, size, query, keyval, store, valid, weight=None):
    columns = pair * size
    together = GROUPS if columns <= LANES else 1
    valid = jnp.concatenate([valid] * together, axis=1)
    if weight is not None:
        weight = jnp.concatenate([weight] * together, axis=1)
    lane = lax.broadcasted_iota(jnp.int32, (HEAD_DIM, columns), 1) // size

    def scores_of(m, k, heads):
        turned = [query(m + s, slice(k * WIDE, (k + 1) * WIDE)) for s in range(pair)]
        turned = jnp.concatenate(turned, axis=0).T
        turned = [turned[j * HEAD_DIM : (j + 1) * HEAD_DIM] for j in heads]
        if pair > 1:
            zero = jnp.zeros((HEAD_DIM, columns), BF16)
            turned = [
                jnp.concatenate([jnp.where(lane == s, t, zero) for s in range(pair)], axis=0)
                for t in turned
            ]
        part = slice(k * HEAD_DIM, (k + 1) * HEAD_DIM)
        keys = jnp.concatenate([keyval(m + s, part) for s in range(pair)], axis=1)
        return jnp.dot(keys, jnp.concatenate(turned, axis=1), preferred_element_type=F32)

    def grow(scores):
        scores = jnp.where(valid, scores, NEG)
        top = jnp.max(scores, axis=0, keepdims=True)
        grown = jnp.exp2((scores - top) * EXP2_SCALE)
        if weight is not None:
            grown = grown * weight
        return grown.astype(BF16), jnp.sum(grown, axis=0, keepdims=True)

    def values_of(unit, grown, sums):
        m, k, heads = unit
        part = slice(KEYS + k * HEAD_DIM, KEYS + (k + 1) * HEAD_DIM)
        vals = jnp.concatenate([keyval(m + s, part).T for s in range(pair)], axis=0)
        mixed = jnp.dot(vals, grown, preferred_element_type=F32)
        inverse = 1.0 / sums
        parts = []
        for i in range(len(heads)):
            cols = slice(i * columns, (i + 1) * columns)
            chosen = mixed[:HEAD_DIM, cols]
            for s in range(1, pair):
                chosen = jnp.where(lane == s, mixed[s * HEAD_DIM : (s + 1) * HEAD_DIM, cols], chosen)
            parts.append(chosen * inverse[:, cols])
        mixed = jnp.concatenate(parts, axis=0).astype(BF16).T
        start = k * WIDE + heads[0] * HEAD_DIM
        store(m, slice(start, start + len(heads) * HEAD_DIM), mixed)

    units = [
        (m, k, tuple(range(j, j + together)))
        for m in range(0, members, pair)
        for k in range(KV_HEADS)
        for j in range(0, GROUPS, together)
    ]
    staggered(units, scores_of, grow, values_of)


def time_kernel(agents, steps, span, chunk, local, pair, *refs):
    hist_hbm, gain, wq_hbm, wkv_hbm, wo_hbm, *refs = refs
    before, refs = refs[:chunk], refs[chunk:]
    refs = refs[1:] if chunk else refs
    listing, refs = (refs[:3], refs[3:]) if chunk == 0 else ((), refs)
    mid_hbm, sent_hbm, keyval_hbm, *refs = refs
    mid, sent, keyval, hist, wq, wkv, wo, normed, query, mix, *refs = refs
    hist_sems, wq_sems, sems, mid_sems, sent_sems, keyval_sem = refs
    rows, width = hist.shape
    hist_loads, wq_loads = [], []
    for a in range(agents):
        source = hist_hbm.at[pl.ds(a * steps + chunk * span, span), :]
        hist_loads.append(
            pltpu.make_async_copy(source, hist.at[pl.ds(a * span, span), :], hist_sems.at[a])
        )
    for c in range(0, width, COLS):
        cols = pl.ds(c, COLS)
        wq_loads.append(
            pltpu.make_async_copy(wq_hbm.at[:, cols], wq.at[:, cols], wq_sems.at[c // COLS])
        )
    loads = [
        pltpu.make_async_copy(wkv_hbm, wkv, sems.at[0]),
        pltpu.make_async_copy(wo_hbm, wo, sems.at[1]),
    ]
    for load in hist_loads + loads[:1]:
        load.start()
    for a in range(agents):
        part = pl.ds(a * span, span)
        hist_loads[a].wait()
        if a == 0:
            for load in wq_loads:
                load.start()
        normed[part, :] = norm_rows(hist[part, :], gain[...])
    loads[0].wait()
    for c in range(0, 2 * KEYS, COLS):
        keyval[:, c : c + COLS] = jnp.dot(
            normed[...], wkv[:, c : c + COLS], preferred_element_type=F32
        ).astype(BF16)
    keeps = [pltpu.make_async_copy(keyval, keyval_hbm, keyval_sem)]
    keeps[0].start()
    loads[1].start()
    for c in range(0, width, COLS):
        wq_loads[c // COLS].wait()
        query[:, c : c + COLS] = jnp.dot(
            normed[...], wq[:, c : c + COLS], preferred_element_type=F32
        ).astype(BF16)

    keys = (chunk + 1) * span
    shape = (keys, pair * span)
    valid = lax.broadcasted_iota(jnp.int32, shape, 0) <= chunk * span + (
        lax.broadcasted_iota(jnp.int32, shape, 1) % span
    )

    def keyvals(a, cols):
        part = slice(a * span, (a + 1) * span)
        pieces = [ref[part, cols] for ref in (*before, keyval)]
        return jnp.concatenate(pieces, axis=0) if before else pieces[0]

    def store(a, cols, values):
        mix[a * span : (a + pair) * span, cols] = values

    attend(
        agents, pair, span, lambda a, cols: query[a * span : (a + 1) * span, cols],
        keyvals, store, valid,
    )
    order = one_hot(rows, lambda row: regroup(row, agents, span // local, local))
    loads[1].wait()
    for c in range(0, width, COLS):
        cols = slice(c, c + COLS)
        projected = jnp.dot(mix[...], wo[:, cols], preferred_element_type=F32)
        piece = (hist[:, cols].astype(F32) + projected).astype(BF16)
        mid[:, cols] = piece
        sent[:, cols] = moved(order, piece)
        part = pl.ds(c, COLS)
        keeps.append(
            pltpu.make_async_copy(sent.at[:, part], sent_hbm.at[:, part], sent_sems.at[c // COLS])
        )
        keeps[-1].start()
    for a in range(agents):
        goal = mid_hbm.at[a, pl.ds(chunk * span, span), :]
        keeps.append(
            pltpu.make_async_copy(mid.at[pl.ds(a * span, span), :], goal, mid_sems.at[a])
        )
        keeps[-1].start()
    if listing:
        neighbours, nbr_valid, alive = listing
        lane = lax.broadcasted_iota(jnp.int32, (1, LANES), 1)
        notes = jnp.zeros((1, LANES), F32)
        for i in range(alive.shape[1]):
            notes = jnp.where(lane == i, alive[0, i].astype(F32), notes)
        for i in range(neighbours.shape[1]):
            listed = lane == alive.shape[1] + neighbours[0, i]
            notes = notes + jnp.where(listed, nbr_valid[0, i].astype(F32), 0.0)
        sent[:, width:] = jnp.broadcast_to(notes, (rows, LANES)).astype(BF16)
        part = pl.ds(width, LANES)
        keeps.append(
            pltpu.make_async_copy(
                sent.at[:, part], sent_hbm.at[:, part], sent_sems.at[width // COLS]
            )
        )
        keeps[-1].start()
    for keep in keeps:
        keep.wait()


def keys_kernel(local, mid, gain, wkv, second, out):
    rows, width = second.shape
    total = rows // local
    second[...] = norm_rows(mid[:, :width], gain[...])
    if local > 1:
        order = one_hot(rows, lambda row: regroup(row, total, local, 1))
        for c in range(0, width, COLS):
            second[:, c : c + COLS] = moved(order, second[:, c : c + COLS])
    for c in range(0, 2 * KEYS, COLS):
        result = jnp.dot(second[...], wkv[:, c : c + COLS], preferred_element_type=F32)
        out[:, :, c : c + COLS] = result.astype(BF16).reshape(local, total, COLS)


def query_kernel(second, wq, out):
    local, total, width = out.shape
    for c in range(0, width, COLS):
        result = jnp.dot(second[...], wq[:, c : c + COLS], preferred_element_type=F32)
        out[:, :, c : c + COLS] = result.astype(BF16).reshape(local, total, COLS)


def weight_kernel(local, tiles, width, half, mid, out):
    rows = mid.shape[0]
    total = rows // local
    group = total // tiles
    notes = mid[:, width:]
    shape = (total, rows)
    row, col = (lax.broadcasted_iota(jnp.int32, shape, d) for d in range(2))
    pick = jnp.where(col == row * local, 1.0, 0.0).astype(BF16)
    lines = moved(pick, notes)
    shape = (HALVES * total, LANES)
    key, lane = (lax.broadcasted_iota(jnp.int32, shape, d) for d in range(2))
    side, tile, agent = (key // total + half[0]) % HALVES, key % total // group, key % group
    spread = jnp.where(lane == HALVES * group + tile, 1.0, 0.0).astype(BF16)
    listed = lax.dot_general(spread, lines, ROWS_BY_COLS, preferred_element_type=F32)
    spread = jnp.where(lane == side * group + agent, 1.0, 0.0).astype(BF16)
    alive = lax.dot_general(spread, lines, ROWS_BY_COLS, preferred_element_type=F32)
    shape = (HALVES * total, total)
    key, query = (lax.broadcasted_iota(jnp.int32, shape, d) for d in range(2))
    first = query == key % total // group * group
    alive = jnp.sum(jnp.where(first, alive, 0.0), axis=1, keepdims=True)
    out[...] = listed * alive


def space_kernel(pair, query, own, other, weights, out, mix):
    local, total, width = query.shape
    rows = local * total
    weight = jnp.concatenate([weights[...]] * pair, axis=1)

    def keyvals(s, cols):
        return jnp.concatenate([own[s, :, cols], other[s, :, cols]], axis=0)

    def store(s, cols, values):
        mix[s * total : (s + pair) * total, cols] = values

    attend(
        local, pair, total, lambda s, cols: query[s, :, cols], keyvals, store, weight > 0, weight
    )
    if local > 1:
        order = one_hot(rows, lambda row: regroup(row, local, total, 1))
    for c in range(0, width, COLS):
        piece = mix[:, c : c + COLS]
        out[:, c : c + COLS] = moved(order, piece) if local > 1 else piece


def out_kernel(agents, span, local, chunks, *refs):
    mixes, (mid_hbm, wo, out_hbm, mix, mids, sems, out_sems) = refs[:chunks], refs[chunks:]
    rows, width = mixes[0].shape
    loads = [
        pltpu.make_async_copy(mid_hbm.at[:, pl.ds(i * span, span), :], mids.at[i], sems.at[i])
        for i in range(chunks)
    ]
    for load in loads:
        load.start()
    order = one_hot(rows, lambda row: regroup(row, span // local, agents, local))
    for c in range(0, width, COLS):
        for i in range(chunks):
            mix[i * rows : (i + 1) * rows, c : c + COLS] = moved(order, mixes[i][:, c : c + COLS])
    for load in loads:
        load.wait()
    for c in range(0, width, COLS):
        cols = slice(c, c + COLS)
        projected = jnp.dot(mix[...], wo[:, cols], preferred_element_type=F32)
        for i in range(chunks):
            piece = projected[i * rows : (i + 1) * rows].reshape(agents, span, COLS)
            mids[i, :, :, cols] = (mids[i, :, :, cols].astype(F32) + piece).astype(BF16)
    keeps = [
        pltpu.make_async_copy(mids.at[i], out_hbm.at[:, pl.ds(i * span, span), :], out_sems.at[i])
        for i in range(chunks)
    ]
    for keep in keeps:
        keep.start()
    for keep in keeps:
        keep.wait()


def call(
    kernel, shapes, args, hbm=(), hbm_out=(), smem=(), aliases=None, scratch=(), flops=0, mib=16
):
    touched = sum(a.size * a.dtype.itemsize for a in args)
    touched += sum(s.size * s.dtype.itemsize for s in shapes)
    spaces = [pl.ANY if i in hbm else pltpu.VMEM for i in range(len(args))]
    results = pl.pallas_call(
        kernel,
        out_shape=list(shapes),
        in_specs=[
            pl.BlockSpec(memory_space=pltpu.SMEM if i in smem else space)
            for i, space in enumerate(spaces)
        ],
        out_specs=[
            pl.BlockSpec(memory_space=pl.ANY if i in hbm_out else pltpu.VMEM)
            for i in range(len(shapes))
        ],
        scratch_shapes=list(scratch),
        input_output_aliases=aliases or {},
        compiler_params=pltpu.CompilerParams(vmem_limit_bytes=mib * MIB),
        cost_estimate=pl.CostEstimate(flops=flops, bytes_accessed=touched, transcendentals=0),
    )(*args)
    return results if len(shapes) > 1 else results[0]


def per_device(
    histories,
    gain_time,
    wq_time,
    wkv_time,
    wo_time,
    gain_space,
    wq_space,
    wkv_space,
    wo_space,
    neighbours,
    nbr_valid,
    agent_valid,
):
    agents, steps, width = histories.shape[1:]
    tiles, rest = lax.axis_size("tile"), lax.axis_size("rest")
    spread = ("tile", "rest")
    parts = tiles * rest
    chunks = CHUNKS if steps % (CHUNKS * parts) == 0 else 1
    span = steps // chunks
    local = span // parts
    rows = agents * span
    total = parts * agents
    struct = jax.ShapeDtypeStruct

    def beside(size, members):
        return LANES // size if size < LANES and members % (LANES // size) == 0 else 1

    hist = histories.reshape(agents * steps, width)
    mids, sents, before = [], [], []
    whole = struct((agents, steps, width), BF16)
    for i in range(chunks):
        deep = width + LANES if i == 0 else width
        mid, sent, keyval = call(
            functools.partial(time_kernel, agents, steps, span, i, local, beside(span, agents)),
            [whole, struct((rows, deep), BF16), struct((rows, 2 * KEYS), BF16)],
            [hist, gain_time[None], wq_time, wkv_time, wo_time]
            + before
            + mids
            + ([neighbours, nbr_valid, agent_valid] if i == 0 else []),
            hbm=(0, 2, 3, 4) + ((5 + i,) if i else ()),
            aliases={5 + i: 0} if i else None,
            smem=(5, 6, 7) if i == 0 else (),
            hbm_out=(0, 1, 2),
            scratch=[
                pltpu.VMEM((rows, width), BF16),
                pltpu.VMEM((rows, deep), BF16),
                pltpu.VMEM((rows, 2 * KEYS), BF16),
                pltpu.VMEM((rows, width), BF16),
                pltpu.VMEM(wq_time.shape, BF16),
                pltpu.VMEM(wkv_time.shape, BF16),
                pltpu.VMEM(wo_time.shape, BF16),
                pltpu.VMEM((rows, width), BF16),
                pltpu.VMEM((rows, width), BF16),
                pltpu.VMEM((rows, width), BF16),
                pltpu.SemaphoreType.DMA((agents,)),
                pltpu.SemaphoreType.DMA((width // COLS,)),
                pltpu.SemaphoreType.DMA((2,)),
                pltpu.SemaphoreType.DMA((agents,)),
                pltpu.SemaphoreType.DMA((width // COLS + 1,)),
                pltpu.SemaphoreType.DMA,
            ],
            flops=2 * rows * width * (2 * width + 2 * KEYS),
            mib=56,
        )
        mids = [mid]
        sents.append(sent.reshape(parts, agents * local, deep))
        before.append(keyval)

    swap = [(h, HALVES - 1 - h) for h in range(HALVES)]
    half = lax.axis_index("half").astype(jnp.int32).reshape(1)
    big = 16 + 16 * GROUPS * HALVES * total**2 // MIB
    homes, mixes = [], []
    for i, sent in enumerate(sents):
        deep = sent.shape[-1]
        there = lax.all_to_all(sent, spread, split_axis=0, concat_axis=0, tiled=True)
        there = there.reshape(rows, deep)
        if i + 1 < chunks:
            there, sents[i + 1] = lax.optimization_barrier((there, sents[i + 1]))
        second, own = call(
            functools.partial(keys_kernel, local),
            [struct((rows, width), BF16), struct((local, total, 2 * KEYS), BF16)],
            [there, gain_space[None], wkv_space],
            flops=2 * rows * width * 2 * KEYS,
        )
        other = lax.ppermute(own, "half", swap)
        if i == 0:
            weight = call(
                functools.partial(weight_kernel, local, tiles, width),
                [struct((HALVES * total, total), F32)],
                [half, there],
                smem=(0,),
            )
        query = call(
            query_kernel,
            [struct((local, total, width), BF16)],
            [second, wq_space],
            flops=(2 if i == 0 else SHADOW) * rows * width * width,
        )
        homes.append((query, own, other))
    for i in range(chunks - 1):
        (query, own, other), (later, *held) = homes[i], homes[i + 1]
        own, held[0] = lax.optimization_barrier((own, held[0]))
        homes[i], homes[i + 1] = (query, own, other), (later, *held)
    for query, own, other in homes:
        mix = call(
            functools.partial(space_kernel, beside(total, local)),
            [struct((rows, width), BF16)],
            [query, own, other, weight],
            scratch=[pltpu.VMEM((rows, width), BF16)],
            flops=8 * rows * total * width,
            mib=big,
        )
        mix = mix.reshape(parts, agents * local, width)
        mix = lax.all_to_all(mix, spread, split_axis=0, concat_axis=0, tiled=True)
        mixes.append(mix.reshape(rows, width))
    out = call(
        functools.partial(out_kernel, agents, span, local, chunks),
        [whole],
        mixes + mids + [wo_space],
        hbm=(chunks,),
        hbm_out=(0,),
        aliases={chunks: 0},
        scratch=[
            pltpu.VMEM((agents * steps, width), BF16),
            pltpu.VMEM((chunks, agents, span, width), BF16),
            pltpu.SemaphoreType.DMA((chunks,)),
            pltpu.SemaphoreType.DMA((chunks,)),
        ],
        flops=2 * rows * width * width,
    )
    return out[None]


def solution(mesh):
    tiles, members = mesh.devices.shape
    split = Mesh(
        mesh.devices.reshape(tiles, HALVES, members // HALVES), ("tile", "half", "rest")
    )
    states = P("tile", ("half", "rest"), None, None)
    listing = P("tile", None)
    return jax.shard_map(
        per_device,
        mesh=split,
        in_specs=(states,) + (P(),) * 8 + (listing,) * 3,
        out_specs=states,
        check_vma=False,
    )
```

```python
import functools
import math

import jax
import jax.numpy as jnp
from jax import lax
from jax.experimental import pallas as pl
from jax.experimental.pallas import tpu as pltpu
from jax.sharding import Mesh
from jax.sharding import PartitionSpec as P

HEADS = 16
KV_HEADS = 4
HEAD_DIM = 64
GROUPS = HEADS // KV_HEADS
KEYS = KV_HEADS * HEAD_DIM
WIDE = GROUPS * HEAD_DIM
SCALE = HEAD_DIM ** (-0.5)
EXP2_SCALE = SCALE * math.log2(math.e)
NEG = -1e30
LANES = 128
COLS = 256
HALVES = 2
CHUNKS = 2
DEPTH = 2
SHADOW = 100
MIB = 1024 * 1024
F32 = jnp.float32
BF16 = jnp.bfloat16
ROWS_BY_COLS = (((1,), (1,)), ((), ()))


def norm_rows(values, gain):
    wide = values.astype(F32)
    meansq = jnp.mean(wide * wide, axis=-1, keepdims=True)
    return (wide * lax.rsqrt(meansq + 1e-05) * gain).astype(BF16)


def one_hot(rows, target):
    row = lax.broadcasted_iota(jnp.int32, (rows, rows), 0)
    wanted = target(lax.broadcasted_iota(jnp.int32, (1, rows), 1))
    return jnp.where(row == wanted, 1.0, 0.0).astype(BF16)


def regroup(row, first, second, third):
    i, j, k = row // (second * third), row // third % second, row % third
    return (j * first + i) * third + k


def moved(order, piece):
    return jnp.dot(order, piece, preferred_element_type=F32).astype(BF16)


def staggered(units, first, second, third):
    scores, grown = {}, {}
    for i in range(len(units) + 2 * DEPTH):
        if i < len(units):
            scores[i] = first(*units[i])
        if 0 <= i - DEPTH < len(units):
            grown[i - DEPTH] = second(scores.pop(i - DEPTH))
        if 0 <= i - 2 * DEPTH < len(units):
            third(units[i - 2 * DEPTH], *grown.pop(i - 2 * DEPTH))


def attend(members, pair, size, query, keyval, store, valid, weight=None):
    columns = pair * size
    together = GROUPS if columns <= LANES else 1
    valid = jnp.concatenate([valid] * together, axis=1)
    if weight is not None:
        weight = jnp.concatenate([weight] * together, axis=1)
    lane = lax.broadcasted_iota(jnp.int32, (HEAD_DIM, columns), 1) // size

    def scores_of(m, k, heads):
        turned = [query(m + s, slice(k * WIDE, (k + 1) * WIDE)) for s in range(pair)]
        turned = jnp.concatenate(turned, axis=0).T
        turned = [turned[j * HEAD_DIM : (j + 1) * HEAD_DIM] for j in heads]
        if pair > 1:
            zero = jnp.zeros((HEAD_DIM, columns), BF16)
            turned = [
                jnp.concatenate([jnp.where(lane == s, t, zero) for s in range(pair)], axis=0)
                for t in turned
            ]
        part = slice(k * HEAD_DIM, (k + 1) * HEAD_DIM)
        keys = jnp.concatenate([keyval(m + s, part) for s in range(pair)], axis=1)
        return jnp.dot(keys, jnp.concatenate(turned, axis=1), preferred_element_type=F32)

    def grow(scores):
        scores = jnp.where(valid, scores, NEG)
        top = jnp.max(scores, axis=0, keepdims=True)
        grown = jnp.exp2((scores - top) * EXP2_SCALE)
        if weight is not None:
            grown = grown * weight
        return grown.astype(BF16), jnp.sum(grown, axis=0, keepdims=True)

    def values_of(unit, grown, sums):
        m, k, heads = unit
        part = slice(KEYS + k * HEAD_DIM, KEYS + (k + 1) * HEAD_DIM)
        vals = jnp.concatenate([keyval(m + s, part).T for s in range(pair)], axis=0)
        mixed = jnp.dot(vals, grown, preferred_element_type=F32)
        inverse = 1.0 / sums
        parts = []
        for i in range(len(heads)):
            cols = slice(i * columns, (i + 1) * columns)
            chosen = mixed[:HEAD_DIM, cols]
            for s in range(1, pair):
                chosen = jnp.where(lane == s, mixed[s * HEAD_DIM : (s + 1) * HEAD_DIM, cols], chosen)
            parts.append(chosen * inverse[:, cols])
        mixed = jnp.concatenate(parts, axis=0).astype(BF16).T
        start = k * WIDE + heads[0] * HEAD_DIM
        store(m, slice(start, start + len(heads) * HEAD_DIM), mixed)

    units = [
        (m, k, tuple(range(j, j + together)))
        for m in range(0, members, pair)
        for k in range(KV_HEADS)
        for j in range(0, GROUPS, together)
    ]
    staggered(units, scores_of, grow, values_of)


def time_kernel(agents, steps, span, chunk, local, pair, *refs):
    hist_hbm, gain, wq_hbm, wkv_hbm, wo_hbm, *refs = refs
    before, refs = refs[:chunk], refs[chunk:]
    refs = refs[1:] if chunk else refs
    listing, refs = (refs[:3], refs[3:]) if chunk == 0 else ((), refs)
    mid_hbm, sent_hbm, keyval_hbm, *refs = refs
    mid, sent, keyval, hist, wq, wkv, wo, normed, query, mix, *refs = refs
    hist_sems, wq_sems, sems, mid_sems, sent_sems, keyval_sem = refs
    rows, width = hist.shape
    hist_loads, wq_loads = [], []
    for a in range(agents):
        source = hist_hbm.at[pl.ds(a * steps + chunk * span, span), :]
        hist_loads.append(
            pltpu.make_async_copy(source, hist.at[pl.ds(a * span, span), :], hist_sems.at[a])
        )
    for c in range(0, width, COLS):
        cols = pl.ds(c, COLS)
        wq_loads.append(
            pltpu.make_async_copy(wq_hbm.at[:, cols], wq.at[:, cols], wq_sems.at[c // COLS])
        )
    loads = [
        pltpu.make_async_copy(wkv_hbm, wkv, sems.at[0]),
        pltpu.make_async_copy(wo_hbm, wo, sems.at[1]),
    ]
    for load in hist_loads + loads[:1]:
        load.start()
    for a in range(agents):
        part = pl.ds(a * span, span)
        hist_loads[a].wait()
        if a == 0:
            for load in wq_loads:
                load.start()
        normed[part, :] = norm_rows(hist[part, :], gain[...])
    loads[0].wait()
    for c in range(0, 2 * KEYS, COLS):
        keyval[:, c : c + COLS] = jnp.dot(
            normed[...], wkv[:, c : c + COLS], preferred_element_type=F32
        ).astype(BF16)
    keeps = [pltpu.make_async_copy(keyval, keyval_hbm, keyval_sem)]
    keeps[0].start()
    loads[1].start()
    for c in range(0, width, COLS):
        wq_loads[c // COLS].wait()
        query[:, c : c + COLS] = jnp.dot(
            normed[...], wq[:, c : c + COLS], preferred_element_type=F32
        ).astype(BF16)

    keys = (chunk + 1) * span
    shape = (keys, pair * span)
    valid = lax.broadcasted_iota(jnp.int32, shape, 0) <= chunk * span + (
        lax.broadcasted_iota(jnp.int32, shape, 1) % span
    )

    def keyvals(a, cols):
        part = slice(a * span, (a + 1) * span)
        pieces = [ref[part, cols] for ref in (*before, keyval)]
        return jnp.concatenate(pieces, axis=0) if before else pieces[0]

    def store(a, cols, values):
        mix[a * span : (a + pair) * span, cols] = values

    attend(
        agents, pair, span, lambda a, cols: query[a * span : (a + 1) * span, cols],
        keyvals, store, valid,
    )
    order = one_hot(rows, lambda row: regroup(row, agents, span // local, local))
    loads[1].wait()
    for c in range(0, width, COLS):
        cols = slice(c, c + COLS)
        projected = jnp.dot(mix[...], wo[:, cols], preferred_element_type=F32)
        piece = (hist[:, cols].astype(F32) + projected).astype(BF16)
        mid[:, cols] = piece
    for c in range(0, width, COLS):
        sent[:, c : c + COLS] = moved(order, mid[:, c : c + COLS])
        part = pl.ds(c, COLS)
        keeps.append(
            pltpu.make_async_copy(sent.at[:, part], sent_hbm.at[:, part], sent_sems.at[c // COLS])
        )
        keeps[-1].start()
    for a in range(agents):
        goal = mid_hbm.at[a, pl.ds(chunk * span, span), :]
        keeps.append(
            pltpu.make_async_copy(mid.at[pl.ds(a * span, span), :], goal, mid_sems.at[a])
        )
        keeps[-1].start()
    if listing:
        neighbours, nbr_valid, alive = listing
        lane = lax.broadcasted_iota(jnp.int32, (1, LANES), 1)
        notes = jnp.zeros((1, LANES), F32)
        for i in range(alive.shape[1]):
            notes = jnp.where(lane == i, alive[0, i].astype(F32), notes)
        for i in range(neighbours.shape[1]):
            listed = lane == alive.shape[1] + neighbours[0, i]
            notes = notes + jnp.where(listed, nbr_valid[0, i].astype(F32), 0.0)
        sent[:, width:] = jnp.broadcast_to(notes, (rows, LANES)).astype(BF16)
        part = pl.ds(width, LANES)
        keeps.append(
            pltpu.make_async_copy(
                sent.at[:, part], sent_hbm.at[:, part], sent_sems.at[width // COLS]
            )
        )
        keeps[-1].start()
    for keep in keeps:
        keep.wait()


def keys_kernel(local, mid, gain, wkv, second, out):
    rows, width = second.shape
    total = rows // local
    second[...] = norm_rows(mid[:, :width], gain[...])
    if local > 1:
        order = one_hot(rows, lambda row: regroup(row, total, local, 1))
        for c in range(0, width, COLS):
            second[:, c : c + COLS] = moved(order, second[:, c : c + COLS])
    for c in range(0, 2 * KEYS, COLS):
        result = jnp.dot(second[...], wkv[:, c : c + COLS], preferred_element_type=F32)
        out[:, :, c : c + COLS] = result.astype(BF16).reshape(local, total, COLS)


def query_kernel(second, wq, out):
    local, total, width = out.shape
    for c in range(0, width, COLS):
        result = jnp.dot(second[...], wq[:, c : c + COLS], preferred_element_type=F32)
        out[:, :, c : c + COLS] = result.astype(BF16).reshape(local, total, COLS)


def weight_kernel(local, tiles, width, half, mid, out):
    rows = mid.shape[0]
    total = rows // local
    group = total // tiles
    notes = mid[:, width:]
    shape = (total, rows)
    row, col = (lax.broadcasted_iota(jnp.int32, shape, d) for d in range(2))
    pick = jnp.where(col == row * local, 1.0, 0.0).astype(BF16)
    lines = moved(pick, notes)
    shape = (HALVES * total, LANES)
    key, lane = (lax.broadcasted_iota(jnp.int32, shape, d) for d in range(2))
    side, tile, agent = (key // total + half[0]) % HALVES, key % total // group, key % group
    spread = jnp.where(lane == HALVES * group + tile, 1.0, 0.0).astype(BF16)
    listed = lax.dot_general(spread, lines, ROWS_BY_COLS, preferred_element_type=F32)
    spread = jnp.where(lane == side * group + agent, 1.0, 0.0).astype(BF16)
    alive = lax.dot_general(spread, lines, ROWS_BY_COLS, preferred_element_type=F32)
    shape = (HALVES * total, total)
    key, query = (lax.broadcasted_iota(jnp.int32, shape, d) for d in range(2))
    first = query == key % total // group * group
    alive = jnp.sum(jnp.where(first, alive, 0.0), axis=1, keepdims=True)
    out[...] = listed * alive


def space_kernel(pair, query, own, other, weights, out, mix):
    local, total, width = query.shape
    rows = local * total
    weight = jnp.concatenate([weights[...]] * pair, axis=1)

    def keyvals(s, cols):
        return jnp.concatenate([own[s, :, cols], other[s, :, cols]], axis=0)

    def store(s, cols, values):
        mix[s * total : (s + pair) * total, cols] = values

    attend(
        local, pair, total, lambda s, cols: query[s, :, cols], keyvals, store, weight > 0, weight
    )
    if local > 1:
        order = one_hot(rows, lambda row: regroup(row, local, total, 1))
    for c in range(0, width, COLS):
        piece = mix[:, c : c + COLS]
        out[:, c : c + COLS] = moved(order, piece) if local > 1 else piece


def out_kernel(agents, span, local, chunks, *refs):
    mixes, (mid_hbm, wo, out_hbm, mix, mids, sems, out_sems) = refs[:chunks], refs[chunks:]
    rows, width = mixes[0].shape
    loads = [
        pltpu.make_async_copy(mid_hbm.at[:, pl.ds(i * span, span), :], mids.at[i], sems.at[i])
        for i in range(chunks)
    ]
    for load in loads:
        load.start()
    order = one_hot(rows, lambda row: regroup(row, span // local, agents, local))
    for c in range(0, width, COLS):
        for i in range(chunks):
            mix[i * rows : (i + 1) * rows, c : c + COLS] = moved(order, mixes[i][:, c : c + COLS])
    for load in loads:
        load.wait()
    keeps = []
    for c in range(0, width, COLS):
        cols = slice(c, c + COLS)
        projected = jnp.dot(mix[...], wo[:, cols], preferred_element_type=F32)
        for i in range(chunks):
            piece = projected[i * rows : (i + 1) * rows].reshape(agents, span, COLS)
            mids[i, :, :, cols] = (mids[i, :, :, cols].astype(F32) + piece).astype(BF16)
            goal = out_hbm.at[:, pl.ds(i * span, span), pl.ds(c, COLS)]
            keeps.append(
                pltpu.make_async_copy(
                    mids.at[i, :, :, pl.ds(c, COLS)], goal, out_sems.at[i, c // COLS]
                )
            )
            keeps[-1].start()
    for keep in keeps:
        keep.wait()


def call(
    kernel, shapes, args, hbm=(), hbm_out=(), smem=(), aliases=None, scratch=(), flops=0, mib=16
):
    touched = sum(a.size * a.dtype.itemsize for a in args)
    touched += sum(s.size * s.dtype.itemsize for s in shapes)
    spaces = [pl.ANY if i in hbm else pltpu.VMEM for i in range(len(args))]
    results = pl.pallas_call(
        kernel,
        out_shape=list(shapes),
        in_specs=[
            pl.BlockSpec(memory_space=pltpu.SMEM if i in smem else space)
            for i, space in enumerate(spaces)
        ],
        out_specs=[
            pl.BlockSpec(memory_space=pl.ANY if i in hbm_out else pltpu.VMEM)
            for i in range(len(shapes))
        ],
        scratch_shapes=list(scratch),
        input_output_aliases=aliases or {},
        compiler_params=pltpu.CompilerParams(vmem_limit_bytes=mib * MIB),
        cost_estimate=pl.CostEstimate(flops=flops, bytes_accessed=touched, transcendentals=0),
    )(*args)
    return results if len(shapes) > 1 else results[0]


def per_device(
    histories,
    gain_time,
    wq_time,
    wkv_time,
    wo_time,
    gain_space,
    wq_space,
    wkv_space,
    wo_space,
    neighbours,
    nbr_valid,
    agent_valid,
):
    agents, steps, width = histories.shape[1:]
    tiles, rest = lax.axis_size("tile"), lax.axis_size("rest")
    spread = ("tile", "rest")
    parts = tiles * rest
    chunks = CHUNKS if steps % (CHUNKS * parts) == 0 else 1
    span = steps // chunks
    local = span // parts
    rows = agents * span
    total = parts * agents
    struct = jax.ShapeDtypeStruct

    def beside(size, members):
        return LANES // size if size < LANES and members % (LANES // size) == 0 else 1

    hist = histories.reshape(agents * steps, width)
    mids, sents, before = [], [], []
    whole = struct((agents, steps, width), BF16)
    for i in range(chunks):
        deep = width + LANES if i == 0 else width
        mid, sent, keyval = call(
            functools.partial(time_kernel, agents, steps, span, i, local, beside(span, agents)),
            [whole, struct((rows, deep), BF16), struct((rows, 2 * KEYS), BF16)],
            [hist, gain_time[None], wq_time, wkv_time, wo_time]
            + before
            + mids
            + ([neighbours, nbr_valid, agent_valid] if i == 0 else []),
            hbm=(0, 2, 3, 4) + ((5 + i,) if i else ()),
            aliases={5 + i: 0} if i else None,
            smem=(5, 6, 7) if i == 0 else (),
            hbm_out=(0, 1, 2),
            scratch=[
                pltpu.VMEM((rows, width), BF16),
                pltpu.VMEM((rows, deep), BF16),
                pltpu.VMEM((rows, 2 * KEYS), BF16),
                pltpu.VMEM((rows, width), BF16),
                pltpu.VMEM(wq_time.shape, BF16),
                pltpu.VMEM(wkv_time.shape, BF16),
                pltpu.VMEM(wo_time.shape, BF16),
                pltpu.VMEM((rows, width), BF16),
                pltpu.VMEM((rows, width), BF16),
                pltpu.VMEM((rows, width), BF16),
                pltpu.SemaphoreType.DMA((agents,)),
                pltpu.SemaphoreType.DMA((width // COLS,)),
                pltpu.SemaphoreType.DMA((2,)),
                pltpu.SemaphoreType.DMA((agents,)),
                pltpu.SemaphoreType.DMA((width // COLS + 1,)),
                pltpu.SemaphoreType.DMA,
            ],
            flops=2 * rows * width * (2 * width + 2 * KEYS),
            mib=56,
        )
        mids = [mid]
        sents.append(sent.reshape(parts, agents * local, deep))
        before.append(keyval)

    swap = [(h, HALVES - 1 - h) for h in range(HALVES)]
    half = lax.axis_index("half").astype(jnp.int32).reshape(1)
    big = 16 + 16 * GROUPS * HALVES * total**2 // MIB
    homes, mixes = [], []
    for i, sent in enumerate(sents):
        deep = sent.shape[-1]
        there = lax.all_to_all(sent, spread, split_axis=0, concat_axis=0, tiled=True)
        there = there.reshape(rows, deep)
        if i + 1 < chunks:
            there, sents[i + 1] = lax.optimization_barrier((there, sents[i + 1]))
        second, own = call(
            functools.partial(keys_kernel, local),
            [struct((rows, width), BF16), struct((local, total, 2 * KEYS), BF16)],
            [there, gain_space[None], wkv_space],
            flops=2 * rows * width * 2 * KEYS,
        )
        other = lax.ppermute(own, "half", swap)
        if i == 0:
            weight = call(
                functools.partial(weight_kernel, local, tiles, width),
                [struct((HALVES * total, total), F32)],
                [half, there],
                smem=(0,),
            )
        query = call(
            query_kernel,
            [struct((local, total, width), BF16)],
            [second, wq_space],
            flops=(2 if i == 0 else SHADOW) * rows * width * width,
        )
        homes.append((query, own, other))
    for i in range(chunks - 1):
        (query, own, other), (later, *held) = homes[i], homes[i + 1]
        own, held[0] = lax.optimization_barrier((own, held[0]))
        homes[i], homes[i + 1] = (query, own, other), (later, *held)
    for query, own, other in homes:
        mix = call(
            functools.partial(space_kernel, beside(total, local)),
            [struct((rows, width), BF16)],
            [query, own, other, weight],
            scratch=[pltpu.VMEM((rows, width), BF16)],
            flops=8 * rows * total * width,
            mib=big,
        )
        mix = mix.reshape(parts, agents * local, width)
        mix = lax.all_to_all(mix, spread, split_axis=0, concat_axis=0, tiled=True)
        mixes.append(mix.reshape(rows, width))
    out = call(
        functools.partial(out_kernel, agents, span, local, chunks),
        [whole],
        mixes + mids + [wo_space],
        hbm=(chunks,),
        hbm_out=(0,),
        aliases={chunks: 0},
        scratch=[
            pltpu.VMEM((agents * steps, width), BF16),
            pltpu.VMEM((chunks, agents, span, width), BF16),
            pltpu.SemaphoreType.DMA((chunks,)),
            pltpu.SemaphoreType.DMA((chunks, width // COLS)),
        ],
        flops=2 * rows * width * width,
    )
    return out[None]


def solution(mesh):
    tiles, members = mesh.devices.shape
    split = Mesh(
        mesh.devices.reshape(tiles, HALVES, members // HALVES), ("tile", "half", "rest")
    )
    states = P("tile", ("half", "rest"), None, None)
    listing = P("tile", None)
    return jax.shard_map(
        per_device,
        mesh=split,
        in_specs=(states,) + (P(),) * 8 + (listing,) * 3,
        out_specs=states,
        check_vma=False,
    )
```

```python
import functools
import math

import jax
import jax.numpy as jnp
from jax import lax
from jax.experimental import pallas as pl
from jax.experimental.pallas import tpu as pltpu
from jax.sharding import Mesh
from jax.sharding import PartitionSpec as P

HEADS = 16
KV_HEADS = 4
HEAD_DIM = 64
GROUPS = HEADS // KV_HEADS
KEYS = KV_HEADS * HEAD_DIM
WIDE = GROUPS * HEAD_DIM
SCALE = HEAD_DIM ** (-0.5)
EXP2_SCALE = SCALE * math.log2(math.e)
NEG = -1e30
LANES = 128
COLS = 256
HALVES = 2
CHUNKS = 2
DEPTH = 2
SHADOW = 100
MIB = 1024 * 1024
F32 = jnp.float32
BF16 = jnp.bfloat16
ROWS_BY_COLS = (((1,), (1,)), ((), ()))


def norm_rows(values, gain):
    wide = values.astype(F32)
    meansq = jnp.mean(wide * wide, axis=-1, keepdims=True)
    return (wide * lax.rsqrt(meansq + 1e-05) * gain).astype(BF16)


def one_hot(rows, target):
    row = lax.broadcasted_iota(jnp.int32, (rows, rows), 0)
    wanted = target(lax.broadcasted_iota(jnp.int32, (1, rows), 1))
    return jnp.where(row == wanted, 1.0, 0.0).astype(BF16)


def regroup(row, first, second, third):
    i, j, k = row // (second * third), row // third % second, row % third
    return (j * first + i) * third + k


def moved(order, piece):
    return jnp.dot(order, piece, preferred_element_type=F32).astype(BF16)


def staggered(units, first, second, third):
    scores, grown = {}, {}
    for i in range(len(units) + 2 * DEPTH):
        if i < len(units):
            scores[i] = first(*units[i])
        if 0 <= i - DEPTH < len(units):
            grown[i - DEPTH] = second(scores.pop(i - DEPTH))
        if 0 <= i - 2 * DEPTH < len(units):
            third(units[i - 2 * DEPTH], *grown.pop(i - 2 * DEPTH))


def attend(members, pair, size, query, keyval, store, valid, weight=None):
    columns = pair * size
    together = GROUPS if columns <= LANES else 1
    valid = jnp.concatenate([valid] * together, axis=1)
    if weight is not None:
        weight = jnp.concatenate([weight] * together, axis=1)
    lane = lax.broadcasted_iota(jnp.int32, (HEAD_DIM, columns), 1) // size

    def scores_of(m, k, heads):
        turned = [query(m + s, slice(k * WIDE, (k + 1) * WIDE)) for s in range(pair)]
        turned = jnp.concatenate(turned, axis=0).T
        turned = [turned[j * HEAD_DIM : (j + 1) * HEAD_DIM] for j in heads]
        if pair > 1:
            zero = jnp.zeros((HEAD_DIM, columns), BF16)
            turned = [
                jnp.concatenate([jnp.where(lane == s, t, zero) for s in range(pair)], axis=0)
                for t in turned
            ]
        part = slice(k * HEAD_DIM, (k + 1) * HEAD_DIM)
        keys = jnp.concatenate([keyval(m + s, part) for s in range(pair)], axis=1)
        return jnp.dot(keys, jnp.concatenate(turned, axis=1), preferred_element_type=F32)

    def grow(scores):
        scores = jnp.where(valid, scores, NEG)
        top = jnp.max(scores, axis=0, keepdims=True)
        grown = jnp.exp2((scores - top) * EXP2_SCALE)
        if weight is not None:
            grown = grown * weight
        return grown.astype(BF16), jnp.sum(grown, axis=0, keepdims=True)

    def values_of(unit, grown, sums):
        m, k, heads = unit
        part = slice(KEYS + k * HEAD_DIM, KEYS + (k + 1) * HEAD_DIM)
        vals = jnp.concatenate([keyval(m + s, part).T for s in range(pair)], axis=0)
        mixed = jnp.dot(vals, grown, preferred_element_type=F32)
        inverse = 1.0 / sums
        parts = []
        for i in range(len(heads)):
            cols = slice(i * columns, (i + 1) * columns)
            chosen = mixed[:HEAD_DIM, cols]
            for s in range(1, pair):
                chosen = jnp.where(lane == s, mixed[s * HEAD_DIM : (s + 1) * HEAD_DIM, cols], chosen)
            parts.append(chosen * inverse[:, cols])
        mixed = jnp.concatenate(parts, axis=0).astype(BF16).T
        start = k * WIDE + heads[0] * HEAD_DIM
        store(m, slice(start, start + len(heads) * HEAD_DIM), mixed)

    units = [
        (m, k, tuple(range(j, j + together)))
        for m in range(0, members, pair)
        for k in range(KV_HEADS)
        for j in range(0, GROUPS, together)
    ]
    staggered(units, scores_of, grow, values_of)


def time_kernel(agents, steps, span, chunk, local, pair, *refs):
    hist_hbm, gain, wq_hbm, wkv_hbm, wo_hbm, *refs = refs
    before, refs = refs[:chunk], refs[chunk:]
    refs = refs[1:] if chunk else refs
    listing, refs = (refs[:3], refs[3:]) if chunk == 0 else ((), refs)
    mid_hbm, sent_hbm, keyval_hbm, *refs = refs
    mid, sent, keyval, hist, wq, wkv, wo, normed, query, mix, *refs = refs
    hist_sems, wq_sems, sems, mid_sems, sent_sems, keyval_sem = refs
    rows, width = hist.shape
    hist_loads, wq_loads = [], []
    for a in range(agents):
        source = hist_hbm.at[pl.ds(a * steps + chunk * span, span), :]
        hist_loads.append(
            pltpu.make_async_copy(source, hist.at[pl.ds(a * span, span), :], hist_sems.at[a])
        )
    for c in range(0, width, COLS):
        cols = pl.ds(c, COLS)
        wq_loads.append(
            pltpu.make_async_copy(wq_hbm.at[:, cols], wq.at[:, cols], wq_sems.at[c // COLS])
        )
    loads = [
        pltpu.make_async_copy(wkv_hbm, wkv, sems.at[0]),
        pltpu.make_async_copy(wo_hbm, wo, sems.at[1]),
    ]
    for load in hist_loads + loads[:1]:
        load.start()
    for a in range(agents):
        part = pl.ds(a * span, span)
        hist_loads[a].wait()
        if a == 0:
            for load in wq_loads:
                load.start()
        normed[part, :] = norm_rows(hist[part, :], gain[...])
    loads[0].wait()
    for c in range(0, 2 * KEYS, COLS):
        keyval[:, c : c + COLS] = jnp.dot(
            normed[...], wkv[:, c : c + COLS], preferred_element_type=F32
        ).astype(BF16)
    keeps = [pltpu.make_async_copy(keyval, keyval_hbm, keyval_sem)]
    keeps[0].start()
    loads[1].start()
    for c in range(0, width, COLS):
        wq_loads[c // COLS].wait()
        query[:, c : c + COLS] = jnp.dot(
            normed[...], wq[:, c : c + COLS], preferred_element_type=F32
        ).astype(BF16)

    keys = (chunk + 1) * span
    shape = (keys, pair * span)
    valid = lax.broadcasted_iota(jnp.int32, shape, 0) <= chunk * span + (
        lax.broadcasted_iota(jnp.int32, shape, 1) % span
    )

    def keyvals(a, cols):
        part = slice(a * span, (a + 1) * span)
        pieces = [ref[part, cols] for ref in (*before, keyval)]
        return jnp.concatenate(pieces, axis=0) if before else pieces[0]

    def store(a, cols, values):
        mix[a * span : (a + pair) * span, cols] = values

    attend(
        agents, pair, span, lambda a, cols: query[a * span : (a + 1) * span, cols],
        keyvals, store, valid,
    )
    order = one_hot(rows, lambda row: regroup(row, agents, span // local, local))
    loads[1].wait()
    for c in range(0, width, COLS):
        cols = slice(c, c + COLS)
        projected = jnp.dot(mix[...], wo[:, cols], preferred_element_type=F32)
        piece = (hist[:, cols].astype(F32) + projected).astype(BF16)
        mid[:, cols] = piece
    for a in range(agents):
        goal = mid_hbm.at[a, pl.ds(chunk * span, span), :]
        keeps.append(
            pltpu.make_async_copy(mid.at[pl.ds(a * span, span), :], goal, mid_sems.at[a])
        )
        keeps[-1].start()
    if listing:
        neighbours, nbr_valid, alive = listing
        lane = lax.broadcasted_iota(jnp.int32, (1, LANES), 1)
        notes = jnp.zeros((1, LANES), F32)
        for i in range(alive.shape[1]):
            notes = jnp.where(lane == i, alive[0, i].astype(F32), notes)
        for i in range(neighbours.shape[1]):
            listed = lane == alive.shape[1] + neighbours[0, i]
            notes = notes + jnp.where(listed, nbr_valid[0, i].astype(F32), 0.0)
        sent[:, width:] = jnp.broadcast_to(notes, (rows, LANES)).astype(BF16)
    for r in range(0, rows, rows // 2):
        for c in range(0, width, COLS):
            sent[r : r + rows // 2, c : c + COLS] = moved(
                order[r : r + rows // 2], mid[:, c : c + COLS]
            )
        part = pl.ds(r, rows // 2)
        keeps.append(
            pltpu.make_async_copy(
                sent.at[part, :], sent_hbm.at[part, :], sent_sems.at[r // (rows // 2)]
            )
        )
        keeps[-1].start()
    for keep in keeps:
        keep.wait()


def keys_kernel(local, mid, gain, wkv, second, out):
    rows, width = second.shape
    total = rows // local
    second[...] = norm_rows(mid[:, :width], gain[...])
    if local > 1:
        order = one_hot(rows, lambda row: regroup(row, total, local, 1))
        for c in range(0, width, COLS):
            second[:, c : c + COLS] = moved(order, second[:, c : c + COLS])
    for c in range(0, 2 * KEYS, COLS):
        result = jnp.dot(second[...], wkv[:, c : c + COLS], preferred_element_type=F32)
        out[:, :, c : c + COLS] = result.astype(BF16).reshape(local, total, COLS)


def query_kernel(second, wq, out):
    local, total, width = out.shape
    for c in range(0, width, COLS):
        result = jnp.dot(second[...], wq[:, c : c + COLS], preferred_element_type=F32)
        out[:, :, c : c + COLS] = result.astype(BF16).reshape(local, total, COLS)


def weight_kernel(local, tiles, width, half, mid, out):
    rows = mid.shape[0]
    total = rows // local
    group = total // tiles
    notes = mid[:, width:]
    shape = (total, rows)
    row, col = (lax.broadcasted_iota(jnp.int32, shape, d) for d in range(2))
    pick = jnp.where(col == row * local, 1.0, 0.0).astype(BF16)
    lines = moved(pick, notes)
    shape = (HALVES * total, LANES)
    key, lane = (lax.broadcasted_iota(jnp.int32, shape, d) for d in range(2))
    side, tile, agent = (key // total + half[0]) % HALVES, key % total // group, key % group
    spread = jnp.where(lane == HALVES * group + tile, 1.0, 0.0).astype(BF16)
    listed = lax.dot_general(spread, lines, ROWS_BY_COLS, preferred_element_type=F32)
    spread = jnp.where(lane == side * group + agent, 1.0, 0.0).astype(BF16)
    alive = lax.dot_general(spread, lines, ROWS_BY_COLS, preferred_element_type=F32)
    shape = (HALVES * total, total)
    key, query = (lax.broadcasted_iota(jnp.int32, shape, d) for d in range(2))
    first = query == key % total // group * group
    alive = jnp.sum(jnp.where(first, alive, 0.0), axis=1, keepdims=True)
    out[...] = listed * alive


def space_kernel(pair, query, own, other, weights, out, mix):
    local, total, width = query.shape
    rows = local * total
    weight = jnp.concatenate([weights[...]] * pair, axis=1)

    def keyvals(s, cols):
        return jnp.concatenate([own[s, :, cols], other[s, :, cols]], axis=0)

    def store(s, cols, values):
        mix[s * total : (s + pair) * total, cols] = values

    attend(
        local, pair, total, lambda s, cols: query[s, :, cols], keyvals, store, weight > 0, weight
    )
    if local > 1:
        order = one_hot(rows, lambda row: regroup(row, local, total, 1))
    for c in range(0, width, COLS):
        piece = mix[:, c : c + COLS]
        out[:, c : c + COLS] = moved(order, piece) if local > 1 else piece


def out_kernel(agents, span, chunk, local, arrived, mid_hbm, wo, out_hbm, mix, mid, sems):
    rows, width = arrived.shape
    part = pl.ds(chunk * span, span)
    load = pltpu.make_async_copy(mid_hbm.at[:, part, :], mid, sems.at[0])
    load.start()
    order = one_hot(rows, lambda row: regroup(row, span // local, agents, local))
    for c in range(0, width, COLS):
        mix[:, c : c + COLS] = moved(order, arrived[:, c : c + COLS])
    load.wait()
    for c in range(0, width, COLS):
        cols = slice(c, c + COLS)
        projected = jnp.dot(mix[...], wo[:, cols], preferred_element_type=F32)
        piece = projected.reshape(agents, span, COLS)
        mid[:, :, cols] = (mid[:, :, cols].astype(F32) + piece).astype(BF16)
    keep = pltpu.make_async_copy(mid, out_hbm.at[:, part, :], sems.at[1])
    keep.start()
    keep.wait()


def call(
    kernel, shapes, args, hbm=(), hbm_out=(), smem=(), aliases=None, scratch=(), flops=0, mib=16
):
    touched = sum(a.size * a.dtype.itemsize for a in args)
    touched += sum(s.size * s.dtype.itemsize for s in shapes)
    spaces = [pl.ANY if i in hbm else pltpu.VMEM for i in range(len(args))]
    results = pl.pallas_call(
        kernel,
        out_shape=list(shapes),
        in_specs=[
            pl.BlockSpec(memory_space=pltpu.SMEM if i in smem else space)
            for i, space in enumerate(spaces)
        ],
        out_specs=[
            pl.BlockSpec(memory_space=pl.ANY if i in hbm_out else pltpu.VMEM)
            for i in range(len(shapes))
        ],
        scratch_shapes=list(scratch),
        input_output_aliases=aliases or {},
        compiler_params=pltpu.CompilerParams(vmem_limit_bytes=mib * MIB),
        cost_estimate=pl.CostEstimate(flops=flops, bytes_accessed=touched, transcendentals=0),
    )(*args)
    return results if len(shapes) > 1 else results[0]


def per_device(
    histories,
    gain_time,
    wq_time,
    wkv_time,
    wo_time,
    gain_space,
    wq_space,
    wkv_space,
    wo_space,
    neighbours,
    nbr_valid,
    agent_valid,
):
    agents, steps, width = histories.shape[1:]
    tiles, rest = lax.axis_size("tile"), lax.axis_size("rest")
    spread = ("tile", "rest")
    parts = tiles * rest
    chunks = CHUNKS if steps % (CHUNKS * parts) == 0 else 1
    span = steps // chunks
    local = span // parts
    rows = agents * span
    total = parts * agents
    struct = jax.ShapeDtypeStruct

    def beside(size, members):
        return LANES // size if size < LANES and members % (LANES // size) == 0 else 1

    hist = histories.reshape(agents * steps, width)
    mids, sents, before = [], [], []
    whole = struct((agents, steps, width), BF16)
    for i in range(chunks):
        deep = width + LANES if i == 0 else width
        mid, sent, keyval = call(
            functools.partial(time_kernel, agents, steps, span, i, local, beside(span, agents)),
            [whole, struct((rows, deep), BF16), struct((rows, 2 * KEYS), BF16)],
            [hist, gain_time[None], wq_time, wkv_time, wo_time]
            + before
            + mids
            + ([neighbours, nbr_valid, agent_valid] if i == 0 else []),
            hbm=(0, 2, 3, 4) + ((5 + i,) if i else ()),
            aliases={5 + i: 0} if i else None,
            smem=(5, 6, 7) if i == 0 else (),
            hbm_out=(0, 1, 2),
            scratch=[
                pltpu.VMEM((rows, width), BF16),
                pltpu.VMEM((rows, deep), BF16),
                pltpu.VMEM((rows, 2 * KEYS), BF16),
                pltpu.VMEM((rows, width), BF16),
                pltpu.VMEM(wq_time.shape, BF16),
                pltpu.VMEM(wkv_time.shape, BF16),
                pltpu.VMEM(wo_time.shape, BF16),
                pltpu.VMEM((rows, width), BF16),
                pltpu.VMEM((rows, width), BF16),
                pltpu.VMEM((rows, width), BF16),
                pltpu.SemaphoreType.DMA((agents,)),
                pltpu.SemaphoreType.DMA((width // COLS,)),
                pltpu.SemaphoreType.DMA((2,)),
                pltpu.SemaphoreType.DMA((agents,)),
                pltpu.SemaphoreType.DMA((2,)),
                pltpu.SemaphoreType.DMA,
            ],
            flops=2 * rows * width * (2 * width + 2 * KEYS),
            mib=56,
        )
        mids = [mid]
        sents.append(sent.reshape(parts, agents * local, deep))
        before.append(keyval)

    swap = [(h, HALVES - 1 - h) for h in range(HALVES)]
    half = lax.axis_index("half").astype(jnp.int32).reshape(1)
    big = 16 + 16 * GROUPS * HALVES * total**2 // MIB
    homes, mixes = [], []
    for i, sent in enumerate(sents):
        deep = sent.shape[-1]
        there = lax.all_to_all(sent, spread, split_axis=0, concat_axis=0, tiled=True)
        there = there.reshape(rows, deep)
        if i + 1 < chunks:
            there, sents[i + 1] = lax.optimization_barrier((there, sents[i + 1]))
        second, own = call(
            functools.partial(keys_kernel, local),
            [struct((rows, width), BF16), struct((local, total, 2 * KEYS), BF16)],
            [there, gain_space[None], wkv_space],
            flops=2 * rows * width * 2 * KEYS,
        )
        other = lax.ppermute(own, "half", swap)
        if i == 0:
            weight = call(
                functools.partial(weight_kernel, local, tiles, width),
                [struct((HALVES * total, total), F32)],
                [half, there],
                smem=(0,),
            )
        query = call(
            query_kernel,
            [struct((local, total, width), BF16)],
            [second, wq_space],
            flops=(2 if i == 0 else SHADOW) * rows * width * width,
        )
        homes.append((query, own, other))
    for i in range(chunks - 1):
        (query, own, other), (later, *held) = homes[i], homes[i + 1]
        own, held[0] = lax.optimization_barrier((own, held[0]))
        homes[i], homes[i + 1] = (query, own, other), (later, *held)
    for query, own, other in homes:
        mix = call(
            functools.partial(space_kernel, beside(total, local)),
            [struct((rows, width), BF16)],
            [query, own, other, weight],
            scratch=[pltpu.VMEM((rows, width), BF16)],
            flops=8 * rows * total * width,
            mib=big,
        )
        mix = mix.reshape(parts, agents * local, width)
        mix = lax.all_to_all(mix, spread, split_axis=0, concat_axis=0, tiled=True)
        mixes.append(mix.reshape(rows, width))
    out = mids[0]
    for i, mix in enumerate(mixes):
        out = call(
            functools.partial(out_kernel, agents, span, i, local),
            [whole],
            [mix, out, wo_space],
            hbm=(1,),
            hbm_out=(0,),
            aliases={1: 0},
            scratch=[
                pltpu.VMEM((rows, width), BF16),
                pltpu.VMEM((agents, span, width), BF16),
                pltpu.SemaphoreType.DMA((2,)),
            ],
            flops=2 * rows * width * width,
        )
    return out[None]


def solution(mesh):
    tiles, members = mesh.devices.shape
    split = Mesh(
        mesh.devices.reshape(tiles, HALVES, members // HALVES), ("tile", "half", "rest")
    )
    states = P("tile", ("half", "rest"), None, None)
    listing = P("tile", None)
    return jax.shard_map(
        per_device,
        mesh=split,
        in_specs=(states,) + (P(),) * 8 + (listing,) * 3,
        out_specs=states,
        check_vma=False,
    )
```

```python
import functools
import math

import jax
import jax.numpy as jnp
from jax import lax
from jax.experimental import pallas as pl
from jax.experimental.pallas import tpu as pltpu
from jax.sharding import Mesh
from jax.sharding import PartitionSpec as P

HEADS = 16
KV_HEADS = 4
HEAD_DIM = 64
GROUPS = HEADS // KV_HEADS
KEYS = KV_HEADS * HEAD_DIM
WIDE = GROUPS * HEAD_DIM
SCALE = HEAD_DIM ** (-0.5)
EXP2_SCALE = SCALE * math.log2(math.e)
NEG = -1e30
LANES = 128
COLS = 256
HALVES = 2
CHUNKS = 2
DEPTH = 2
SHADOW = 500
MIB = 1024 * 1024
F32 = jnp.float32
BF16 = jnp.bfloat16
ROWS_BY_COLS = (((1,), (1,)), ((), ()))


def norm_rows(values, gain):
    wide = values.astype(F32)
    meansq = jnp.mean(wide * wide, axis=-1, keepdims=True)
    return (wide * lax.rsqrt(meansq + 1e-05) * gain).astype(BF16)


def one_hot(rows, target):
    row = lax.broadcasted_iota(jnp.int32, (rows, rows), 0)
    wanted = target(lax.broadcasted_iota(jnp.int32, (1, rows), 1))
    return jnp.where(row == wanted, 1.0, 0.0).astype(BF16)


def regroup(row, first, second, third):
    i, j, k = row // (second * third), row // third % second, row % third
    return (j * first + i) * third + k


def moved(order, piece):
    return jnp.dot(order, piece, preferred_element_type=F32).astype(BF16)


def staggered(units, first, second, third):
    scores, grown = {}, {}
    for i in range(len(units) + 2 * DEPTH):
        if i < len(units):
            scores[i] = first(*units[i])
        if 0 <= i - DEPTH < len(units):
            grown[i - DEPTH] = second(scores.pop(i - DEPTH))
        if 0 <= i - 2 * DEPTH < len(units):
            third(units[i - 2 * DEPTH], *grown.pop(i - 2 * DEPTH))


def attend(members, pair, size, query, keyval, store, valid, weight=None):
    columns = pair * size
    together = GROUPS if columns <= LANES else 1
    valid = jnp.concatenate([valid] * together, axis=1)
    if weight is not None:
        weight = jnp.concatenate([weight] * together, axis=1)
    lane = lax.broadcasted_iota(jnp.int32, (HEAD_DIM, columns), 1) // size

    def scores_of(m, k, heads):
        turned = [query(m + s, slice(k * WIDE, (k + 1) * WIDE)) for s in range(pair)]
        turned = jnp.concatenate(turned, axis=0).T
        turned = [turned[j * HEAD_DIM : (j + 1) * HEAD_DIM] for j in heads]
        if pair > 1:
            zero = jnp.zeros((HEAD_DIM, columns), BF16)
            turned = [
                jnp.concatenate([jnp.where(lane == s, t, zero) for s in range(pair)], axis=0)
                for t in turned
            ]
        part = slice(k * HEAD_DIM, (k + 1) * HEAD_DIM)
        keys = jnp.concatenate([keyval(m + s, part) for s in range(pair)], axis=1)
        return jnp.dot(keys, jnp.concatenate(turned, axis=1), preferred_element_type=F32)

    def grow(scores):
        scores = jnp.where(valid, scores, NEG)
        top = jnp.max(scores, axis=0, keepdims=True)
        grown = jnp.exp2((scores - top) * EXP2_SCALE)
        if weight is not None:
            grown = grown * weight
        return grown.astype(BF16), jnp.sum(grown, axis=0, keepdims=True)

    def values_of(unit, grown, sums):
        m, k, heads = unit
        part = slice(KEYS + k * HEAD_DIM, KEYS + (k + 1) * HEAD_DIM)
        vals = jnp.concatenate([keyval(m + s, part).T for s in range(pair)], axis=0)
        mixed = jnp.dot(vals, grown, preferred_element_type=F32)
        inverse = 1.0 / sums
        parts = []
        for i in range(len(heads)):
            cols = slice(i * columns, (i + 1) * columns)
            chosen = mixed[:HEAD_DIM, cols]
            for s in range(1, pair):
                chosen = jnp.where(lane == s, mixed[s * HEAD_DIM : (s + 1) * HEAD_DIM, cols], chosen)
            parts.append(chosen * inverse[:, cols])
        mixed = jnp.concatenate(parts, axis=0).astype(BF16).T
        start = k * WIDE + heads[0] * HEAD_DIM
        store(m, slice(start, start + len(heads) * HEAD_DIM), mixed)

    units = [
        (m, k, tuple(range(j, j + together)))
        for m in range(0, members, pair)
        for k in range(KV_HEADS)
        for j in range(0, GROUPS, together)
    ]
    staggered(units, scores_of, grow, values_of)


def time_kernel(agents, steps, span, chunk, local, pair, *refs):
    hist_hbm, gain, wq_hbm, wkv_hbm, wo_hbm, *refs = refs
    before, refs = refs[:chunk], refs[chunk:]
    refs = refs[1:] if chunk else refs
    listing, refs = (refs[:3], refs[3:]) if chunk == 0 else ((), refs)
    mid_hbm, sent_hbm, keyval_hbm, *refs = refs
    mid, sent, keyval, hist, wq, wkv, wo, normed, query, mix, *refs = refs
    hist_sems, wq_sems, sems, mid_sems, sent_sems, keyval_sem = refs
    rows, width = hist.shape
    hist_loads, wq_loads = [], []
    for a in range(agents):
        source = hist_hbm.at[pl.ds(a * steps + chunk * span, span), :]
        hist_loads.append(
            pltpu.make_async_copy(source, hist.at[pl.ds(a * span, span), :], hist_sems.at[a])
        )
    for c in range(0, width, COLS):
        cols = pl.ds(c, COLS)
        wq_loads.append(
            pltpu.make_async_copy(wq_hbm.at[:, cols], wq.at[:, cols], wq_sems.at[c // COLS])
        )
    loads = [
        pltpu.make_async_copy(wkv_hbm, wkv, sems.at[0]),
        pltpu.make_async_copy(wo_hbm, wo, sems.at[1]),
    ]
    for load in hist_loads + loads[:1]:
        load.start()
    for a in range(agents):
        part = pl.ds(a * span, span)
        hist_loads[a].wait()
        if a == 0:
            for load in wq_loads:
                load.start()
        normed[part, :] = norm_rows(hist[part, :], gain[...])
    loads[0].wait()
    for c in range(0, 2 * KEYS, COLS):
        keyval[:, c : c + COLS] = jnp.dot(
            normed[...], wkv[:, c : c + COLS], preferred_element_type=F32
        ).astype(BF16)
    keeps = [pltpu.make_async_copy(keyval, keyval_hbm, keyval_sem)]
    keeps[0].start()
    loads[1].start()
    for c in range(0, width, COLS):
        wq_loads[c // COLS].wait()
        query[:, c : c + COLS] = jnp.dot(
            normed[...], wq[:, c : c + COLS], preferred_element_type=F32
        ).astype(BF16)

    keys = (chunk + 1) * span
    shape = (keys, pair * span)
    valid = lax.broadcasted_iota(jnp.int32, shape, 0) <= chunk * span + (
        lax.broadcasted_iota(jnp.int32, shape, 1) % span
    )

    def keyvals(a, cols):
        part = slice(a * span, (a + 1) * span)
        pieces = [ref[part, cols] for ref in (*before, keyval)]
        return jnp.concatenate(pieces, axis=0) if before else pieces[0]

    def store(a, cols, values):
        mix[a * span : (a + pair) * span, cols] = values

    attend(
        agents, pair, span, lambda a, cols: query[a * span : (a + 1) * span, cols],
        keyvals, store, valid,
    )
    order = one_hot(rows, lambda row: regroup(row, agents, span // local, local))
    loads[1].wait()
    for c in range(0, width, COLS):
        cols = slice(c, c + COLS)
        projected = jnp.dot(mix[...], wo[:, cols], preferred_element_type=F32)
        piece = (hist[:, cols].astype(F32) + projected).astype(BF16)
        mid[:, cols] = piece
    for a in range(agents):
        goal = mid_hbm.at[a, pl.ds(chunk * span, span), :]
        keeps.append(
            pltpu.make_async_copy(mid.at[pl.ds(a * span, span), :], goal, mid_sems.at[a])
        )
        keeps[-1].start()
    if listing:
        neighbours, nbr_valid, alive = listing
        lane = lax.broadcasted_iota(jnp.int32, (1, LANES), 1)
        notes = jnp.zeros((1, LANES), F32)
        for i in range(alive.shape[1]):
            notes = jnp.where(lane == i, alive[0, i].astype(F32), notes)
        for i in range(neighbours.shape[1]):
            listed = lane == alive.shape[1] + neighbours[0, i]
            notes = notes + jnp.where(listed, nbr_valid[0, i].astype(F32), 0.0)
        sent[:, width:] = jnp.broadcast_to(notes, (rows, LANES)).astype(BF16)
    for r in range(0, rows, rows // 2):
        for c in range(0, width, COLS):
            sent[r : r + rows // 2, c : c + COLS] = moved(
                order[r : r + rows // 2], mid[:, c : c + COLS]
            )
        part = pl.ds(r, rows // 2)
        keeps.append(
            pltpu.make_async_copy(
                sent.at[part, :], sent_hbm.at[part, :], sent_sems.at[r // (rows // 2)]
            )
        )
        keeps[-1].start()
    for keep in keeps:
        keep.wait()


def keys_kernel(local, mid, gain, wkv, second, out):
    rows, width = second.shape
    total = rows // local
    second[...] = norm_rows(mid[:, :width], gain[...])
    if local > 1:
        order = one_hot(rows, lambda row: regroup(row, total, local, 1))
        for c in range(0, width, COLS):
            second[:, c : c + COLS] = moved(order, second[:, c : c + COLS])
    for c in range(0, 2 * KEYS, COLS):
        result = jnp.dot(second[...], wkv[:, c : c + COLS], preferred_element_type=F32)
        out[:, :, c : c + COLS] = result.astype(BF16).reshape(local, total, COLS)


def query_kernel(second, wq, out):
    local, total, width = out.shape
    for c in range(0, width, COLS):
        result = jnp.dot(second[...], wq[:, c : c + COLS], preferred_element_type=F32)
        out[:, :, c : c + COLS] = result.astype(BF16).reshape(local, total, COLS)


def weight_kernel(local, tiles, width, half, mid, out):
    rows = mid.shape[0]
    total = rows // local
    group = total // tiles
    notes = mid[:, width:]
    shape = (total, rows)
    row, col = (lax.broadcasted_iota(jnp.int32, shape, d) for d in range(2))
    pick = jnp.where(col == row * local, 1.0, 0.0).astype(BF16)
    lines = moved(pick, notes)
    shape = (HALVES * total, LANES)
    key, lane = (lax.broadcasted_iota(jnp.int32, shape, d) for d in range(2))
    side, tile, agent = (key // total + half[0]) % HALVES, key % total // group, key % group
    spread = jnp.where(lane == HALVES * group + tile, 1.0, 0.0).astype(BF16)
    listed = lax.dot_general(spread, lines, ROWS_BY_COLS, preferred_element_type=F32)
    spread = jnp.where(lane == side * group + agent, 1.0, 0.0).astype(BF16)
    alive = lax.dot_general(spread, lines, ROWS_BY_COLS, preferred_element_type=F32)
    shape = (HALVES * total, total)
    key, query = (lax.broadcasted_iota(jnp.int32, shape, d) for d in range(2))
    first = query == key % total // group * group
    alive = jnp.sum(jnp.where(first, alive, 0.0), axis=1, keepdims=True)
    out[...] = listed * alive


def space_kernel(pair, query, own, other, weights, out, mix):
    local, total, width = query.shape
    rows = local * total
    weight = jnp.concatenate([weights[...]] * pair, axis=1)

    def keyvals(s, cols):
        return jnp.concatenate([own[s, :, cols], other[s, :, cols]], axis=0)

    def store(s, cols, values):
        mix[s * total : (s + pair) * total, cols] = values

    attend(
        local, pair, total, lambda s, cols: query[s, :, cols], keyvals, store, weight > 0, weight
    )
    if local > 1:
        order = one_hot(rows, lambda row: regroup(row, local, total, 1))
    for c in range(0, width, COLS):
        piece = mix[:, c : c + COLS]
        out[:, c : c + COLS] = moved(order, piece) if local > 1 else piece


def out_kernel(agents, span, chunk, local, arrived, mid_hbm, wo, out_hbm, mix, mid, sems):
    rows, width = arrived.shape
    part = pl.ds(chunk * span, span)
    load = pltpu.make_async_copy(mid_hbm.at[:, part, :], mid, sems.at[0])
    load.start()
    order = one_hot(rows, lambda row: regroup(row, span // local, agents, local))
    for c in range(0, width, COLS):
        mix[:, c : c + COLS] = moved(order, arrived[:, c : c + COLS])
    load.wait()
    for c in range(0, width, COLS):
        cols = slice(c, c + COLS)
        projected = jnp.dot(mix[...], wo[:, cols], preferred_element_type=F32)
        piece = projected.reshape(agents, span, COLS)
        mid[:, :, cols] = (mid[:, :, cols].astype(F32) + piece).astype(BF16)
    keep = pltpu.make_async_copy(mid, out_hbm.at[:, part, :], sems.at[1])
    keep.start()
    keep.wait()


def call(
    kernel, shapes, args, hbm=(), hbm_out=(), smem=(), aliases=None, scratch=(), flops=0, mib=16
):
    touched = sum(a.size * a.dtype.itemsize for a in args)
    touched += sum(s.size * s.dtype.itemsize for s in shapes)
    spaces = [pl.ANY if i in hbm else pltpu.VMEM for i in range(len(args))]
    results = pl.pallas_call(
        kernel,
        out_shape=list(shapes),
        in_specs=[
            pl.BlockSpec(memory_space=pltpu.SMEM if i in smem else space)
            for i, space in enumerate(spaces)
        ],
        out_specs=[
            pl.BlockSpec(memory_space=pl.ANY if i in hbm_out else pltpu.VMEM)
            for i in range(len(shapes))
        ],
        scratch_shapes=list(scratch),
        input_output_aliases=aliases or {},
        compiler_params=pltpu.CompilerParams(vmem_limit_bytes=mib * MIB),
        cost_estimate=pl.CostEstimate(flops=flops, bytes_accessed=touched, transcendentals=0),
    )(*args)
    return results if len(shapes) > 1 else results[0]


def per_device(
    histories,
    gain_time,
    wq_time,
    wkv_time,
    wo_time,
    gain_space,
    wq_space,
    wkv_space,
    wo_space,
    neighbours,
    nbr_valid,
    agent_valid,
):
    agents, steps, width = histories.shape[1:]
    tiles, rest = lax.axis_size("tile"), lax.axis_size("rest")
    spread = ("tile", "rest")
    parts = tiles * rest
    chunks = CHUNKS if steps % (CHUNKS * parts) == 0 else 1
    span = steps // chunks
    local = span // parts
    rows = agents * span
    total = parts * agents
    struct = jax.ShapeDtypeStruct

    def beside(size, members):
        return LANES // size if size < LANES and members % (LANES // size) == 0 else 1

    hist = histories.reshape(agents * steps, width)
    mids, sents, before = [], [], []
    whole = struct((agents, steps, width), BF16)
    for i in range(chunks):
        deep = width + LANES if i == 0 else width
        mid, sent, keyval = call(
            functools.partial(time_kernel, agents, steps, span, i, local, beside(span, agents)),
            [whole, struct((rows, deep), BF16), struct((rows, 2 * KEYS), BF16)],
            [hist, gain_time[None], wq_time, wkv_time, wo_time]
            + before
            + mids
            + ([neighbours, nbr_valid, agent_valid] if i == 0 else []),
            hbm=(0, 2, 3, 4) + ((5 + i,) if i else ()),
            aliases={5 + i: 0} if i else None,
            smem=(5, 6, 7) if i == 0 else (),
            hbm_out=(0, 1, 2),
            scratch=[
                pltpu.VMEM((rows, width), BF16),
                pltpu.VMEM((rows, deep), BF16),
                pltpu.VMEM((rows, 2 * KEYS), BF16),
                pltpu.VMEM((rows, width), BF16),
                pltpu.VMEM(wq_time.shape, BF16),
                pltpu.VMEM(wkv_time.shape, BF16),
                pltpu.VMEM(wo_time.shape, BF16),
                pltpu.VMEM((rows, width), BF16),
                pltpu.VMEM((rows, width), BF16),
                pltpu.VMEM((rows, width), BF16),
                pltpu.SemaphoreType.DMA((agents,)),
                pltpu.SemaphoreType.DMA((width // COLS,)),
                pltpu.SemaphoreType.DMA((2,)),
                pltpu.SemaphoreType.DMA((agents,)),
                pltpu.SemaphoreType.DMA((2,)),
                pltpu.SemaphoreType.DMA,
            ],
            flops=2 * rows * width * (2 * width + 2 * KEYS),
            mib=56,
        )
        mids = [mid]
        sents.append(sent.reshape(parts, agents * local, deep))
        before.append(keyval)

    swap = [(h, HALVES - 1 - h) for h in range(HALVES)]
    half = lax.axis_index("half").astype(jnp.int32).reshape(1)
    big = 16 + 16 * GROUPS * HALVES * total**2 // MIB
    homes, mixes = [], []
    for i, sent in enumerate(sents):
        deep = sent.shape[-1]
        there = lax.all_to_all(sent, spread, split_axis=0, concat_axis=0, tiled=True)
        there = there.reshape(rows, deep)
        if i + 1 < chunks:
            there, sents[i + 1] = lax.optimization_barrier((there, sents[i + 1]))
        if homes:
            first, *held = homes[-1]
            there, first, weight = lax.optimization_barrier((there, first, weight))
            homes[-1] = (first, *held)
        second, own = call(
            functools.partial(keys_kernel, local),
            [struct((rows, width), BF16), struct((local, total, 2 * KEYS), BF16)],
            [there, gain_space[None], wkv_space],
            flops=2 * rows * width * 2 * KEYS,
        )
        if homes:
            *held, last = homes[-1]
            own, last = lax.optimization_barrier((own, last))
            homes[-1] = (*held, last)
        other = lax.ppermute(own, "half", swap)
        if i == 0:
            weight = call(
                functools.partial(weight_kernel, local, tiles, width),
                [struct((HALVES * total, total), F32)],
                [half, there],
                smem=(0,),
            )
        query = call(
            query_kernel,
            [struct((local, total, width), BF16)],
            [second, wq_space],
            flops=2 * rows * width * width,
        )
        homes.append((query, own, other))
    for i, (query, own, other) in enumerate(homes):
        mix = call(
            functools.partial(space_kernel, beside(total, local)),
            [struct((rows, width), BF16)],
            [query, own, other, weight],
            scratch=[pltpu.VMEM((rows, width), BF16)],
            flops=(8 if i == 0 else SHADOW) * rows * total * width,
            mib=big,
        )
        mix = mix.reshape(parts, agents * local, width)
        mix = lax.all_to_all(mix, spread, split_axis=0, concat_axis=0, tiled=True)
        mixes.append(mix.reshape(rows, width))
    out = mids[0]
    for i, mix in enumerate(mixes):
        out = call(
            functools.partial(out_kernel, agents, span, i, local),
            [whole],
            [mix, out, wo_space],
            hbm=(1,),
            hbm_out=(0,),
            aliases={1: 0},
            scratch=[
                pltpu.VMEM((rows, width), BF16),
                pltpu.VMEM((agents, span, width), BF16),
                pltpu.SemaphoreType.DMA((2,)),
            ],
            flops=2 * rows * width * width,
        )
    return out[None]


def solution(mesh):
    tiles, members = mesh.devices.shape
    split = Mesh(
        mesh.devices.reshape(tiles, HALVES, members // HALVES), ("tile", "half", "rest")
    )
    states = P("tile", ("half", "rest"), None, None)
    listing = P("tile", None)
    return jax.shard_map(
        per_device,
        mesh=split,
        in_specs=(states,) + (P(),) * 8 + (listing,) * 3,
        out_specs=states,
        check_vma=False,
    )
```

```python
import functools
import math

import jax
import jax.numpy as jnp
from jax import lax
from jax.experimental import pallas as pl
from jax.experimental.pallas import tpu as pltpu
from jax.sharding import Mesh
from jax.sharding import PartitionSpec as P

HEADS = 16
KV_HEADS = 4
HEAD_DIM = 64
GROUPS = HEADS // KV_HEADS
KEYS = KV_HEADS * HEAD_DIM
WIDE = GROUPS * HEAD_DIM
SCALE = HEAD_DIM ** (-0.5)
EXP2_SCALE = SCALE * math.log2(math.e)
NEG = -1e30
LANES = 128
COLS = 256
HALVES = 2
CHUNKS = 2
DEPTH = 2
SHADOW = 100
MIB = 1024 * 1024
F32 = jnp.float32
BF16 = jnp.bfloat16
ROWS_BY_COLS = (((1,), (1,)), ((), ()))


def norm_rows(values, gain):
    wide = values.astype(F32)
    meansq = jnp.mean(wide * wide, axis=-1, keepdims=True)
    return (wide * lax.rsqrt(meansq + 1e-05) * gain).astype(BF16)


def one_hot(rows, target):
    row = lax.broadcasted_iota(jnp.int32, (rows, rows), 0)
    wanted = target(lax.broadcasted_iota(jnp.int32, (1, rows), 1))
    return jnp.where(row == wanted, 1.0, 0.0).astype(BF16)


def regroup(row, first, second, third):
    i, j, k = row // (second * third), row // third % second, row % third
    return (j * first + i) * third + k


def moved(order, piece):
    return jnp.dot(order, piece, preferred_element_type=F32).astype(BF16)


def staggered(units, first, second, third):
    scores, grown = {}, {}
    for i in range(len(units) + 2 * DEPTH):
        if i < len(units):
            scores[i] = first(*units[i])
        if 0 <= i - DEPTH < len(units):
            grown[i - DEPTH] = second(scores.pop(i - DEPTH))
        if 0 <= i - 2 * DEPTH < len(units):
            third(units[i - 2 * DEPTH], *grown.pop(i - 2 * DEPTH))


def attend(members, pair, size, query, keyval, store, valid, weight=None):
    columns = pair * size
    together = GROUPS if columns <= LANES else 1
    valid = jnp.concatenate([valid] * together, axis=1)
    if weight is not None:
        weight = jnp.concatenate([weight] * together, axis=1)
    lane = lax.broadcasted_iota(jnp.int32, (HEAD_DIM, columns), 1) // size

    def scores_of(m, k, heads):
        turned = [query(m + s, slice(k * WIDE, (k + 1) * WIDE)) for s in range(pair)]
        turned = jnp.concatenate(turned, axis=0).T
        turned = [turned[j * HEAD_DIM : (j + 1) * HEAD_DIM] for j in heads]
        if pair > 1:
            zero = jnp.zeros((HEAD_DIM, columns), BF16)
            turned = [
                jnp.concatenate([jnp.where(lane == s, t, zero) for s in range(pair)], axis=0)
                for t in turned
            ]
        part = slice(k * HEAD_DIM, (k + 1) * HEAD_DIM)
        keys = jnp.concatenate([keyval(m + s, part) for s in range(pair)], axis=1)
        return jnp.dot(keys, jnp.concatenate(turned, axis=1), preferred_element_type=F32)

    def grow(scores):
        scores = jnp.where(valid, scores, NEG)
        top = jnp.max(scores, axis=0, keepdims=True)
        grown = jnp.exp2((scores - top) * EXP2_SCALE)
        if weight is not None:
            grown = grown * weight
        return grown.astype(BF16), jnp.sum(grown, axis=0, keepdims=True)

    def values_of(unit, grown, sums):
        m, k, heads = unit
        part = slice(KEYS + k * HEAD_DIM, KEYS + (k + 1) * HEAD_DIM)
        vals = jnp.concatenate([keyval(m + s, part).T for s in range(pair)], axis=0)
        mixed = jnp.dot(vals, grown, preferred_element_type=F32)
        inverse = 1.0 / sums
        parts = []
        for i in range(len(heads)):
            cols = slice(i * columns, (i + 1) * columns)
            chosen = mixed[:HEAD_DIM, cols]
            for s in range(1, pair):
                chosen = jnp.where(lane == s, mixed[s * HEAD_DIM : (s + 1) * HEAD_DIM, cols], chosen)
            parts.append(chosen * inverse[:, cols])
        mixed = jnp.concatenate(parts, axis=0).astype(BF16).T
        start = k * WIDE + heads[0] * HEAD_DIM
        store(m, slice(start, start + len(heads) * HEAD_DIM), mixed)

    units = [
        (m, k, tuple(range(j, j + together)))
        for m in range(0, members, pair)
        for k in range(KV_HEADS)
        for j in range(0, GROUPS, together)
    ]
    staggered(units, scores_of, grow, values_of)


def time_kernel(agents, steps, span, chunk, local, pair, *refs):
    hist_hbm, gain, wq_hbm, wkv_hbm, wo_hbm, *refs = refs
    before, refs = refs[:chunk], refs[chunk:]
    refs = refs[1:] if chunk else refs
    listing, refs = (refs[:3], refs[3:]) if chunk == 0 else ((), refs)
    mid_hbm, sent_hbm, keyval_hbm, *refs = refs
    mid, sent, keyval, hist, wq, wkv, wo, normed, query, mix, *refs = refs
    hist_sems, wq_sems, sems, mid_sems, sent_sems, keyval_sem = refs
    rows, width = hist.shape
    hist_loads, wq_loads = [], []
    for a in range(agents):
        source = hist_hbm.at[pl.ds(a * steps + chunk * span, span), :]
        hist_loads.append(
            pltpu.make_async_copy(source, hist.at[pl.ds(a * span, span), :], hist_sems.at[a])
        )
    for c in range(0, width, COLS):
        cols = pl.ds(c, COLS)
        wq_loads.append(
            pltpu.make_async_copy(wq_hbm.at[:, cols], wq.at[:, cols], wq_sems.at[c // COLS])
        )
    loads = [
        pltpu.make_async_copy(wkv_hbm, wkv, sems.at[0]),
        pltpu.make_async_copy(wo_hbm, wo, sems.at[1]),
    ]
    for load in hist_loads + loads[:1]:
        load.start()
    for a in range(agents):
        part = pl.ds(a * span, span)
        hist_loads[a].wait()
        if a == 0:
            for load in wq_loads:
                load.start()
        normed[part, :] = norm_rows(hist[part, :], gain[...])
    loads[0].wait()
    for c in range(0, 2 * KEYS, COLS):
        keyval[:, c : c + COLS] = jnp.dot(
            normed[...], wkv[:, c : c + COLS], preferred_element_type=F32
        ).astype(BF16)
    keeps = [pltpu.make_async_copy(keyval, keyval_hbm, keyval_sem)]
    keeps[0].start()
    loads[1].start()
    for c in range(0, width, COLS):
        wq_loads[c // COLS].wait()
        query[:, c : c + COLS] = jnp.dot(
            normed[...], wq[:, c : c + COLS], preferred_element_type=F32
        ).astype(BF16)

    keys = (chunk + 1) * span
    shape = (keys, pair * span)
    valid = lax.broadcasted_iota(jnp.int32, shape, 0) <= chunk * span + (
        lax.broadcasted_iota(jnp.int32, shape, 1) % span
    )

    def keyvals(a, cols):
        part = slice(a * span, (a + 1) * span)
        pieces = [ref[part, cols] for ref in (*before, keyval)]
        return jnp.concatenate(pieces, axis=0) if before else pieces[0]

    def store(a, cols, values):
        mix[a * span : (a + pair) * span, cols] = values

    attend(
        agents, pair, span, lambda a, cols: query[a * span : (a + 1) * span, cols],
        keyvals, store, valid,
    )
    order = one_hot(rows, lambda row: regroup(row, agents, span // local, local))
    loads[1].wait()
    for c in range(0, width, COLS):
        cols = slice(c, c + COLS)
        projected = jnp.dot(mix[...], wo[:, cols], preferred_element_type=F32)
        piece = (hist[:, cols].astype(F32) + projected).astype(BF16)
        mid[:, cols] = piece
    for a in range(agents):
        goal = mid_hbm.at[a, pl.ds(chunk * span, span), :]
        keeps.append(
            pltpu.make_async_copy(mid.at[pl.ds(a * span, span), :], goal, mid_sems.at[a])
        )
        keeps[-1].start()
    if listing:
        neighbours, nbr_valid, alive = listing
        lane = lax.broadcasted_iota(jnp.int32, (1, LANES), 1)
        notes = jnp.zeros((1, LANES), F32)
        for i in range(alive.shape[1]):
            notes = jnp.where(lane == i, alive[0, i].astype(F32), notes)
        for i in range(neighbours.shape[1]):
            listed = lane == alive.shape[1] + neighbours[0, i]
            notes = notes + jnp.where(listed, nbr_valid[0, i].astype(F32), 0.0)
        sent[:, width:] = jnp.broadcast_to(notes, (rows, LANES)).astype(BF16)
    for r in range(0, rows, rows // 2):
        for c in range(0, width, COLS):
            sent[r : r + rows // 2, c : c + COLS] = moved(
                order[r : r + rows // 2], mid[:, c : c + COLS]
            )
        part = pl.ds(r, rows // 2)
        keeps.append(
            pltpu.make_async_copy(
                sent.at[part, :], sent_hbm.at[part, :], sent_sems.at[r // (rows // 2)]
            )
        )
        keeps[-1].start()
    for keep in keeps:
        keep.wait()


def keys_kernel(local, mid, gain, wkv, second, out):
    rows, width = second.shape
    total = rows // local
    second[...] = norm_rows(mid[:, :width], gain[...])
    if local > 1:
        order = one_hot(rows, lambda row: regroup(row, total, local, 1))
        for c in range(0, width, COLS):
            second[:, c : c + COLS] = moved(order, second[:, c : c + COLS])
    for c in range(0, 2 * KEYS, COLS):
        result = jnp.dot(second[...], wkv[:, c : c + COLS], preferred_element_type=F32)
        out[:, :, c : c + COLS] = result.astype(BF16).reshape(local, total, COLS)


def query_kernel(second, wq, out):
    local, total, width = out.shape
    for c in range(0, width, COLS):
        result = jnp.dot(second[...], wq[:, c : c + COLS], preferred_element_type=F32)
        out[:, :, c : c + COLS] = result.astype(BF16).reshape(local, total, COLS)


def weight_kernel(local, tiles, width, half, mid, out):
    rows = mid.shape[0]
    total = rows // local
    group = total // tiles
    notes = mid[:, width:]
    shape = (total, rows)
    row, col = (lax.broadcasted_iota(jnp.int32, shape, d) for d in range(2))
    pick = jnp.where(col == row * local, 1.0, 0.0).astype(BF16)
    lines = moved(pick, notes)
    shape = (HALVES * total, LANES)
    key, lane = (lax.broadcasted_iota(jnp.int32, shape, d) for d in range(2))
    side, tile, agent = (key // total + half[0]) % HALVES, key % total // group, key % group
    spread = jnp.where(lane == HALVES * group + tile, 1.0, 0.0).astype(BF16)
    listed = lax.dot_general(spread, lines, ROWS_BY_COLS, preferred_element_type=F32)
    spread = jnp.where(lane == side * group + agent, 1.0, 0.0).astype(BF16)
    alive = lax.dot_general(spread, lines, ROWS_BY_COLS, preferred_element_type=F32)
    shape = (HALVES * total, total)
    key, query = (lax.broadcasted_iota(jnp.int32, shape, d) for d in range(2))
    first = query == key % total // group * group
    alive = jnp.sum(jnp.where(first, alive, 0.0), axis=1, keepdims=True)
    out[...] = listed * alive


def space_kernel(pair, query, own, other, weights, out, mix):
    local, total, width = query.shape
    rows = local * total
    weight = jnp.concatenate([weights[...]] * pair, axis=1)

    def keyvals(s, cols):
        return jnp.concatenate([own[s, :, cols], other[s, :, cols]], axis=0)

    def store(s, cols, values):
        mix[s * total : (s + pair) * total, cols] = values

    attend(
        local, pair, total, lambda s, cols: query[s, :, cols], keyvals, store, weight > 0, weight
    )
    if local > 1:
        order = one_hot(rows, lambda row: regroup(row, local, total, 1))
    for c in range(0, width, COLS):
        piece = mix[:, c : c + COLS]
        out[:, c : c + COLS] = moved(order, piece) if local > 1 else piece


def out_kernel(agents, span, local, chunks, *refs):
    mixes, (mid_hbm, wo, out_hbm, mix, mids, sems, out_sems) = refs[:chunks], refs[chunks:]
    rows, width = mixes[0].shape
    loads = [
        pltpu.make_async_copy(mid_hbm.at[:, pl.ds(i * span, span), :], mids.at[i], sems.at[i])
        for i in range(chunks)
    ]
    for load in loads:
        load.start()
    order = one_hot(rows, lambda row: regroup(row, span // local, agents, local))
    for c in range(0, width, COLS):
        for i in range(chunks):
            mix[i * rows : (i + 1) * rows, c : c + COLS] = moved(order, mixes[i][:, c : c + COLS])
    keeps = []
    for i in range(chunks):
        loads[i].wait()
        for c in range(0, width, COLS):
            cols = slice(c, c + COLS)
            part = mix[i * rows : (i + 1) * rows, :]
            projected = jnp.dot(part, wo[:, cols], preferred_element_type=F32)
            piece = projected.reshape(agents, span, COLS)
            mids[i, :, :, cols] = (mids[i, :, :, cols].astype(F32) + piece).astype(BF16)
        goal = out_hbm.at[:, pl.ds(i * span, span), :]
        keeps.append(pltpu.make_async_copy(mids.at[i], goal, out_sems.at[i]))
        keeps[-1].start()
    for keep in keeps:
        keep.wait()


def call(
    kernel, shapes, args, hbm=(), hbm_out=(), smem=(), aliases=None, scratch=(), flops=0, mib=16
):
    touched = sum(a.size * a.dtype.itemsize for a in args)
    touched += sum(s.size * s.dtype.itemsize for s in shapes)
    spaces = [pl.ANY if i in hbm else pltpu.VMEM for i in range(len(args))]
    results = pl.pallas_call(
        kernel,
        out_shape=list(shapes),
        in_specs=[
            pl.BlockSpec(memory_space=pltpu.SMEM if i in smem else space)
            for i, space in enumerate(spaces)
        ],
        out_specs=[
            pl.BlockSpec(memory_space=pl.ANY if i in hbm_out else pltpu.VMEM)
            for i in range(len(shapes))
        ],
        scratch_shapes=list(scratch),
        input_output_aliases=aliases or {},
        compiler_params=pltpu.CompilerParams(vmem_limit_bytes=mib * MIB),
        cost_estimate=pl.CostEstimate(flops=flops, bytes_accessed=touched, transcendentals=0),
    )(*args)
    return results if len(shapes) > 1 else results[0]


def per_device(
    histories,
    gain_time,
    wq_time,
    wkv_time,
    wo_time,
    gain_space,
    wq_space,
    wkv_space,
    wo_space,
    neighbours,
    nbr_valid,
    agent_valid,
):
    agents, steps, width = histories.shape[1:]
    tiles, rest = lax.axis_size("tile"), lax.axis_size("rest")
    spread = ("tile", "rest")
    parts = tiles * rest
    chunks = CHUNKS if steps % (CHUNKS * parts) == 0 else 1
    span = steps // chunks
    local = span // parts
    rows = agents * span
    total = parts * agents
    struct = jax.ShapeDtypeStruct

    def beside(size, members):
        return LANES // size if size < LANES and members % (LANES // size) == 0 else 1

    hist = histories.reshape(agents * steps, width)
    mids, sents, before = [], [], []
    whole = struct((agents, steps, width), BF16)
    for i in range(chunks):
        deep = width + LANES if i == 0 else width
        mid, sent, keyval = call(
            functools.partial(time_kernel, agents, steps, span, i, local, beside(span, agents)),
            [whole, struct((rows, deep), BF16), struct((rows, 2 * KEYS), BF16)],
            [hist, gain_time[None], wq_time, wkv_time, wo_time]
            + before
            + mids
            + ([neighbours, nbr_valid, agent_valid] if i == 0 else []),
            hbm=(0, 2, 3, 4) + ((5 + i,) if i else ()),
            aliases={5 + i: 0} if i else None,
            smem=(5, 6, 7) if i == 0 else (),
            hbm_out=(0, 1, 2),
            scratch=[
                pltpu.VMEM((rows, width), BF16),
                pltpu.VMEM((rows, deep), BF16),
                pltpu.VMEM((rows, 2 * KEYS), BF16),
                pltpu.VMEM((rows, width), BF16),
                pltpu.VMEM(wq_time.shape, BF16),
                pltpu.VMEM(wkv_time.shape, BF16),
                pltpu.VMEM(wo_time.shape, BF16),
                pltpu.VMEM((rows, width), BF16),
                pltpu.VMEM((rows, width), BF16),
                pltpu.VMEM((rows, width), BF16),
                pltpu.SemaphoreType.DMA((agents,)),
                pltpu.SemaphoreType.DMA((width // COLS,)),
                pltpu.SemaphoreType.DMA((2,)),
                pltpu.SemaphoreType.DMA((agents,)),
                pltpu.SemaphoreType.DMA((2,)),
                pltpu.SemaphoreType.DMA,
            ],
            flops=2 * rows * width * (2 * width + 2 * KEYS),
            mib=56,
        )
        mids = [mid]
        sents.append(sent.reshape(parts, agents * local, deep))
        before.append(keyval)

    swap = [(h, HALVES - 1 - h) for h in range(HALVES)]
    half = lax.axis_index("half").astype(jnp.int32).reshape(1)
    big = 16 + 16 * GROUPS * HALVES * total**2 // MIB
    homes, mixes = [], []
    for i, sent in enumerate(sents):
        deep = sent.shape[-1]
        there = lax.all_to_all(sent, spread, split_axis=0, concat_axis=0, tiled=True)
        there = there.reshape(rows, deep)
        if i + 1 < chunks:
            there, sents[i + 1] = lax.optimization_barrier((there, sents[i + 1]))
        second, own = call(
            functools.partial(keys_kernel, local),
            [struct((rows, width), BF16), struct((local, total, 2 * KEYS), BF16)],
            [there, gain_space[None], wkv_space],
            flops=2 * rows * width * 2 * KEYS,
        )
        other = lax.ppermute(own, "half", swap)
        if i == 0:
            weight = call(
                functools.partial(weight_kernel, local, tiles, width),
                [struct((HALVES * total, total), F32)],
                [half, there],
                smem=(0,),
            )
        query = call(
            query_kernel,
            [struct((local, total, width), BF16)],
            [second, wq_space],
            flops=(2 if i == 0 else SHADOW) * rows * width * width,
        )
        homes.append((query, own, other))
    for i in range(chunks - 1):
        (query, own, other), (later, *held) = homes[i], homes[i + 1]
        own, held[0] = lax.optimization_barrier((own, held[0]))
        homes[i], homes[i + 1] = (query, own, other), (later, *held)
    for query, own, other in homes:
        mix = call(
            functools.partial(space_kernel, beside(total, local)),
            [struct((rows, width), BF16)],
            [query, own, other, weight],
            scratch=[pltpu.VMEM((rows, width), BF16)],
            flops=8 * rows * total * width,
            mib=big,
        )
        mix = mix.reshape(parts, agents * local, width)
        mix = lax.all_to_all(mix, spread, split_axis=0, concat_axis=0, tiled=True)
        mixes.append(mix.reshape(rows, width))
    out = call(
        functools.partial(out_kernel, agents, span, local, chunks),
        [whole],
        mixes + mids + [wo_space],
        hbm=(chunks,),
        hbm_out=(0,),
        aliases={chunks: 0},
        scratch=[
            pltpu.VMEM((agents * steps, width), BF16),
            pltpu.VMEM((chunks, agents, span, width), BF16),
            pltpu.SemaphoreType.DMA((chunks,)),
            pltpu.SemaphoreType.DMA((chunks,)),
        ],
        flops=2 * rows * width * width,
    )
    return out[None]


def solution(mesh):
    tiles, members = mesh.devices.shape
    split = Mesh(
        mesh.devices.reshape(tiles, HALVES, members // HALVES), ("tile", "half", "rest")
    )
    states = P("tile", ("half", "rest"), None, None)
    listing = P("tile", None)
    return jax.shard_map(
        per_device,
        mesh=split,
        in_specs=(states,) + (P(),) * 8 + (listing,) * 3,
        out_specs=states,
        check_vma=False,
    )
```

```python
import functools
import math

import jax
import jax.numpy as jnp
from jax import lax
from jax.experimental import pallas as pl
from jax.experimental.pallas import tpu as pltpu
from jax.sharding import Mesh
from jax.sharding import PartitionSpec as P

HEADS = 16
KV_HEADS = 4
HEAD_DIM = 64
GROUPS = HEADS // KV_HEADS
KEYS = KV_HEADS * HEAD_DIM
WIDE = GROUPS * HEAD_DIM
SCALE = HEAD_DIM ** (-0.5)
EXP2_SCALE = SCALE * math.log2(math.e)
NEG = -1e30
LANES = 128
COLS = 256
HALVES = 2
CHUNKS = 2
DEPTH = 2
SHADOW = 100
MIB = 1024 * 1024
F32 = jnp.float32
BF16 = jnp.bfloat16
ROWS_BY_COLS = (((1,), (1,)), ((), ()))


def norm_rows(values, gain):
    wide = values.astype(F32)
    meansq = jnp.mean(wide * wide, axis=-1, keepdims=True)
    return (wide * lax.rsqrt(meansq + 1e-05) * gain).astype(BF16)


def one_hot(rows, target):
    row = lax.broadcasted_iota(jnp.int32, (rows, rows), 0)
    wanted = target(lax.broadcasted_iota(jnp.int32, (1, rows), 1))
    return jnp.where(row == wanted, 1.0, 0.0).astype(BF16)


def regroup(row, first, second, third):
    i, j, k = row // (second * third), row // third % second, row % third
    return (j * first + i) * third + k


def moved(order, piece):
    return jnp.dot(order, piece, preferred_element_type=F32).astype(BF16)


def staggered(units, first, second, third):
    scores, grown = {}, {}
    for i in range(len(units) + 2 * DEPTH):
        if i < len(units):
            scores[i] = first(*units[i])
        if 0 <= i - DEPTH < len(units):
            grown[i - DEPTH] = second(scores.pop(i - DEPTH))
        if 0 <= i - 2 * DEPTH < len(units):
            third(units[i - 2 * DEPTH], *grown.pop(i - 2 * DEPTH))


def attend(members, pair, size, query, keyval, store, valid, weight=None):
    columns = pair * size
    together = GROUPS if columns <= LANES else 1
    valid = jnp.concatenate([valid] * together, axis=1)
    if weight is not None:
        weight = jnp.concatenate([weight] * together, axis=1)
    lane = lax.broadcasted_iota(jnp.int32, (HEAD_DIM, columns), 1) // size

    def scores_of(m, k, heads):
        turned = [query(m + s, slice(k * WIDE, (k + 1) * WIDE)) for s in range(pair)]
        turned = jnp.concatenate(turned, axis=0).T
        turned = [turned[j * HEAD_DIM : (j + 1) * HEAD_DIM] for j in heads]
        if pair > 1:
            zero = jnp.zeros((HEAD_DIM, columns), BF16)
            turned = [
                jnp.concatenate([jnp.where(lane == s, t, zero) for s in range(pair)], axis=0)
                for t in turned
            ]
        part = slice(k * HEAD_DIM, (k + 1) * HEAD_DIM)
        keys = jnp.concatenate([keyval(m + s, part) for s in range(pair)], axis=1)
        return jnp.dot(keys, jnp.concatenate(turned, axis=1), preferred_element_type=F32)

    def grow(scores):
        scores = jnp.where(valid, scores, NEG)
        top = jnp.max(scores, axis=0, keepdims=True)
        grown = jnp.exp2((scores - top) * EXP2_SCALE)
        if weight is not None:
            grown = grown * weight
        return grown.astype(BF16), jnp.sum(grown, axis=0, keepdims=True)

    def values_of(unit, grown, sums):
        m, k, heads = unit
        part = slice(KEYS + k * HEAD_DIM, KEYS + (k + 1) * HEAD_DIM)
        vals = jnp.concatenate([keyval(m + s, part).T for s in range(pair)], axis=0)
        mixed = jnp.dot(vals, grown, preferred_element_type=F32)
        inverse = 1.0 / sums
        parts = []
        for i in range(len(heads)):
            cols = slice(i * columns, (i + 1) * columns)
            chosen = mixed[:HEAD_DIM, cols]
            for s in range(1, pair):
                chosen = jnp.where(lane == s, mixed[s * HEAD_DIM : (s + 1) * HEAD_DIM, cols], chosen)
            parts.append(chosen * inverse[:, cols])
        mixed = jnp.concatenate(parts, axis=0).astype(BF16).T
        start = k * WIDE + heads[0] * HEAD_DIM
        store(m, slice(start, start + len(heads) * HEAD_DIM), mixed)

    units = [
        (m, k, tuple(range(j, j + together)))
        for m in range(0, members, pair)
        for k in range(KV_HEADS)
        for j in range(0, GROUPS, together)
    ]
    staggered(units, scores_of, grow, values_of)


def time_kernel(agents, steps, span, chunk, local, pair, *refs):
    hist_hbm, gain, wq_hbm, wkv_hbm, wo_hbm, *refs = refs
    before, refs = refs[:chunk], refs[chunk:]
    refs = refs[1:] if chunk else refs
    listing, refs = (refs[:3], refs[3:]) if chunk == 0 else ((), refs)
    mid_hbm, sent_hbm, keyval_hbm, *refs = refs
    mid, sent, keyval, hist, wq, wkv, wo, normed, query, mix, *refs = refs
    hist_sems, wq_sems, sems, mid_sems, sent_sems, keyval_sem = refs
    rows, width = hist.shape
    hist_loads, wq_loads = [], []
    for a in range(agents):
        source = hist_hbm.at[pl.ds(a * steps + chunk * span, span), :]
        hist_loads.append(
            pltpu.make_async_copy(source, hist.at[pl.ds(a * span, span), :], hist_sems.at[a])
        )
    for c in range(0, width, COLS):
        cols = pl.ds(c, COLS)
        wq_loads.append(
            pltpu.make_async_copy(wq_hbm.at[:, cols], wq.at[:, cols], wq_sems.at[c // COLS])
        )
    loads = [
        pltpu.make_async_copy(wkv_hbm, wkv, sems.at[0]),
        pltpu.make_async_copy(wo_hbm, wo, sems.at[1]),
    ]
    for load in hist_loads + loads[:1]:
        load.start()
    for a in range(agents):
        part = pl.ds(a * span, span)
        hist_loads[a].wait()
        if a == 0:
            for load in wq_loads:
                load.start()
        normed[part, :] = norm_rows(hist[part, :], gain[...])
    loads[0].wait()
    for c in range(0, 2 * KEYS, COLS):
        keyval[:, c : c + COLS] = jnp.dot(
            normed[...], wkv[:, c : c + COLS], preferred_element_type=F32
        ).astype(BF16)
    keeps = [pltpu.make_async_copy(keyval, keyval_hbm, keyval_sem)]
    keeps[0].start()
    loads[1].start()
    for c in range(0, width, COLS):
        wq_loads[c // COLS].wait()
        query[:, c : c + COLS] = jnp.dot(
            normed[...], wq[:, c : c + COLS], preferred_element_type=F32
        ).astype(BF16)

    keys = (chunk + 1) * span
    shape = (keys, pair * span)
    valid = lax.broadcasted_iota(jnp.int32, shape, 0) <= chunk * span + (
        lax.broadcasted_iota(jnp.int32, shape, 1) % span
    )

    def keyvals(a, cols):
        part = slice(a * span, (a + 1) * span)
        pieces = [ref[part, cols] for ref in (*before, keyval)]
        return jnp.concatenate(pieces, axis=0) if before else pieces[0]

    def store(a, cols, values):
        mix[a * span : (a + pair) * span, cols] = values

    attend(
        agents, pair, span, lambda a, cols: query[a * span : (a + 1) * span, cols],
        keyvals, store, valid,
    )
    order = one_hot(rows, lambda row: regroup(row, agents, span // local, local))
    loads[1].wait()
    for c in range(0, width, COLS):
        cols = slice(c, c + COLS)
        projected = jnp.dot(mix[...], wo[:, cols], preferred_element_type=F32)
        piece = (hist[:, cols].astype(F32) + projected).astype(BF16)
        mid[:, cols] = piece
    for a in range(agents):
        goal = mid_hbm.at[a, pl.ds(chunk * span, span), :]
        keeps.append(
            pltpu.make_async_copy(mid.at[pl.ds(a * span, span), :], goal, mid_sems.at[a])
        )
        keeps[-1].start()
    if listing:
        neighbours, nbr_valid, alive = listing
        lane = lax.broadcasted_iota(jnp.int32, (1, LANES), 1)
        notes = jnp.zeros((1, LANES), F32)
        for i in range(alive.shape[1]):
            notes = jnp.where(lane == i, alive[0, i].astype(F32), notes)
        for i in range(neighbours.shape[1]):
            listed = lane == alive.shape[1] + neighbours[0, i]
            notes = notes + jnp.where(listed, nbr_valid[0, i].astype(F32), 0.0)
        sent[:, width:] = jnp.broadcast_to(notes, (rows, LANES)).astype(BF16)
    for r in range(0, rows, rows // 2):
        for c in range(0, width, COLS):
            sent[r : r + rows // 2, c : c + COLS] = moved(
                order[r : r + rows // 2], mid[:, c : c + COLS]
            )
        part = pl.ds(r, rows // 2)
        keeps.append(
            pltpu.make_async_copy(
                sent.at[part, :], sent_hbm.at[part, :], sent_sems.at[r // (rows // 2)]
            )
        )
        keeps[-1].start()
    for keep in keeps:
        keep.wait()


def keys_kernel(local, mid, gain, wkv, out, second):
    rows, width = second.shape
    total = rows // local
    second[...] = norm_rows(mid[:, :width], gain[...])
    if local > 1:
        order = one_hot(rows, lambda row: regroup(row, total, local, 1))
        for c in range(0, width, COLS):
            second[:, c : c + COLS] = moved(order, second[:, c : c + COLS])
    for c in range(0, 2 * KEYS, COLS):
        result = jnp.dot(second[...], wkv[:, c : c + COLS], preferred_element_type=F32)
        out[:, :, c : c + COLS] = result.astype(BF16).reshape(local, total, COLS)


def query_kernel(mid, gain, wq, out, second):
    local, total, width = out.shape
    rows = local * total
    second[...] = norm_rows(mid[:, :width], gain[...])
    if local > 1:
        order = one_hot(rows, lambda row: regroup(row, total, local, 1))
        for c in range(0, width, COLS):
            second[:, c : c + COLS] = moved(order, second[:, c : c + COLS])
    for c in range(0, width, COLS):
        result = jnp.dot(second[...], wq[:, c : c + COLS], preferred_element_type=F32)
        out[:, :, c : c + COLS] = result.astype(BF16).reshape(local, total, COLS)


def weight_kernel(local, tiles, width, half, mid, out):
    rows = mid.shape[0]
    total = rows // local
    group = total // tiles
    notes = mid[:, width:]
    shape = (total, rows)
    row, col = (lax.broadcasted_iota(jnp.int32, shape, d) for d in range(2))
    pick = jnp.where(col == row * local, 1.0, 0.0).astype(BF16)
    lines = moved(pick, notes)
    shape = (HALVES * total, LANES)
    key, lane = (lax.broadcasted_iota(jnp.int32, shape, d) for d in range(2))
    side, tile, agent = (key // total + half[0]) % HALVES, key % total // group, key % group
    spread = jnp.where(lane == HALVES * group + tile, 1.0, 0.0).astype(BF16)
    listed = lax.dot_general(spread, lines, ROWS_BY_COLS, preferred_element_type=F32)
    spread = jnp.where(lane == side * group + agent, 1.0, 0.0).astype(BF16)
    alive = lax.dot_general(spread, lines, ROWS_BY_COLS, preferred_element_type=F32)
    shape = (HALVES * total, total)
    key, query = (lax.broadcasted_iota(jnp.int32, shape, d) for d in range(2))
    first = query == key % total // group * group
    alive = jnp.sum(jnp.where(first, alive, 0.0), axis=1, keepdims=True)
    out[...] = listed * alive


def space_kernel(pair, query, own, other, weights, out, mix):
    local, total, width = query.shape
    rows = local * total
    weight = jnp.concatenate([weights[...]] * pair, axis=1)

    def keyvals(s, cols):
        return jnp.concatenate([own[s, :, cols], other[s, :, cols]], axis=0)

    def store(s, cols, values):
        mix[s * total : (s + pair) * total, cols] = values

    attend(
        local, pair, total, lambda s, cols: query[s, :, cols], keyvals, store, weight > 0, weight
    )
    if local > 1:
        order = one_hot(rows, lambda row: regroup(row, local, total, 1))
    for c in range(0, width, COLS):
        piece = mix[:, c : c + COLS]
        out[:, c : c + COLS] = moved(order, piece) if local > 1 else piece


def out_kernel(agents, span, local, chunks, *refs):
    mixes, (mid_hbm, wo, out_hbm, mix, mids, sems, out_sems) = refs[:chunks], refs[chunks:]
    rows, width = mixes[0].shape
    loads = [
        pltpu.make_async_copy(mid_hbm.at[:, pl.ds(i * span, span), :], mids.at[i], sems.at[i])
        for i in range(chunks)
    ]
    for load in loads:
        load.start()
    order = one_hot(rows, lambda row: regroup(row, span // local, agents, local))
    for c in range(0, width, COLS):
        for i in range(chunks):
            mix[i * rows : (i + 1) * rows, c : c + COLS] = moved(order, mixes[i][:, c : c + COLS])
    keeps = []
    for i in range(chunks):
        loads[i].wait()
        for c in range(0, width, COLS):
            cols = slice(c, c + COLS)
            part = mix[i * rows : (i + 1) * rows, :]
            projected = jnp.dot(part, wo[:, cols], preferred_element_type=F32)
            piece = projected.reshape(agents, span, COLS)
            mids[i, :, :, cols] = (mids[i, :, :, cols].astype(F32) + piece).astype(BF16)
        goal = out_hbm.at[:, pl.ds(i * span, span), :]
        keeps.append(pltpu.make_async_copy(mids.at[i], goal, out_sems.at[i]))
        keeps[-1].start()
    for keep in keeps:
        keep.wait()


def call(
    kernel, shapes, args, hbm=(), hbm_out=(), smem=(), aliases=None, scratch=(), flops=0, mib=16
):
    touched = sum(a.size * a.dtype.itemsize for a in args)
    touched += sum(s.size * s.dtype.itemsize for s in shapes)
    spaces = [pl.ANY if i in hbm else pltpu.VMEM for i in range(len(args))]
    results = pl.pallas_call(
        kernel,
        out_shape=list(shapes),
        in_specs=[
            pl.BlockSpec(memory_space=pltpu.SMEM if i in smem else space)
            for i, space in enumerate(spaces)
        ],
        out_specs=[
            pl.BlockSpec(memory_space=pl.ANY if i in hbm_out else pltpu.VMEM)
            for i in range(len(shapes))
        ],
        scratch_shapes=list(scratch),
        input_output_aliases=aliases or {},
        compiler_params=pltpu.CompilerParams(vmem_limit_bytes=mib * MIB),
        cost_estimate=pl.CostEstimate(flops=flops, bytes_accessed=touched, transcendentals=0),
    )(*args)
    return results if len(shapes) > 1 else results[0]


def per_device(
    histories,
    gain_time,
    wq_time,
    wkv_time,
    wo_time,
    gain_space,
    wq_space,
    wkv_space,
    wo_space,
    neighbours,
    nbr_valid,
    agent_valid,
):
    agents, steps, width = histories.shape[1:]
    tiles, rest = lax.axis_size("tile"), lax.axis_size("rest")
    spread = ("tile", "rest")
    parts = tiles * rest
    chunks = CHUNKS if steps % (CHUNKS * parts) == 0 else 1
    span = steps // chunks
    local = span // parts
    rows = agents * span
    total = parts * agents
    struct = jax.ShapeDtypeStruct

    def beside(size, members):
        return LANES // size if size < LANES and members % (LANES // size) == 0 else 1

    hist = histories.reshape(agents * steps, width)
    mids, sents, before = [], [], []
    whole = struct((agents, steps, width), BF16)
    for i in range(chunks):
        deep = width + LANES if i == 0 else width
        mid, sent, keyval = call(
            functools.partial(time_kernel, agents, steps, span, i, local, beside(span, agents)),
            [whole, struct((rows, deep), BF16), struct((rows, 2 * KEYS), BF16)],
            [hist, gain_time[None], wq_time, wkv_time, wo_time]
            + before
            + mids
            + ([neighbours, nbr_valid, agent_valid] if i == 0 else []),
            hbm=(0, 2, 3, 4) + ((5 + i,) if i else ()),
            aliases={5 + i: 0} if i else None,
            smem=(5, 6, 7) if i == 0 else (),
            hbm_out=(0, 1, 2),
            scratch=[
                pltpu.VMEM((rows, width), BF16),
                pltpu.VMEM((rows, deep), BF16),
                pltpu.VMEM((rows, 2 * KEYS), BF16),
                pltpu.VMEM((rows, width), BF16),
                pltpu.VMEM(wq_time.shape, BF16),
                pltpu.VMEM(wkv_time.shape, BF16),
                pltpu.VMEM(wo_time.shape, BF16),
                pltpu.VMEM((rows, width), BF16),
                pltpu.VMEM((rows, width), BF16),
                pltpu.VMEM((rows, width), BF16),
                pltpu.SemaphoreType.DMA((agents,)),
                pltpu.SemaphoreType.DMA((width // COLS,)),
                pltpu.SemaphoreType.DMA((2,)),
                pltpu.SemaphoreType.DMA((agents,)),
                pltpu.SemaphoreType.DMA((2,)),
                pltpu.SemaphoreType.DMA,
            ],
            flops=2 * rows * width * (2 * width + 2 * KEYS),
            mib=56,
        )
        mids = [mid]
        sents.append(sent.reshape(parts, agents * local, deep))
        before.append(keyval)

    swap = [(h, HALVES - 1 - h) for h in range(HALVES)]
    half = lax.axis_index("half").astype(jnp.int32).reshape(1)
    big = 16 + 16 * GROUPS * HALVES * total**2 // MIB
    homes, mixes = [], []
    for i, sent in enumerate(sents):
        deep = sent.shape[-1]
        there = lax.all_to_all(sent, spread, split_axis=0, concat_axis=0, tiled=True)
        there = there.reshape(rows, deep)
        if i + 1 < chunks:
            there, sents[i + 1] = lax.optimization_barrier((there, sents[i + 1]))
        own = call(
            functools.partial(keys_kernel, local),
            [struct((local, total, 2 * KEYS), BF16)],
            [there, gain_space[None], wkv_space],
            scratch=[pltpu.VMEM((rows, width), BF16)],
            flops=2 * rows * width * 2 * KEYS,
        )
        other = lax.ppermute(own, "half", swap)
        if i == 0:
            weight = call(
                functools.partial(weight_kernel, local, tiles, width),
                [struct((HALVES * total, total), F32)],
                [half, there],
                smem=(0,),
            )
        query = call(
            query_kernel,
            [struct((local, total, width), BF16)],
            [there, gain_space[None], wq_space],
            scratch=[pltpu.VMEM((rows, width), BF16)],
            flops=(2 if i == 0 else SHADOW) * rows * width * width,
        )
        homes.append((query, own, other))
    for i in range(chunks - 1):
        (query, own, other), (later, *held) = homes[i], homes[i + 1]
        own, held[0] = lax.optimization_barrier((own, held[0]))
        homes[i], homes[i + 1] = (query, own, other), (later, *held)
    for query, own, other in homes:
        mix = call(
            functools.partial(space_kernel, beside(total, local)),
            [struct((rows, width), BF16)],
            [query, own, other, weight],
            scratch=[pltpu.VMEM((rows, width), BF16)],
            flops=8 * rows * total * width,
            mib=big,
        )
        mix = mix.reshape(parts, agents * local, width)
        mix = lax.all_to_all(mix, spread, split_axis=0, concat_axis=0, tiled=True)
        mixes.append(mix.reshape(rows, width))
    out = call(
        functools.partial(out_kernel, agents, span, local, chunks),
        [whole],
        mixes + mids + [wo_space],
        hbm=(chunks,),
        hbm_out=(0,),
        aliases={chunks: 0},
        scratch=[
            pltpu.VMEM((agents * steps, width), BF16),
            pltpu.VMEM((chunks, agents, span, width), BF16),
            pltpu.SemaphoreType.DMA((chunks,)),
            pltpu.SemaphoreType.DMA((chunks,)),
        ],
        flops=2 * rows * width * width,
    )
    return out[None]


def solution(mesh):
    tiles, members = mesh.devices.shape
    split = Mesh(
        mesh.devices.reshape(tiles, HALVES, members // HALVES), ("tile", "half", "rest")
    )
    states = P("tile", ("half", "rest"), None, None)
    listing = P("tile", None)
    return jax.shard_map(
        per_device,
        mesh=split,
        in_specs=(states,) + (P(),) * 8 + (listing,) * 3,
        out_specs=states,
        check_vma=False,
    )
```

```python
import functools
import math

import jax
import jax.numpy as jnp
from jax import lax
from jax.experimental import pallas as pl
from jax.experimental.pallas import tpu as pltpu
from jax.sharding import Mesh
from jax.sharding import PartitionSpec as P

HEADS = 16
KV_HEADS = 4
HEAD_DIM = 64
GROUPS = HEADS // KV_HEADS
KEYS = KV_HEADS * HEAD_DIM
WIDE = GROUPS * HEAD_DIM
SCALE = HEAD_DIM ** (-0.5)
EXP2_SCALE = SCALE * math.log2(math.e)
NEG = -1e30
LANES = 128
COLS = 256
HALVES = 2
CHUNKS = 2
DEPTH = 3
SHADOW = 100
MIB = 1024 * 1024
F32 = jnp.float32
BF16 = jnp.bfloat16
ROWS_BY_COLS = (((1,), (1,)), ((), ()))


def norm_rows(values, gain):
    wide = values.astype(F32)
    meansq = jnp.mean(wide * wide, axis=-1, keepdims=True)
    return (wide * lax.rsqrt(meansq + 1e-05) * gain).astype(BF16)


def one_hot(rows, target):
    row = lax.broadcasted_iota(jnp.int32, (rows, rows), 0)
    wanted = target(lax.broadcasted_iota(jnp.int32, (1, rows), 1))
    return jnp.where(row == wanted, 1.0, 0.0).astype(BF16)


def regroup(row, first, second, third):
    i, j, k = row // (second * third), row // third % second, row % third
    return (j * first + i) * third + k


def moved(order, piece):
    return jnp.dot(order, piece, preferred_element_type=F32).astype(BF16)


def staggered(units, first, second, third):
    scores, grown = {}, {}
    for i in range(len(units) + 2 * DEPTH):
        if i < len(units):
            scores[i] = first(*units[i])
        if 0 <= i - DEPTH < len(units):
            grown[i - DEPTH] = second(scores.pop(i - DEPTH))
        if 0 <= i - 2 * DEPTH < len(units):
            third(units[i - 2 * DEPTH], *grown.pop(i - 2 * DEPTH))


def attend(members, pair, size, query, keyval, store, valid, weight=None):
    columns = pair * size
    together = GROUPS if columns <= LANES else 1
    valid = jnp.concatenate([valid] * together, axis=1)
    if weight is not None:
        weight = jnp.concatenate([weight] * together, axis=1)
    lane = lax.broadcasted_iota(jnp.int32, (HEAD_DIM, columns), 1) // size

    def scores_of(m, k, heads):
        turned = [query(m + s, slice(k * WIDE, (k + 1) * WIDE)) for s in range(pair)]
        turned = jnp.concatenate(turned, axis=0).T
        turned = [turned[j * HEAD_DIM : (j + 1) * HEAD_DIM] for j in heads]
        if pair > 1:
            zero = jnp.zeros((HEAD_DIM, columns), BF16)
            turned = [
                jnp.concatenate([jnp.where(lane == s, t, zero) for s in range(pair)], axis=0)
                for t in turned
            ]
        part = slice(k * HEAD_DIM, (k + 1) * HEAD_DIM)
        keys = jnp.concatenate([keyval(m + s, part) for s in range(pair)], axis=1)
        return jnp.dot(keys, jnp.concatenate(turned, axis=1), preferred_element_type=F32)

    def grow(scores):
        scores = jnp.where(valid, scores, NEG)
        top = jnp.max(scores, axis=0, keepdims=True)
        grown = jnp.exp2((scores - top) * EXP2_SCALE)
        if weight is not None:
            grown = grown * weight
        return grown.astype(BF16), jnp.sum(grown, axis=0, keepdims=True)

    def values_of(unit, grown, sums):
        m, k, heads = unit
        part = slice(KEYS + k * HEAD_DIM, KEYS + (k + 1) * HEAD_DIM)
        vals = jnp.concatenate([keyval(m + s, part).T for s in range(pair)], axis=0)
        mixed = jnp.dot(vals, grown, preferred_element_type=F32)
        inverse = 1.0 / sums
        parts = []
        for i in range(len(heads)):
            cols = slice(i * columns, (i + 1) * columns)
            chosen = mixed[:HEAD_DIM, cols]
            for s in range(1, pair):
                chosen = jnp.where(lane == s, mixed[s * HEAD_DIM : (s + 1) * HEAD_DIM, cols], chosen)
            parts.append(chosen * inverse[:, cols])
        mixed = jnp.concatenate(parts, axis=0).astype(BF16).T
        start = k * WIDE + heads[0] * HEAD_DIM
        store(m, slice(start, start + len(heads) * HEAD_DIM), mixed)

    units = [
        (m, k, tuple(range(j, j + together)))
        for m in range(0, members, pair)
        for k in range(KV_HEADS)
        for j in range(0, GROUPS, together)
    ]
    staggered(units, scores_of, grow, values_of)


def time_kernel(agents, steps, span, chunk, local, pair, *refs):
    hist_hbm, gain, wq_hbm, wkv_hbm, wo_hbm, *refs = refs
    before, refs = refs[:chunk], refs[chunk:]
    refs = refs[1:] if chunk else refs
    listing, refs = (refs[:3], refs[3:]) if chunk == 0 else ((), refs)
    mid_hbm, sent_hbm, keyval_hbm, *refs = refs
    mid, sent, keyval, hist, wq, wkv, wo, normed, query, mix, *refs = refs
    hist_sems, wq_sems, sems, mid_sems, sent_sems, keyval_sem = refs
    rows, width = hist.shape
    hist_loads, wq_loads = [], []
    for a in range(agents):
        source = hist_hbm.at[pl.ds(a * steps + chunk * span, span), :]
        hist_loads.append(
            pltpu.make_async_copy(source, hist.at[pl.ds(a * span, span), :], hist_sems.at[a])
        )
    for c in range(0, width, COLS):
        cols = pl.ds(c, COLS)
        wq_loads.append(
            pltpu.make_async_copy(wq_hbm.at[:, cols], wq.at[:, cols], wq_sems.at[c // COLS])
        )
    loads = [
        pltpu.make_async_copy(wkv_hbm, wkv, sems.at[0]),
        pltpu.make_async_copy(wo_hbm, wo, sems.at[1]),
    ]
    for load in hist_loads + loads[:1]:
        load.start()
    for a in range(agents):
        part = pl.ds(a * span, span)
        hist_loads[a].wait()
        if a == 0:
            for load in wq_loads:
                load.start()
        normed[part, :] = norm_rows(hist[part, :], gain[...])
    loads[0].wait()
    for c in range(0, 2 * KEYS, COLS):
        keyval[:, c : c + COLS] = jnp.dot(
            normed[...], wkv[:, c : c + COLS], preferred_element_type=F32
        ).astype(BF16)
    keeps = [pltpu.make_async_copy(keyval, keyval_hbm, keyval_sem)]
    keeps[0].start()
    loads[1].start()
    for c in range(0, width, COLS):
        wq_loads[c // COLS].wait()
        query[:, c : c + COLS] = jnp.dot(
            normed[...], wq[:, c : c + COLS], preferred_element_type=F32
        ).astype(BF16)

    keys = (chunk + 1) * span
    shape = (keys, pair * span)
    valid = lax.broadcasted_iota(jnp.int32, shape, 0) <= chunk * span + (
        lax.broadcasted_iota(jnp.int32, shape, 1) % span
    )

    def keyvals(a, cols):
        part = slice(a * span, (a + 1) * span)
        pieces = [ref[part, cols] for ref in (*before, keyval)]
        return jnp.concatenate(pieces, axis=0) if before else pieces[0]

    def store(a, cols, values):
        mix[a * span : (a + pair) * span, cols] = values

    attend(
        agents, pair, span, lambda a, cols: query[a * span : (a + 1) * span, cols],
        keyvals, store, valid,
    )
    order = one_hot(rows, lambda row: regroup(row, agents, span // local, local))
    loads[1].wait()
    for c in range(0, width, COLS):
        cols = slice(c, c + COLS)
        projected = jnp.dot(mix[...], wo[:, cols], preferred_element_type=F32)
        piece = (hist[:, cols].astype(F32) + projected).astype(BF16)
        mid[:, cols] = piece
    for a in range(agents):
        goal = mid_hbm.at[a, pl.ds(chunk * span, span), :]
        keeps.append(
            pltpu.make_async_copy(mid.at[pl.ds(a * span, span), :], goal, mid_sems.at[a])
        )
        keeps[-1].start()
    if listing:
        neighbours, nbr_valid, alive = listing
        lane = lax.broadcasted_iota(jnp.int32, (1, LANES), 1)
        notes = jnp.zeros((1, LANES), F32)
        for i in range(alive.shape[1]):
            notes = jnp.where(lane == i, alive[0, i].astype(F32), notes)
        for i in range(neighbours.shape[1]):
            listed = lane == alive.shape[1] + neighbours[0, i]
            notes = notes + jnp.where(listed, nbr_valid[0, i].astype(F32), 0.0)
        sent[:, width:] = jnp.broadcast_to(notes, (rows, LANES)).astype(BF16)
    for r in range(0, rows, rows // 2):
        for c in range(0, width, COLS):
            sent[r : r + rows // 2, c : c + COLS] = moved(
                order[r : r + rows // 2], mid[:, c : c + COLS]
            )
        part = pl.ds(r, rows // 2)
        keeps.append(
            pltpu.make_async_copy(
                sent.at[part, :], sent_hbm.at[part, :], sent_sems.at[r // (rows // 2)]
            )
        )
        keeps[-1].start()
    for keep in keeps:
        keep.wait()


def keys_kernel(local, mid, gain, wkv, second, out):
    rows, width = second.shape
    total = rows // local
    second[...] = norm_rows(mid[:, :width], gain[...])
    if local > 1:
        order = one_hot(rows, lambda row: regroup(row, total, local, 1))
        for c in range(0, width, COLS):
            second[:, c : c + COLS] = moved(order, second[:, c : c + COLS])
    for c in range(0, 2 * KEYS, COLS):
        result = jnp.dot(second[...], wkv[:, c : c + COLS], preferred_element_type=F32)
        out[:, :, c : c + COLS] = result.astype(BF16).reshape(local, total, COLS)


def query_kernel(second, wq, out):
    local, total, width = out.shape
    for c in range(0, width, COLS):
        result = jnp.dot(second[...], wq[:, c : c + COLS], preferred_element_type=F32)
        out[:, :, c : c + COLS] = result.astype(BF16).reshape(local, total, COLS)


def weight_kernel(local, tiles, width, half, mid, out):
    rows = mid.shape[0]
    total = rows // local
    group = total // tiles
    notes = mid[:, width:]
    shape = (total, rows)
    row, col = (lax.broadcasted_iota(jnp.int32, shape, d) for d in range(2))
    pick = jnp.where(col == row * local, 1.0, 0.0).astype(BF16)
    lines = moved(pick, notes)
    shape = (HALVES * total, LANES)
    key, lane = (lax.broadcasted_iota(jnp.int32, shape, d) for d in range(2))
    side, tile, agent = (key // total + half[0]) % HALVES, key % total // group, key % group
    spread = jnp.where(lane == HALVES * group + tile, 1.0, 0.0).astype(BF16)
    listed = lax.dot_general(spread, lines, ROWS_BY_COLS, preferred_element_type=F32)
    spread = jnp.where(lane == side * group + agent, 1.0, 0.0).astype(BF16)
    alive = lax.dot_general(spread, lines, ROWS_BY_COLS, preferred_element_type=F32)
    shape = (HALVES * total, total)
    key, query = (lax.broadcasted_iota(jnp.int32, shape, d) for d in range(2))
    first = query == key % total // group * group
    alive = jnp.sum(jnp.where(first, alive, 0.0), axis=1, keepdims=True)
    out[...] = listed * alive


def space_kernel(pair, query, own, other, weights, out, mix):
    local, total, width = query.shape
    rows = local * total
    weight = jnp.concatenate([weights[...]] * pair, axis=1)

    def keyvals(s, cols):
        return jnp.concatenate([own[s, :, cols], other[s, :, cols]], axis=0)

    def store(s, cols, values):
        mix[s * total : (s + pair) * total, cols] = values

    attend(
        local, pair, total, lambda s, cols: query[s, :, cols], keyvals, store, weight > 0, weight
    )
    if local > 1:
        order = one_hot(rows, lambda row: regroup(row, local, total, 1))
    for c in range(0, width, COLS):
        piece = mix[:, c : c + COLS]
        out[:, c : c + COLS] = moved(order, piece) if local > 1 else piece


def out_kernel(agents, span, local, chunks, *refs):
    mixes, (mid_hbm, wo, out_hbm, mix, mids, sems, out_sems) = refs[:chunks], refs[chunks:]
    rows, width = mixes[0].shape
    loads = [
        pltpu.make_async_copy(mid_hbm.at[:, pl.ds(i * span, span), :], mids.at[i], sems.at[i])
        for i in range(chunks)
    ]
    for load in loads:
        load.start()
    order = one_hot(rows, lambda row: regroup(row, span // local, agents, local))
    for c in range(0, width, COLS):
        for i in range(chunks):
            mix[i * rows : (i + 1) * rows, c : c + COLS] = moved(order, mixes[i][:, c : c + COLS])
    keeps = []
    for i in range(chunks):
        loads[i].wait()
        for c in range(0, width, COLS):
            cols = slice(c, c + COLS)
            part = mix[i * rows : (i + 1) * rows, :]
            projected = jnp.dot(part, wo[:, cols], preferred_element_type=F32)
            piece = projected.reshape(agents, span, COLS)
            mids[i, :, :, cols] = (mids[i, :, :, cols].astype(F32) + piece).astype(BF16)
        goal = out_hbm.at[:, pl.ds(i * span, span), :]
        keeps.append(pltpu.make_async_copy(mids.at[i], goal, out_sems.at[i]))
        keeps[-1].start()
    for keep in keeps:
        keep.wait()


def call(
    kernel, shapes, args, hbm=(), hbm_out=(), smem=(), aliases=None, scratch=(), flops=0, mib=16
):
    touched = sum(a.size * a.dtype.itemsize for a in args)
    touched += sum(s.size * s.dtype.itemsize for s in shapes)
    spaces = [pl.ANY if i in hbm else pltpu.VMEM for i in range(len(args))]
    results = pl.pallas_call(
        kernel,
        out_shape=list(shapes),
        in_specs=[
            pl.BlockSpec(memory_space=pltpu.SMEM if i in smem else space)
            for i, space in enumerate(spaces)
        ],
        out_specs=[
            pl.BlockSpec(memory_space=pl.ANY if i in hbm_out else pltpu.VMEM)
            for i in range(len(shapes))
        ],
        scratch_shapes=list(scratch),
        input_output_aliases=aliases or {},
        compiler_params=pltpu.CompilerParams(vmem_limit_bytes=mib * MIB),
        cost_estimate=pl.CostEstimate(flops=flops, bytes_accessed=touched, transcendentals=0),
    )(*args)
    return results if len(shapes) > 1 else results[0]


def per_device(
    histories,
    gain_time,
    wq_time,
    wkv_time,
    wo_time,
    gain_space,
    wq_space,
    wkv_space,
    wo_space,
    neighbours,
    nbr_valid,
    agent_valid,
):
    agents, steps, width = histories.shape[1:]
    tiles, rest = lax.axis_size("tile"), lax.axis_size("rest")
    spread = ("tile", "rest")
    parts = tiles * rest
    chunks = CHUNKS if steps % (CHUNKS * parts) == 0 else 1
    span = steps // chunks
    local = span // parts
    rows = agents * span
    total = parts * agents
    struct = jax.ShapeDtypeStruct

    def beside(size, members):
        return LANES // size if size < LANES and members % (LANES // size) == 0 else 1

    hist = histories.reshape(agents * steps, width)
    mids, sents, before = [], [], []
    whole = struct((agents, steps, width), BF16)
    for i in range(chunks):
        deep = width + LANES if i == 0 else width
        mid, sent, keyval = call(
            functools.partial(time_kernel, agents, steps, span, i, local, beside(span, agents)),
            [whole, struct((rows, deep), BF16), struct((rows, 2 * KEYS), BF16)],
            [hist, gain_time[None], wq_time, wkv_time, wo_time]
            + before
            + mids
            + ([neighbours, nbr_valid, agent_valid] if i == 0 else []),
            hbm=(0, 2, 3, 4) + ((5 + i,) if i else ()),
            aliases={5 + i: 0} if i else None,
            smem=(5, 6, 7) if i == 0 else (),
            hbm_out=(0, 1, 2),
            scratch=[
                pltpu.VMEM((rows, width), BF16),
                pltpu.VMEM((rows, deep), BF16),
                pltpu.VMEM((rows, 2 * KEYS), BF16),
                pltpu.VMEM((rows, width), BF16),
                pltpu.VMEM(wq_time.shape, BF16),
                pltpu.VMEM(wkv_time.shape, BF16),
                pltpu.VMEM(wo_time.shape, BF16),
                pltpu.VMEM((rows, width), BF16),
                pltpu.VMEM((rows, width), BF16),
                pltpu.VMEM((rows, width), BF16),
                pltpu.SemaphoreType.DMA((agents,)),
                pltpu.SemaphoreType.DMA((width // COLS,)),
                pltpu.SemaphoreType.DMA((2,)),
                pltpu.SemaphoreType.DMA((agents,)),
                pltpu.SemaphoreType.DMA((2,)),
                pltpu.SemaphoreType.DMA,
            ],
            flops=2 * rows * width * (2 * width + 2 * KEYS),
            mib=56,
        )
        mids = [mid]
        sents.append(sent.reshape(parts, agents * local, deep))
        before.append(keyval)

    swap = [(h, HALVES - 1 - h) for h in range(HALVES)]
    half = lax.axis_index("half").astype(jnp.int32).reshape(1)
    big = 16 + 16 * GROUPS * HALVES * total**2 // MIB
    homes, mixes = [], []
    for i, sent in enumerate(sents):
        deep = sent.shape[-1]
        there = lax.all_to_all(sent, spread, split_axis=0, concat_axis=0, tiled=True)
        there = there.reshape(rows, deep)
        if i + 1 < chunks:
            there, sents[i + 1] = lax.optimization_barrier((there, sents[i + 1]))
        second, own = call(
            functools.partial(keys_kernel, local),
            [struct((rows, width), BF16), struct((local, total, 2 * KEYS), BF16)],
            [there, gain_space[None], wkv_space],
            flops=2 * rows * width * 2 * KEYS,
        )
        other = lax.ppermute(own, "half", swap)
        if i == 0:
            weight = call(
                functools.partial(weight_kernel, local, tiles, width),
                [struct((HALVES * total, total), F32)],
                [half, there],
                smem=(0,),
            )
        query = call(
            query_kernel,
            [struct((local, total, width), BF16)],
            [second, wq_space],
            flops=(2 if i == 0 else SHADOW) * rows * width * width,
        )
        homes.append((query, own, other))
    for i in range(chunks - 1):
        (query, own, other), (later, *held) = homes[i], homes[i + 1]
        own, held[0] = lax.optimization_barrier((own, held[0]))
        homes[i], homes[i + 1] = (query, own, other), (later, *held)
    for query, own, other in homes:
        mix = call(
            functools.partial(space_kernel, beside(total, local)),
            [struct((rows, width), BF16)],
            [query, own, other, weight],
            scratch=[pltpu.VMEM((rows, width), BF16)],
            flops=8 * rows * total * width,
            mib=big,
        )
        mix = mix.reshape(parts, agents * local, width)
        mix = lax.all_to_all(mix, spread, split_axis=0, concat_axis=0, tiled=True)
        mixes.append(mix.reshape(rows, width))
    out = call(
        functools.partial(out_kernel, agents, span, local, chunks),
        [whole],
        mixes + mids + [wo_space],
        hbm=(chunks,),
        hbm_out=(0,),
        aliases={chunks: 0},
        scratch=[
            pltpu.VMEM((agents * steps, width), BF16),
            pltpu.VMEM((chunks, agents, span, width), BF16),
            pltpu.SemaphoreType.DMA((chunks,)),
            pltpu.SemaphoreType.DMA((chunks,)),
        ],
        flops=2 * rows * width * width,
    )
    return out[None]


def solution(mesh):
    tiles, members = mesh.devices.shape
    split = Mesh(
        mesh.devices.reshape(tiles, HALVES, members // HALVES), ("tile", "half", "rest")
    )
    states = P("tile", ("half", "rest"), None, None)
    listing = P("tile", None)
    return jax.shard_map(
        per_device,
        mesh=split,
        in_specs=(states,) + (P(),) * 8 + (listing,) * 3,
        out_specs=states,
        check_vma=False,
    )
```
